32 devices in a mesh: lat: 4 (over x, core), lon: 8 (over z, y).
Axes of the slice: x: 2, y: 2, z: 4, core: 2. Of those that a mesh axis runs over, the one named last changes fastest.
Arguments:
- control: float32 [20, 4, 64, 1024], P(None, None, 'lat', 'lon'), may hold values from -6 to 6
- kappa: float32 [64, 1024], P('lat', 'lon'), may hold values from 0.05 to 0.49
- sea_mask: int32 [64, 1024], P('lat', 'lon'), may hold values 0 or 1
- vert_coef: float32 [20, 64, 1024], P(None, 'lat', 'lon'), may hold values from 0.5 to 20
- stencil_offsets: int32 [8, 1024, 1024], P(None, ('lat', 'lon')), may hold values from 0 to 2047
- stencil_weights: float32 [8, 1024, 1024], P(None, ('lat', 'lon')), may hold values from 0.05 to 0.3
- slot_target: int32 [1024, 1024], P(('lat', 'lon')), may hold values from 0 to 8191
- observed: float32 [262144], P(('lat', 'lon')), may hold values from -6 to 6
- inv_error: float32 [262144], P(('lat', 'lon')), may hold values from 0.5 to 2
Outputs:
- increment: float32 [20, 4, 64, 1024], P(None, None, 'lat', 'lon')
- misfit: float32 [262144], P(('lat', 'lon'))
The draws below stay inside these ranges and needn't reach their ends.
Inputs may be any that keep to these rules, and one draw needn't show every extreme that they name: `stencil_offsets`: an offset indexes one horizontal cell of one device's tile, as row * 128 + column.
All inputs are finite; a program needn't handle non-finite values. No bound on the sum of `sea_mask` on one device may be relied on, other than what follows from the above.
Results may differ from the reference program's by a relative error of at most 0.00002.
Values sent between devices are 32-bit elements; how exact they have to be, the bound alone decides.
A program may use at most 64 MiB of HBM per device.

```python
import math
import jax
import jax.numpy as jnp
from jax import lax

FIELDS = 4
LEV = 20
CLAT = 16
CLON = 128
STEPS = 10
STEN = 8
CAP = 1024
OWN = 8192
NLAT = 64
NLON = 1024
PAIRS = 1024
OBS = 262144
N_LAT = 4
N_LON = 8


def place_ends(values, stream_key, smallest, high):
    longest = values.shape.index(max(values.shape))
    spots = []
    for shift in (0, 1):
        where = [jax.random.randint(jax.random.fold_in(stream_key, axis), (), 0, length) for axis, length in enumerate(values.shape)]
        where[longest] = (where[longest] + shift) % values.shape[longest]
        spots.append(tuple(where))
    return values.at[spots[0]].set(smallest).at[spots[1]].set(high)


def block_levels(rng, dims, split, low, top_value):
    level, own = 1.0, jax.random.fold_in(rng, 6)
    for dim, parts in split:
        heights = jnp.exp(jax.random.uniform(jax.random.fold_in(own, dim), (parts,), jnp.float32, low / len(split), top_value / len(split)))
        level = level * jnp.repeat(heights, dims[dim] // parts).reshape([-1 if axis == dim else 1 for axis in range(len(dims))])
    return level


def noise(rng, shape, width, bound, split=(), kind=jnp.bfloat16):
    values = jax.random.normal(rng, shape, jnp.float32) * width
    if len(split) > 0:
        values = block_levels(rng, shape, split, -0.22, 0.18) * values
    return jnp.clip(values, min=-bound, max=bound).astype(kind)


def setup_inputs(seed: int = 0) -> dict:
    key_list = jax.random.split(jax.random.key(seed), 10)
    control = noise(key_list[0], (LEV, FIELDS, NLAT, NLON), 1.0, 6.0, ((2, 4), (3, 8)), jnp.float32)
    kappa = jnp.clip(jnp.exp(math.log(0.49) - 2.2823824 * jax.random.uniform(key_list[1], (NLAT, NLON), jnp.float32) ** block_levels(key_list[1], (NLAT, NLON), ((0, 4), (1, 8)), -0.2, 0.2)), 0.05, 0.49)
    sea_mask = place_ends((jax.random.randint(key_list[2], (NLAT, NLON), 0, 5) < 4).astype(jnp.int32), jax.random.fold_in(key_list[2], 1), 0, 1)
    vert_coef = jnp.clip(jnp.exp(math.log(20.0) - 3.6888795 * jax.random.uniform(key_list[3], (LEV, NLAT, NLON), jnp.float32) ** block_levels(key_list[3], (LEV, NLAT, NLON), ((1, 4), (2, 8)), -0.2, 0.2)), 0.5, 20.0)
    stencil_offsets = place_ends(jax.random.randint(key_list[4], (STEN, PAIRS, CAP), 0, CLAT * CLON), jax.random.fold_in(key_list[4], 1), 0, (CLAT * CLON) - 1).astype(jnp.int32)
    stencil_weights = jnp.clip(0.05 + 0.25 * jax.random.uniform(key_list[5], (STEN, PAIRS, CAP), jnp.float32) ** block_levels(key_list[5], (STEN, PAIRS, CAP), ((1, 32),), -0.2, 0.2), 0.05, 0.3)
    slot_target = place_ends(jax.random.randint(key_list[6], (PAIRS, CAP), 0, OWN), jax.random.fold_in(key_list[6], 1), 0, OWN - 1).astype(jnp.int32)
    observed = noise(key_list[7], (OBS,), 1.0, 6.0, ((0, 32),), jnp.float32)
    inv_error = jnp.clip(jnp.exp(math.log(2.0) - 1.3862944 * jax.random.uniform(key_list[8], (OBS,), jnp.float32) ** block_levels(key_list[8], (OBS,), ((0, 32),), -0.2, 0.2)), 0.5, 2.0)
    return dict(control=control, kappa=kappa, sea_mask=sea_mask, vert_coef=vert_coef, stencil_offsets=stencil_offsets, stencil_weights=stencil_weights, slot_target=slot_target, observed=observed, inv_error=inv_error)


def diffuse_step(wide, gwide):
    centre = wide[:, 1:-1, 1:-1]
    flux = gwide[2:, 1:-1] * (wide[:, 2:, 1:-1] - centre)
    flux = flux + gwide[:-2, 1:-1] * (wide[:, :-2, 1:-1] - centre)
    flux = flux + gwide[1:-1, 2:] * (wide[:, 1:-1, 2:] - centre)
    flux = flux + gwide[1:-1, :-2] * (wide[:, 1:-1, :-2] - centre)
    return centre + gwide[1:-1, 1:-1] * flux


def column_solve(rhs, vert_coef):
    upper_coef = jnp.concatenate([vert_coef[1:], jnp.zeros_like(vert_coef[:1])], axis=0)
    diag = 1.0 + vert_coef + upper_coef
    lower = -vert_coef
    upper = -upper_coef

    def forward(carry, items):
        cprev, dprev = carry
        low, mid, up, right = items
        denom = mid - low * cprev
        cnew = up / denom
        dnew = (right - low[None] * dprev) / denom[None]
        return (cnew, dnew), (cnew, dnew)

    init = (jnp.zeros(rhs.shape[2:], jnp.float32), jnp.zeros(rhs.shape[1:], jnp.float32))
    _, (cstore, dstore) = lax.scan(forward, init, (lower, diag, upper, rhs))

    def backward(ynext, items):
        cval, dval = items
        yval = dval - cval[None] * ynext
        return yval, yval

    _, result = lax.scan(backward, jnp.zeros(rhs.shape[1:], jnp.float32), (cstore, dstore), reverse=True)
    return result


def reference(control, kappa, sea_mask, vert_coef, stencil_offsets, stencil_weights, slot_target, observed, inv_error):
    devices = N_LAT * N_LON
    coef = kappa * sea_mask.astype(jnp.float32)
    gwide = jnp.pad(coef, ((0, 0), (1, 1)), mode="wrap")
    gwide = jnp.pad(gwide, ((1, 1), (0, 0)))
    field = control.reshape(LEV * FIELDS, NLAT, NLON)
    for step in range(STEPS):
        wide = jnp.pad(field, ((0, 0), (0, 0), (1, 1)), mode="wrap")
        wide = jnp.pad(wide, ((0, 0), (1, 1), (0, 0)))
        field = diffuse_step(wide, gwide)
    increment = column_solve(field.reshape(LEV, FIELDS, NLAT, NLON), vert_coef)
    tiles = increment.reshape(LEV, FIELDS, N_LAT, CLAT, N_LON, CLON)
    tiles = tiles.transpose(2, 4, 0, 1, 3, 5).reshape(devices, LEV * FIELDS * CLAT * CLON)
    slot_index = jnp.arange(devices * CAP, dtype=jnp.int32) % CAP
    layer = (slot_index % (LEV * FIELDS)).astype(jnp.int32)
    offsets = stencil_offsets.reshape(STEN, devices, devices * CAP).astype(jnp.int32)
    offsets = offsets + (layer * (CLAT * CLON)).astype(jnp.int32)[None, None, :]
    weights = stencil_weights.reshape(STEN, devices, devices * CAP)
    values = jax.vmap(lambda tile, idx: tile[idx], in_axes=(0, 1), out_axes=1)(tiles, offsets)
    partial_value = jnp.sum(values * weights, axis=0).reshape(devices, devices, CAP)
    received = partial_value.transpose(1, 0, 2)
    owner = jnp.arange(devices, dtype=jnp.int32).reshape(devices, 1, 1)
    target = owner * OWN + slot_target.reshape(devices, devices, CAP)
    value = jnp.zeros((devices * OWN,), jnp.float32).at[target.reshape(-1)].add(received.reshape(-1))
    misfit = (value - observed) * inv_error
    return increment, misfit
```

```python
import functools

import jax
import jax.numpy as jnp
from jax import lax
from jax.experimental import pallas as pl
from jax.experimental.pallas import tpu as pltpu
from jax.sharding import PartitionSpec as P

STEPS = 10
LANES = 128
SUB = 8


def lane_ids():
    return lax.broadcasted_iota(jnp.int32, (SUB, LANES), 1)


def lay_kernel(rows, layers, field_ref, kappa_ref, mask_ref, out_ref):
    wide = layers + SUB
    coef = kappa_ref[...] * mask_ref[...].astype(jnp.float32)
    for r in range(rows):
        for g in range(layers // SUB):
            out_ref[pl.ds(r * wide + g * SUB, SUB), :] = field_ref[
                pl.ds(g * SUB * rows + r, SUB, stride=rows), :
            ]
        out_ref[pl.ds(r * wide + layers, SUB), :] = jnp.broadcast_to(
            coef[r : r + 1, :], (SUB, LANES)
        )


def pack_kernel(rows, groups, main_ref, north_ref, south_ref, head_ref, tail_ref):
    lane = lane_ids()
    pitch = LANES // groups
    wide = groups * SUB

    def pack(src, count, start):
        def one_row(r, carry):
            base = pl.multiple_of(r * wide, SUB)
            head = jnp.zeros((SUB, LANES), jnp.float32)
            tail = head
            for g in range(groups):
                cells = src[pl.ds(base + g * SUB, SUB), :]
                spot = (lane >= g * pitch) & (lane < g * pitch + STEPS)
                head = jnp.where(spot, pltpu.roll(cells, g * pitch, 1), head)
                move = (g * pitch + STEPS) % LANES
                tail = jnp.where(spot, pltpu.roll(cells, move, 1), tail)
            at = pl.ds(pl.multiple_of((start + r) * SUB, SUB), SUB)
            head_ref[at, :] = head
            tail_ref[at, :] = tail
            return carry

        lax.fori_loop(0, count, one_row, 0, unroll=2)

    pack(north_ref, STEPS, 0)
    pack(main_ref, rows, STEPS)
    pack(south_ref, STEPS, STEPS + rows)


def diffuse(rows, layers, main_ref, north_ref, south_ref, west_ref, east_ref, near, far, near_b, far_b, coefs):
    lane = lane_ids()
    groups = layers // SUB + 1
    pitch = LANES // groups
    wide = groups * SUB
    tall = rows + 2 * STEPS

    def outer(r, g):
        at = pl.ds(pl.multiple_of(r * SUB, SUB), SUB)
        east = pltpu.roll(east_ref[at, :], (LANES - g * pitch) % LANES, 1)
        west = pltpu.roll(west_ref[at, :], (2 * LANES - STEPS - g * pitch) % LANES, 1)
        return jnp.where(lane < STEPS, east, jnp.where(lane >= LANES - STEPS, west, 0.0))

    def fill(src, count, start):
        def one_row(r, carry):
            base = pl.multiple_of(r * wide, SUB)
            row = start + r
            for g in range(groups - 1):
                at = pl.ds(pl.multiple_of(row * layers + g * SUB, SUB), SUB)
                near[at, :] = src[pl.ds(base + g * SUB, SUB), :]
                far[at, :] = outer(row, g)
            at = pl.ds(pl.multiple_of(row * SUB, SUB), SUB)
            coefs[10, at, :] = src[pl.ds(base + layers, SUB), :]
            coefs[11, at, :] = outer(row, groups - 1)
            return carry

        lax.fori_loop(0, count, one_row, 0, unroll=2)

    fill(north_ref, STEPS, 0)
    fill(main_ref, rows, STEPS)
    fill(south_ref, STEPS, STEPS + rows)

    def sides(a, b):
        ra, rb = pltpu.roll(a, 1, 1), pltpu.roll(b, 1, 1)
        la, lb = pltpu.roll(a, LANES - 1, 1), pltpu.roll(b, LANES - 1, 1)
        first, last = lane == 0, lane == LANES - 1
        return (
            (jnp.where(first, rb, ra), jnp.where(last, lb, la)),
            (jnp.where(first, ra, rb), jnp.where(last, la, lb)),
        )

    def weigh(r, carry):
        at = pl.ds(pl.multiple_of(r * SUB, SUB), SUB)
        up = pl.ds(pl.multiple_of((r - 1) * SUB, SUB), SUB)
        down = pl.ds(pl.multiple_of((r + 1) * SUB, SUB), SUB)
        both = sides(coefs[10, at, :], coefs[11, at, :])
        for k in range(2):
            here = coefs[10 + k, at, :]
            n = here * coefs[10 + k, up, :]
            s = here * coefs[10 + k, down, :]
            w = here * both[k][0]
            e = here * both[k][1]
            coefs[5 * k, at, :] = 1.0 - ((n + s) + (w + e))
            coefs[5 * k + 1, at, :] = n
            coefs[5 * k + 2, at, :] = s
            coefs[5 * k + 3, at, :] = w
            coefs[5 * k + 4, at, :] = e
        return carry

    lax.fori_loop(1, tall - 1, weigh, 0, unroll=2)

    for step in range(STEPS):
        old, new = (near, far), (near_b, far_b)
        if step % 2:
            old, new = new, old

        def two_rows(turn, carry, old=old, new=new, first=step + 1):
            r = first + 2 * turn
            c = [
                [coefs[k, pl.ds(pl.multiple_of((r + d) * SUB, SUB), SUB), :] for k in range(10)]
                for d in range(2)
            ]
            for g in range(groups - 1):
                spots = [
                    pl.ds(pl.multiple_of((r + d) * layers + g * SUB, SUB), SUB)
                    for d in range(-1, 3)
                ]
                cells = [[old[k][spot, :] for spot in spots] for k in range(2)]
                results = []
                for d in range(2):
                    both = sides(cells[0][d + 1], cells[1][d + 1])
                    for k in range(2):
                        p = c[d][5 * k : 5 * k + 5]
                        total = p[0] * cells[k][d + 1] + p[1] * cells[k][d]
                        other = p[3] * both[k][0] + p[4] * both[k][1]
                        results.append((k, spots[d + 1], (total + p[2] * cells[k][d + 2]) + other))
                for k, spot, value in results:
                    new[k][spot, :] = value
            return carry

        lax.fori_loop(0, (tall - 2 - 2 * step) // 2, two_rows, 0)


def solve_columns(rows, layers, done, vert_ref, inc_ref):
    levels = vert_ref.shape[0] // rows
    fields = layers // levels
    for h in range(rows // SUB):
        ratio = []
        coef = vert_ref[pl.ds(h * SUB, SUB), :]
        cprev = jnp.zeros((SUB, LANES), jnp.float32)
        prev = [cprev] * fields
        for k in range(levels):
            if k + 1 < levels:
                below = vert_ref[pl.ds((k + 1) * rows + h * SUB, SUB), :]
            else:
                below = jnp.zeros((SUB, LANES), jnp.float32)
            inv = 1.0 / (((1.0 + coef) + below) + coef * cprev)
            cprev = -below * inv
            ratio.append(cprev)
            for f in range(fields):
                layer = k * fields + f
                right = done[pl.ds((STEPS + h * SUB) * layers + layer, SUB, stride=layers), :]
                prev[f] = (right + coef * prev[f]) * inv
                inc_ref[pl.ds(layer * rows + h * SUB, SUB), :] = prev[f]
            coef = below
        for k in range(levels - 2, -1, -1):
            for f in range(fields):
                at = pl.ds((k * fields + f) * rows + h * SUB, SUB)
                prev[f] = inc_ref[at, :] - ratio[k] * prev[f]
                inc_ref[at, :] = prev[f]


def pick(table, row, col):
    level = [jnp.take_along_axis(t, col, axis=1) for t in table]
    bit = 1
    while len(level) > 1:
        odd = (row & bit) != 0
        level = [jnp.where(odd, level[i + 1], level[i]) for i in range(0, len(level), 2)]
        bit *= 2
    return level[0]


def turn_kernel(off_ref, w_ref, off_t, w_t):
    cap = off_ref.shape[1]
    groups = off_ref.shape[0] // LANES
    padded = off_t.shape[1]
    if padded > cap:
        for g in range(groups):
            off_t[g, cap:padded, :] = jnp.zeros((padded - cap, LANES), jnp.int32)
            w_t[g, cap:padded, :] = jnp.zeros((padded - cap, LANES), jnp.float32)
    for g in range(groups):
        for c in range(cap // LANES):
            here = pl.ds(c * LANES, LANES)
            off_t[g, here, :] = off_ref[pl.ds(g * LANES, LANES), here].T
            w_t[g, here, :] = w_ref[pl.ds(g * LANES, LANES), here].T


def column_kernel(
    rows,
    layers,
    owners,
    main_ref,
    north_ref,
    south_ref,
    west_ref,
    east_ref,
    vert_ref,
    off_t,
    w_t,
    inc_ref,
    out_ref,
    near,
    far,
    near_b,
    far_b,
    coefs,
    acc,
):
    diffuse(
        rows, layers, main_ref, north_ref, south_ref, west_ref, east_ref, near, far, near_b, far_b, coefs
    )
    solve_columns(rows, layers, near_b if STEPS % 2 else near, vert_ref, inc_ref)
    blocks = out_ref.shape[0] // owners
    cap = blocks * LANES
    groups = off_t.shape[0]
    turns = -(-cap // layers)

    def one_group(lg, carry):
        base = pl.multiple_of(lg * SUB, SUB)
        table = [inc_ref[pl.ds(base * rows + r, SUB, stride=rows), :] for r in range(rows)]
        for m in range(turns):
            at = pl.ds(m * layers + base, SUB)
            total = None
            for g in range(groups):
                idx = off_t[g, at, :]
                term = pick(table, idx >> 7, idx & (LANES - 1)) * w_t[g, at, :]
                total = term if total is None else total + term
            acc[at, :] = total
        return carry

    lax.fori_loop(0, layers // SUB, one_group, 0, unroll=2)
    for c in range(cap // LANES):
        here = pl.ds(c * LANES, LANES)
        block = acc[here, :].T
        total = block[:owners]
        for k in range(1, LANES // owners):
            total = total + block[k * owners : (k + 1) * owners]
        out_ref[pl.ds(c, owners, stride=blocks), :] = total


def shift(block, axis, step, closed):
    count = lax.axis_size(axis)
    pairs = [(i, (i + step) % count) for i in range(count)]
    if not closed:
        pairs = [(i, j) for i, j in pairs if j == i + step]
    return lax.ppermute(block, axis, pairs)


def local_call(kernel, shapes, count, scratch=(), name=None):
    return pl.pallas_call(
        kernel,
        out_shape=shapes,
        in_specs=[pl.BlockSpec(memory_space=pltpu.VMEM)] * count,
        out_specs=jax.tree.map(lambda _: pl.BlockSpec(memory_space=pltpu.VMEM), shapes),
        scratch_shapes=list(scratch),
        compiler_params=pltpu.CompilerParams(vmem_limit_bytes=40 * 1024 * 1024),
        name=name,
    )


def floats(*shape):
    return jax.ShapeDtypeStruct(shape, jnp.float32)


def columns_and_partials(control, kappa, sea_mask, vert_coef, offsets, weights):
    levels, fields, rows, cols = control.shape
    layers = levels * fields
    groups = layers // SUB + 1
    wide = groups * SUB
    tall = rows + 2 * STEPS
    sten, owners, cap = offsets.shape
    bundles = sten * owners // LANES
    padded = -(-cap // layers) * layers

    main = local_call(
        functools.partial(lay_kernel, rows, layers), floats(rows * wide, LANES), 3, name="lay"
    )(control.reshape(layers * rows, cols), kappa, sea_mask)
    north = shift(main[(rows - STEPS) * wide :], "lat", 1, False)
    south = shift(main[: STEPS * wide], "lat", -1, False)
    head, tail = local_call(
        functools.partial(pack_kernel, rows, groups),
        (floats(tall * SUB, LANES), floats(tall * SUB, LANES)),
        3,
        name="pack",
    )(main, north, south)
    west = shift(tail, "lon", 1, True)
    east = shift(head, "lon", -1, True)
    off_t, w_t = local_call(
        turn_kernel,
        (
            jax.ShapeDtypeStruct((bundles, padded, LANES), jnp.int32),
            floats(bundles, padded, LANES),
        ),
        2,
        name="turn",
    )(offsets.reshape(sten * owners, cap), weights.reshape(sten * owners, cap))
    increment, partial_value = local_call(
        functools.partial(column_kernel, rows, layers, owners),
        (floats(layers * rows, LANES), floats(owners * cap // LANES, LANES)),
        8,
        [
            pltpu.VMEM((tall * layers, LANES), jnp.float32),
            pltpu.VMEM((tall * layers, LANES), jnp.float32),
            pltpu.VMEM((tall * layers, LANES), jnp.float32),
            pltpu.VMEM((tall * layers, LANES), jnp.float32),
            pltpu.VMEM((12, tall * SUB, LANES), jnp.float32),
            pltpu.VMEM((padded, LANES), jnp.float32),
        ],
        name="columns",
    )(
        main,
        north,
        south,
        west,
        east,
        vert_coef.reshape(levels * rows, cols),
        off_t,
        w_t,
    )
    return increment.reshape(control.shape), partial_value.reshape(owners, cap // LANES, LANES)


def spread(v, t, high):
    cap = v.shape[1]
    hit = lax.broadcasted_iota(jnp.int32, (high, cap), 0) == (t >> 7)
    ones = lax.broadcasted_iota(jnp.int32, (LANES, cap), 0) == (t & (LANES - 1))
    first = v.astype(jnp.bfloat16).astype(jnp.float32)
    left = jnp.concatenate(
        [jnp.where(hit, part, 0.0).astype(jnp.bfloat16) for part in (first, v - first)], axis=0
    )
    right = jnp.where(ones, 1.0, 0.0).astype(jnp.bfloat16)
    return lax.dot_general(
        left, right, (((1,), (1,)), ((), ())), preferred_element_type=jnp.float32
    )


def owner_kernel(n_lon, devices, part_ref, tgt_ref, obs_ref, err_ref, out_ref, recv, acc, send_sem, recv_sem):
    high = obs_ref.shape[0]
    blocks = part_ref.shape[1]
    me = lax.axis_index("lat") * n_lon + lax.axis_index("lon")

    def place(q):
        return (q // n_lon, q % n_lon)

    def copy(k):
        q = lax.rem(me + k, devices)
        return pltpu.make_async_remote_copy(
            src_ref=part_ref.at[q],
            dst_ref=recv.at[k],
            send_sem=send_sem.at[k],
            recv_sem=recv_sem.at[k],
            device_id=place(q),
            device_id_type=pl.DeviceIdType.MESH,
        )

    barrier = pltpu.get_barrier_semaphore()

    def greet(k, carry):
        q = lax.rem(me + k, devices)
        pl.semaphore_signal(
            barrier, inc=1, device_id=place(q), device_id_type=pl.DeviceIdType.MESH
        )
        return carry

    lax.fori_loop(1, devices, greet, 0)
    recv[0] = part_ref[me]
    acc[...] = jnp.zeros_like(acc)
    pl.semaphore_wait(barrier, devices - 1)

    def send(k, carry):
        copy(k).start()
        return carry

    lax.fori_loop(1, devices, send, 0)

    def add(k):
        p = lax.rem(me - k + devices, devices)
        cells = recv[k]
        v = jnp.concatenate([cells[c : c + 1, :] for c in range(blocks)], axis=1)
        acc[...] += spread(v, tgt_ref[pl.ds(p, 1), :], high)

    add(0)

    def one_source(k, carry):
        copy(k).wait_recv()
        add(k)
        return carry

    lax.fori_loop(1, devices, one_source, 0)

    def drain(k, carry):
        copy(k).wait_send()
        return carry

    lax.fori_loop(1, devices, drain, 0)
    out_ref[...] = (acc[:high] + acc[high:] - obs_ref[...]) * err_ref[...]


def owner_misfit(partial_value, target, observed, inv_error):
    high = observed.shape[0] // LANES
    devices, blocks, _ = partial_value.shape
    out = pl.pallas_call(
        functools.partial(owner_kernel, lax.axis_size("lon"), devices),
        out_shape=jax.ShapeDtypeStruct((high, LANES), jnp.float32),
        in_specs=[pl.BlockSpec(memory_space=pltpu.VMEM)] * 4,
        out_specs=pl.BlockSpec(memory_space=pltpu.VMEM),
        scratch_shapes=[
            pltpu.VMEM(partial_value.shape, jnp.float32),
            pltpu.VMEM((2 * high, LANES), jnp.float32),
            pltpu.SemaphoreType.DMA((devices,)),
            pltpu.SemaphoreType.DMA((devices,)),
        ],
        compiler_params=pltpu.CompilerParams(
            vmem_limit_bytes=32 * 1024 * 1024, collective_id=1, has_side_effects=True
        ),
        name="owner_misfit",
    )(partial_value, target, observed.reshape(high, LANES), inv_error.reshape(high, LANES))
    return out.reshape(-1)


def per_device(
    control,
    kappa,
    sea_mask,
    vert_coef,
    stencil_offsets,
    stencil_weights,
    slot_target,
    observed,
    inv_error,
):
    increment, partial_value = columns_and_partials(
        control, kappa, sea_mask, vert_coef, stencil_offsets, stencil_weights
    )
    misfit = owner_misfit(partial_value, slot_target, observed, inv_error)
    return (increment, misfit)


def solution(mesh):
    return jax.shard_map(
        per_device,
        mesh=mesh,
        in_specs=(
            P(None, None, "lat", "lon"),
            P("lat", "lon"),
            P("lat", "lon"),
            P(None, "lat", "lon"),
            P(None, ("lat", "lon"), None),
            P(None, ("lat", "lon"), None),
            P(("lat", "lon"), None),
            P(("lat", "lon")),
            P(("lat", "lon")),
        ),
        out_specs=(P(None, None, "lat", "lon"), P(("lat", "lon"))),
        check_vma=False,
    )
```

```python
import functools

import jax
import jax.numpy as jnp
from jax import lax
from jax.experimental import pallas as pl
from jax.experimental.pallas import tpu as pltpu
from jax.sharding import PartitionSpec as P

STEPS = 10
LANES = 128
SUB = 8


WAYS = ((-1, 0), (1, 0), (0, -1), (0, 1), (-1, -1), (-1, 1), (1, -1), (1, 1))
PAD = 16
PITCH = LANES + 2 * PAD


def aligned(start, size):
    return pl.ds(pl.multiple_of(start, SUB), size)


def corner_spots():
    spots, at = [], 0
    for d in range(1, STEPS):
        spots.append((d, at, STEPS - d))
        at += STEPS - d
    return spots, -(-at // SUB) * SUB


def update(old, new, c0, k2, count, first, low, high):
    def two_rows(turn, carry):
        base = (first + 2 * turn) * PITCH
        for v in range(low, high):
            spot = [aligned(base + d * PITCH + v * SUB, SUB) for d in range(-1, 3)]
            cells = [old[s, :] for s in spot]
            for d in range(2):
                at = base + d * PITCH + v * SUB
                side = old[pl.ds(at - 1, SUB), :] + old[pl.ds(at + 1, SUB), :]
                around = (cells[d] + cells[d + 2]) + side
                new[spot[d + 1], :] = c0[spot[d + 1], :] * cells[d + 1] + k2[spot[d + 1], :] * around
        return carry

    lax.fori_loop(0, count, two_rows, 0)


def diffuse(rows, old, new, c0, k2):
    tall = rows + 2 * STEPS
    width = PITCH // SUB
    update(old, new, c0, k2, (tall - 2) // 2, 1, 0, width)
    update(new, old, c0, k2, (tall - 4) // 2, 2, 1, width - 1)

    def two_steps(s, carry):
        first = 2 * s + 1
        update(old, new, c0, k2, (tall - 2 * first) // 2, first, 1, width - 1)
        update(new, old, c0, k2, (tall - 2 * first - 2) // 2, first + 1, 1, width - 1)
        return carry

    lax.fori_loop(1, STEPS // 2, two_steps, 0)


def solve_columns(rows, layers, done, control, coef, vert_ref, inc_ref):
    levels = vert_ref.shape[0] // rows
    fields = layers // levels
    for h in range(rows // SUB):
        here = coef[pl.ds(rows + h * SUB, SUB), :]
        sea = here != 0.0
        back = 1.0 / jnp.where(sea, here, 1.0)
        ratio = []
        above = vert_ref[pl.ds(h * SUB, SUB), :]
        cprev = jnp.zeros((SUB, LANES), jnp.float32)
        prev = [cprev] * fields
        for k in range(levels):
            if k + 1 < levels:
                below = vert_ref[pl.ds((k + 1) * rows + h * SUB, SUB), :]
            else:
                below = jnp.zeros((SUB, LANES), jnp.float32)
            inv = 1.0 / (((1.0 + above) + below) + above * cprev)
            cprev = -below * inv
            ratio.append(cprev)
            for f in range(fields):
                layer = k * fields + f
                at = pl.ds(layer * rows + h * SUB, SUB)
                right = done[pl.ds(h * SUB * LANES + layer, SUB, stride=LANES), :] * back
                right = jnp.where(sea, right, control[at, :])
                prev[f] = (right + above * prev[f]) * inv
                inc_ref[at, :] = prev[f]
            above = below
        for k in range(levels - 2, -1, -1):
            for f in range(fields):
                at = pl.ds((k * fields + f) * rows + h * SUB, SUB)
                prev[f] = inc_ref[at, :] - ratio[k] * prev[f]
                inc_ref[at, :] = prev[f]


def weigh(rows, coefs, held):
    lane = lax.broadcasted_iota(jnp.int32, (40, LANES), 1)
    mid = pl.ds(rows - STEPS + 1, 40)
    up = pl.ds(rows - STEPS, 40)
    down = pl.ds(rows - STEPS + 2, 40)
    here = [coefs[k, mid, :] for k in range(3)]
    right = [pltpu.roll(c, 1, 1) for c in here]
    left = [pltpu.roll(c, LANES - 1, 1) for c in here]
    first, last = lane == 0, lane == LANES - 1
    wests = [right[0], jnp.where(first, right[0], right[1]), jnp.where(first, right[1], right[2])]
    easts = [jnp.where(last, left[1], left[0]), jnp.where(last, left[2], left[1]), left[2]]
    for k in range(3):
        around = (coefs[k, up, :] + coefs[k, down, :]) + (wests[k] + easts[k])
        held[0, k, :, :] = 1.0 - here[k] * around
        held[1, k, :, :] = here[k] * here[k]


def broaden(rows, held, kind, out):
    lane = lax.broadcasted_iota(jnp.int32, (40, LANES), 1)
    rest = jnp.zeros((LANES - 40, LANES), jnp.float32)
    main = jnp.concatenate([held[kind, 1, :, :], rest], axis=0).T
    outer = jnp.where(lane >= LANES - PAD, held[kind, 0, :, :], held[kind, 2, :, :])
    outer = jnp.concatenate([outer, rest], axis=0).T
    for j in range(rows + 2 * STEPS - 2):
        base = (j + 1) * PITCH
        column = outer[:, j : j + 1]
        out[pl.ds(base, PAD), :] = jnp.broadcast_to(column[LANES - PAD :], (PAD, LANES))
        out[pl.ds(base + PAD, LANES), :] = jnp.broadcast_to(main[:, j : j + 1], (LANES, LANES))
        out[pl.ds(base + PAD + LANES, PAD), :] = jnp.broadcast_to(column[:PAD], (PAD, LANES))


def turn(off_ref, w_ref, off_t, w_t):
    cap = off_ref.shape[1]
    groups = off_ref.shape[0] // LANES
    padded = off_t.shape[1]
    if padded > cap:
        for g in range(groups):
            off_t[g, cap:padded, :] = jnp.zeros((padded - cap, LANES), jnp.int32)
            w_t[g, cap:padded, :] = jnp.zeros((padded - cap, LANES), jnp.float32)
    for g in range(groups):
        for c in range(cap // LANES):
            here = pl.ds(c * LANES, LANES)
            off_t[g, here, :] = off_ref[pl.ds(g * LANES, LANES), here].T
            w_t[g, here, :] = w_ref[pl.ds(g * LANES, LANES), here].T


def field_kernel(
    n_lat,
    n_lon,
    rows,
    layers,
    control_ref,
    kappa_ref,
    mask_ref,
    vert_ref,
    off_ref,
    w_ref,
    inc_ref,
    off_t,
    w_t,
    control,
    kappa,
    mask,
    vert,
    off,
    weight,
    coefs,
    held,
    laid,
    far_rows,
    side_out,
    side_in,
    corner_out,
    corner_in,
    near,
    far,
    c0,
    k2,
    done,
    load_sem,
    coef_send,
    coef_recv,
    send_sem,
    recv_sem,
):
    lat, lon = lax.axis_index("lat"), lax.axis_index("lon")
    tall = rows + 2 * STEPS
    pairs = ((control_ref, control), (kappa_ref, kappa), (mask_ref, mask))
    pairs += ((vert_ref, vert), (off_ref, off), (w_ref, weight))
    loads = [pltpu.make_async_copy(a, b, load_sem.at[i]) for i, (a, b) in enumerate(pairs)]
    for i in (1, 2, 0, 3, 4, 5):
        loads[i].start()

    def place(i):
        return (lat + WAYS[i][0], lax.rem(lon + WAYS[i][1] + n_lon, n_lon))

    def guard(step, body):
        if step == 0:
            body()
        else:
            pl.when(lat > 0 if step < 0 else lat < n_lat - 1)(body)

    side_in[...] = jnp.zeros_like(side_in)
    corner_in[...] = jnp.zeros_like(corner_in)

    @pl.when(lat == 0)
    def _():
        coefs[:, :rows, :] = jnp.zeros((3, rows, LANES), jnp.float32)
        far_rows[1] = jnp.zeros((STEPS * layers, LANES), jnp.float32)

    @pl.when(lat == n_lat - 1)
    def _():
        coefs[:, 2 * rows :, :] = jnp.zeros((3, rows, LANES), jnp.float32)
        far_rows[0] = jnp.zeros((STEPS * layers, LANES), jnp.float32)

    barrier = pltpu.get_barrier_semaphore()
    for i, way in enumerate(WAYS):
        guard(
            way[0],
            lambda i=i: pl.semaphore_signal(
                barrier, inc=1, device_id=place(i), device_id_type=pl.DeviceIdType.MESH
            ),
        )

    def remote(i, src, dst, out_sem, in_sem):
        return pltpu.make_async_remote_copy(
            src_ref=src,
            dst_ref=dst,
            send_sem=out_sem.at[i],
            recv_sem=in_sem.at[i],
            device_id=place(i),
            device_id_type=pl.DeviceIdType.MESH,
        )

    def coef_copy(i):
        dl, dn = WAYS[i]
        return remote(
            i, coefs.at[1, pl.ds(rows, rows)], coefs.at[1 - dn, pl.ds((1 - dl) * rows, rows)], coef_send, coef_recv
        )

    spots, corner_size = corner_spots()

    def field_copy(i):
        dl, dn = WAYS[i]
        if dn == 0:
            start = 0 if dl < 0 else (rows - STEPS) * layers
            src = laid.at[pl.ds(start, STEPS * layers)]
            dst = far_rows.at[i]
        elif dl == 0:
            src = side_out.at[i - 2, pl.ds(0, rows * STEPS)]
            dst = side_in.at[i - 2, pl.ds(PAD, rows * STEPS)]
        else:
            src = corner_out.at[i - 4, pl.ds(0, corner_size)]
            dst = corner_in.at[i - 4, pl.ds(PAD, corner_size)]
        return remote(i, src, dst, send_sem, recv_sem)

    loads[1].wait()
    loads[2].wait()
    coefs[1, pl.ds(rows, rows), :] = kappa[...] * mask[...].astype(jnp.float32)
    north, south = (lat > 0).astype(jnp.int32), (lat < n_lat - 1).astype(jnp.int32)
    pl.semaphore_wait(barrier, 2 + 3 * (north + south))
    for i, way in enumerate(WAYS):
        guard(way[0], lambda i=i: coef_copy(i).start())

    loads[0].wait()
    for r in range(rows):
        here = coefs[1, pl.ds(rows + r, 1), :]
        for g in range(layers // SUB):
            laid[pl.ds(r * layers + g * SUB, SUB), :] = (
                control[pl.ds(g * SUB * rows + r, SUB, stride=rows), :] * here
            )
    guard(-1, lambda: field_copy(0).start())
    guard(1, lambda: field_copy(1).start())

    def upright(block):
        return jnp.concatenate([block, block[: LANES - layers]], axis=0).T

    def main_row(r, carry):
        block = laid[aligned(r * layers, layers), :]
        near[aligned((r + STEPS) * PITCH + PAD, LANES), :] = upright(block)
        return carry

    lax.fori_loop(0, rows, main_row, 0, unroll=2)
    for k, first in ((0, PAD), (1, PAD + LANES - STEPS)):
        for r in range(rows):
            side_out[k, pl.ds(r * STEPS, PAD), :] = near[
                pl.ds((r + STEPS) * PITCH + first, PAD), :
            ]
    guard(0, lambda: field_copy(2).start())
    guard(0, lambda: field_copy(3).start())
    for i in range(4, 8):
        dl, dn = WAYS[i]
        for d, at, count in spots:
            r = d - 1 if dl < 0 else rows - d
            first = PAD if dn < 0 else PAD + LANES - count
            corner_out[i - 4, pl.ds(at, PAD), :] = near[pl.ds((r + STEPS) * PITCH + first, PAD), :]
        guard(dl, lambda i=i: field_copy(i).start())

    for i, way in enumerate(WAYS):
        guard(-way[0], lambda i=i: coef_copy(i).wait_recv())
    weigh(rows, coefs, held)
    broaden(rows, held, 0, c0)
    broaden(rows, held, 1, k2)
    loads[4].wait()
    loads[5].wait()
    turn(off, weight, off_t, w_t)

    for i in (0, 1):
        guard(-WAYS[i][0], lambda i=i: field_copy(i).wait_recv())
        start = (STEPS + rows) if i == 0 else 0

        def far_row(r, carry, i=i, start=start):
            block = far_rows[i, aligned(r * layers, layers), :]
            near[aligned((r + start) * PITCH + PAD, LANES), :] = upright(block)
            return carry

        lax.fori_loop(0, STEPS, far_row, 0, unroll=2)
    for i in (2, 3):
        field_copy(i).wait_recv()
        for r in range(rows):
            base = (r + STEPS) * PITCH
            if i == 3:
                near[pl.ds(base, PAD), :] = side_in[1, pl.ds((r + 1) * STEPS, PAD), :]
            else:
                near[pl.ds(base + PAD + LANES, PAD), :] = side_in[0, pl.ds(PAD + r * STEPS, PAD), :]
    for i in range(4, 8):
        dl, dn = WAYS[i]
        guard(-dl, lambda i=i: field_copy(i).wait_recv())
        for d in range(1, STEPS + 1):
            at, count = spots[d - 1][1:] if d < STEPS else (0, 0)
            r = STEPS + rows + d - 1 if dl < 0 else STEPS - d
            if dn > 0:
                near[pl.ds(r * PITCH, PAD), :] = corner_in[i - 4, pl.ds(at + count, PAD), :]
            else:
                near[pl.ds(r * PITCH + PAD + LANES, PAD), :] = corner_in[i - 4, pl.ds(PAD + at, PAD), :]

    diffuse(rows, near, far, c0, k2)

    def back_row(r, carry):
        done[aligned(r * LANES, LANES), :] = near[aligned((r + STEPS) * PITCH + PAD, LANES), :].T
        return carry

    lax.fori_loop(0, rows, back_row, 0, unroll=2)
    loads[3].wait()
    solve_columns(rows, layers, done, control, coefs.at[1], vert, inc_ref)
    for i, way in enumerate(WAYS):
        guard(way[0], lambda i=i: coef_copy(i).wait_send())
        guard(way[0], lambda i=i: field_copy(i).wait_send())


def pick(table, row, col):
    level = [jnp.take_along_axis(t, col, axis=1) for t in table]
    bit = 1
    while len(level) > 1:
        odd = (row & bit) != 0
        level = [jnp.where(odd, level[i + 1], level[i]) for i in range(0, len(level), 2)]
        bit *= 2
    return level[0]


def lookup_kernel(rows, layers, owners, inc_ref, off_t, w_t, out_ref, acc):
    blocks = out_ref.shape[0] // owners
    cap = blocks * LANES
    groups = off_t.shape[0]
    turns = -(-cap // layers)

    def one_group(lg, carry):
        base = pl.multiple_of(lg * SUB, SUB)
        table = [inc_ref[pl.ds(base * rows + r, SUB, stride=rows), :] for r in range(rows)]
        for m in range(turns):
            at = pl.ds(m * layers + base, SUB)
            total = None
            for g in range(groups):
                idx = off_t[g, at, :]
                term = pick(table, idx >> 7, idx & (LANES - 1)) * w_t[g, at, :]
                total = term if total is None else total + term
            acc[at, :] = total
        return carry

    lax.fori_loop(0, layers // SUB, one_group, 0, unroll=2)
    for c in range(cap // LANES):
        here = pl.ds(c * LANES, LANES)
        block = acc[here, :].T
        total = block[:owners]
        for k in range(1, LANES // owners):
            total = total + block[k * owners : (k + 1) * owners]
        out_ref[pl.ds(c, owners, stride=blocks), :] = total


def local_call(kernel, shapes, count, scratch=(), name=None):
    return pl.pallas_call(
        kernel,
        out_shape=shapes,
        in_specs=[pl.BlockSpec(memory_space=pltpu.VMEM)] * count,
        out_specs=jax.tree.map(lambda _: pl.BlockSpec(memory_space=pltpu.VMEM), shapes),
        scratch_shapes=list(scratch),
        compiler_params=pltpu.CompilerParams(vmem_limit_bytes=40 * 1024 * 1024),
        name=name,
    )


def floats(*shape):
    return jax.ShapeDtypeStruct(shape, jnp.float32)


def columns_and_partials(control, kappa, sea_mask, vert_coef, offsets, weights):
    levels, fields, rows, cols = control.shape
    layers = levels * fields
    tall = rows + 2 * STEPS
    sten, owners, cap = offsets.shape
    bundles = sten * owners // LANES
    padded = -(-cap // layers) * layers
    corner = corner_spots()[1] + 2 * PAD
    vmem = pltpu.VMEM
    wide = (tall * PITCH, LANES)
    shapes = (
        floats(layers * rows, LANES),
        jax.ShapeDtypeStruct((bundles, padded, LANES), jnp.int32),
        floats(bundles, padded, LANES),
    )
    increment, off_t, w_t = pl.pallas_call(
        functools.partial(field_kernel, lax.axis_size("lat"), lax.axis_size("lon"), rows, layers),
        out_shape=shapes,
        in_specs=[pl.BlockSpec(memory_space=pl.ANY)] * 6,
        out_specs=tuple(pl.BlockSpec(memory_space=pltpu.VMEM) for _ in shapes),
        scratch_shapes=[
            vmem((layers * rows, LANES), jnp.float32),
            vmem((rows, LANES), jnp.float32),
            vmem((rows, LANES), jnp.int32),
            vmem((levels * rows, LANES), jnp.float32),
            vmem((sten * owners, cap), jnp.int32),
            vmem((sten * owners, cap), jnp.float32),
            vmem((3, 3 * rows, LANES), jnp.float32),
            vmem((2, 3, 40, LANES), jnp.float32),
            vmem((rows * layers, LANES), jnp.float32),
            vmem((2, STEPS * layers, LANES), jnp.float32),
            vmem((2, rows * STEPS + 2 * PAD, LANES), jnp.float32),
            vmem((2, rows * STEPS + 2 * PAD, LANES), jnp.float32),
            vmem((4, corner, LANES), jnp.float32),
            vmem((4, corner, LANES), jnp.float32),
            vmem(wide, jnp.float32),
            vmem(wide, jnp.float32),
            vmem(wide, jnp.float32),
            vmem(wide, jnp.float32),
            vmem((rows * LANES, LANES), jnp.float32),
            pltpu.SemaphoreType.DMA((6,)),
            pltpu.SemaphoreType.DMA((len(WAYS),)),
            pltpu.SemaphoreType.DMA((len(WAYS),)),
            pltpu.SemaphoreType.DMA((len(WAYS),)),
            pltpu.SemaphoreType.DMA((len(WAYS),)),
        ],
        compiler_params=pltpu.CompilerParams(
            vmem_limit_bytes=48 * 1024 * 1024, collective_id=2, has_side_effects=True
        ),
        name="field",
    )(
        control.reshape(layers * rows, cols),
        kappa,
        sea_mask,
        vert_coef.reshape(levels * rows, cols),
        offsets.reshape(sten * owners, cap),
        weights.reshape(sten * owners, cap),
    )
    partial_value = local_call(
        functools.partial(lookup_kernel, rows, layers, owners),
        floats(owners * cap // LANES, LANES),
        3,
        [vmem((padded, LANES), jnp.float32)],
        name="lookup",
    )(increment, off_t, w_t)
    return increment.reshape(control.shape), partial_value.reshape(owners, cap // LANES, LANES)


def spread(v, t, high):
    cap = v.shape[1]
    hit = lax.broadcasted_iota(jnp.int32, (high, cap), 0) == (t >> 7)
    ones = lax.broadcasted_iota(jnp.int32, (LANES, cap), 0) == (t & (LANES - 1))
    first = v.astype(jnp.bfloat16).astype(jnp.float32)
    left = jnp.concatenate(
        [jnp.where(hit, part, 0.0).astype(jnp.bfloat16) for part in (first, v - first)], axis=0
    )
    right = jnp.where(ones, 1.0, 0.0).astype(jnp.bfloat16)
    return lax.dot_general(
        left, right, (((1,), (1,)), ((), ())), preferred_element_type=jnp.float32
    )


def owner_kernel(n_lon, devices, part_ref, tgt_ref, obs_ref, err_ref, out_ref, recv, acc, send_sem, recv_sem):
    high = obs_ref.shape[0]
    blocks = part_ref.shape[1]
    me = lax.axis_index("lat") * n_lon + lax.axis_index("lon")

    def place(q):
        return (q // n_lon, q % n_lon)

    def copy(k):
        q = lax.rem(me + k, devices)
        return pltpu.make_async_remote_copy(
            src_ref=part_ref.at[q],
            dst_ref=recv.at[k],
            send_sem=send_sem.at[k],
            recv_sem=recv_sem.at[k],
            device_id=place(q),
            device_id_type=pl.DeviceIdType.MESH,
        )

    barrier = pltpu.get_barrier_semaphore()

    def greet(k, carry):
        q = lax.rem(me + k, devices)
        pl.semaphore_signal(
            barrier, inc=1, device_id=place(q), device_id_type=pl.DeviceIdType.MESH
        )
        return carry

    lax.fori_loop(1, devices, greet, 0)
    recv[0] = part_ref[me]
    acc[...] = jnp.zeros_like(acc)
    pl.semaphore_wait(barrier, devices - 1)

    def send(k, carry):
        copy(k).start()
        return carry

    lax.fori_loop(1, devices, send, 0)

    def add(k):
        p = lax.rem(me - k + devices, devices)
        cells = recv[k]
        v = jnp.concatenate([cells[c : c + 1, :] for c in range(blocks)], axis=1)
        acc[...] += spread(v, tgt_ref[pl.ds(p, 1), :], high)

    add(0)

    def one_source(k, carry):
        copy(k).wait_recv()
        add(k)
        return carry

    lax.fori_loop(1, devices, one_source, 0)

    def drain(k, carry):
        copy(k).wait_send()
        return carry

    lax.fori_loop(1, devices, drain, 0)
    out_ref[...] = (acc[:high] + acc[high:] - obs_ref[...]) * err_ref[...]


def owner_misfit(partial_value, target, observed, inv_error):
    high = observed.shape[0] // LANES
    devices, blocks, _ = partial_value.shape
    out = pl.pallas_call(
        functools.partial(owner_kernel, lax.axis_size("lon"), devices),
        out_shape=jax.ShapeDtypeStruct((high, LANES), jnp.float32),
        in_specs=[pl.BlockSpec(memory_space=pltpu.VMEM)] * 4,
        out_specs=pl.BlockSpec(memory_space=pltpu.VMEM),
        scratch_shapes=[
            pltpu.VMEM(partial_value.shape, jnp.float32),
            pltpu.VMEM((2 * high, LANES), jnp.float32),
            pltpu.SemaphoreType.DMA((devices,)),
            pltpu.SemaphoreType.DMA((devices,)),
        ],
        compiler_params=pltpu.CompilerParams(
            vmem_limit_bytes=32 * 1024 * 1024, collective_id=1, has_side_effects=True
        ),
        name="owner_misfit",
    )(partial_value, target, observed.reshape(high, LANES), inv_error.reshape(high, LANES))
    return out.reshape(-1)


def per_device(
    control,
    kappa,
    sea_mask,
    vert_coef,
    stencil_offsets,
    stencil_weights,
    slot_target,
    observed,
    inv_error,
):
    increment, partial_value = columns_and_partials(
        control, kappa, sea_mask, vert_coef, stencil_offsets, stencil_weights
    )
    misfit = owner_misfit(partial_value, slot_target, observed, inv_error)
    return (increment, misfit)


def solution(mesh):
    return jax.shard_map(
        per_device,
        mesh=mesh,
        in_specs=(
            P(None, None, "lat", "lon"),
            P("lat", "lon"),
            P("lat", "lon"),
            P(None, "lat", "lon"),
            P(None, ("lat", "lon"), None),
            P(None, ("lat", "lon"), None),
            P(("lat", "lon"), None),
            P(("lat", "lon")),
            P(("lat", "lon")),
        ),
        out_specs=(P(None, None, "lat", "lon"), P(("lat", "lon"))),
        check_vma=False,
    )
```

```python
import functools

import jax
import jax.numpy as jnp
from jax import lax
from jax.experimental import pallas as pl
from jax.experimental.pallas import tpu as pltpu
from jax.sharding import PartitionSpec as P

STEPS = 10
LANES = 128
SUB = 8


CHUNKS = 2
GROUP = 8
WAYS = ((-1, 0), (1, 0), (0, -1), (0, 1), (-1, -1), (-1, 1), (1, -1), (1, 1))
PAD = 16
PITCH = LANES + 2 * PAD


def aligned(start, size):
    return pl.ds(pl.multiple_of(start, SUB), size)


def corner_spots():
    spots, at = [], 0
    for d in range(1, STEPS):
        spots.append((d, at, STEPS - d))
        at += STEPS - d
    return spots, -(-at // SUB) * SUB


def update(old, new, c0, k2, count, first, low, high):
    def two_rows(turn, carry):
        base = (first + 2 * turn) * PITCH
        for v in range(low, high):
            spot = [aligned(base + d * PITCH + v * SUB, SUB) for d in range(-1, 3)]
            cells = [old[s, :] for s in spot]
            for d in range(2):
                at = base + d * PITCH + v * SUB
                side = old[pl.ds(at - 1, SUB), :] + old[pl.ds(at + 1, SUB), :]
                around = (cells[d] + cells[d + 2]) + side
                new[spot[d + 1], :] = c0[spot[d + 1], :] * cells[d + 1] + k2[spot[d + 1], :] * around
        return carry

    lax.fori_loop(0, count, two_rows, 0)


def diffuse(rows, old, new, c0, k2):
    tall = rows + 2 * STEPS
    width = PITCH // SUB
    update(old, new, c0, k2, (tall - 2) // 2, 1, 0, width)
    update(new, old, c0, k2, (tall - 4) // 2, 2, 1, width - 1)

    def two_steps(s, carry):
        first = 2 * s + 1
        update(old, new, c0, k2, (tall - 2 * first) // 2, first, 1, width - 1)
        update(new, old, c0, k2, (tall - 2 * first - 2) // 2, first + 1, 1, width - 1)
        return carry

    lax.fori_loop(1, STEPS // 2, two_steps, 0)


def solve_columns(rows, layers, done, control, coef, vert_ref, inc_ref):
    levels = vert_ref.shape[0] // rows
    fields = layers // levels
    for h in range(rows // SUB):
        here = coef[pl.ds(rows + h * SUB, SUB), :]
        sea = here != 0.0
        back = 1.0 / jnp.where(sea, here, 1.0)
        ratio = []
        above = vert_ref[pl.ds(h * SUB, SUB), :]
        cprev = jnp.zeros((SUB, LANES), jnp.float32)
        prev = [cprev] * fields
        for k in range(levels):
            if k + 1 < levels:
                below = vert_ref[pl.ds((k + 1) * rows + h * SUB, SUB), :]
            else:
                below = jnp.zeros((SUB, LANES), jnp.float32)
            inv = 1.0 / (((1.0 + above) + below) + above * cprev)
            cprev = -below * inv
            ratio.append(cprev)
            for f in range(fields):
                layer = k * fields + f
                at = pl.ds(layer * rows + h * SUB, SUB)
                right = done[pl.ds(h * SUB * LANES + layer, SUB, stride=LANES), :] * back
                right = jnp.where(sea, right, control[at, :])
                prev[f] = (right + above * prev[f]) * inv
                inc_ref[at, :] = prev[f]
            above = below
        for k in range(levels - 2, -1, -1):
            for f in range(fields):
                at = pl.ds((k * fields + f) * rows + h * SUB, SUB)
                prev[f] = inc_ref[at, :] - ratio[k] * prev[f]
                inc_ref[at, :] = prev[f]


def weigh(rows, coefs, held):
    lane = lax.broadcasted_iota(jnp.int32, (40, LANES), 1)
    mid = pl.ds(rows - STEPS + 1, 40)
    up = pl.ds(rows - STEPS, 40)
    down = pl.ds(rows - STEPS + 2, 40)
    here = [coefs[k, mid, :] for k in range(3)]
    right = [pltpu.roll(c, 1, 1) for c in here]
    left = [pltpu.roll(c, LANES - 1, 1) for c in here]
    first, last = lane == 0, lane == LANES - 1
    wests = [right[0], jnp.where(first, right[0], right[1]), jnp.where(first, right[1], right[2])]
    easts = [jnp.where(last, left[1], left[0]), jnp.where(last, left[2], left[1]), left[2]]
    for k in range(3):
        around = (coefs[k, up, :] + coefs[k, down, :]) + (wests[k] + easts[k])
        held[0, k, :, :] = 1.0 - here[k] * around
        held[1, k, :, :] = here[k] * here[k]


def broaden(rows, held, kind, out):
    lane = lax.broadcasted_iota(jnp.int32, (40, LANES), 1)
    rest = jnp.zeros((LANES - 40, LANES), jnp.float32)
    main = jnp.concatenate([held[kind, 1, :, :], rest], axis=0).T
    outer = jnp.where(lane >= LANES - PAD, held[kind, 0, :, :], held[kind, 2, :, :])
    outer = jnp.concatenate([outer, rest], axis=0).T
    for j in range(rows + 2 * STEPS - 2):
        base = (j + 1) * PITCH
        column = outer[:, j : j + 1]
        out[pl.ds(base, PAD), :] = jnp.broadcast_to(column[LANES - PAD :], (PAD, LANES))
        out[pl.ds(base + PAD, LANES), :] = jnp.broadcast_to(main[:, j : j + 1], (LANES, LANES))
        out[pl.ds(base + PAD + LANES, PAD), :] = jnp.broadcast_to(column[:PAD], (PAD, LANES))


def turn(off_ref, w_ref, off_t, w_t):
    cap = off_ref.shape[1]
    groups = off_ref.shape[0] // LANES
    padded = off_t.shape[1]
    if padded > cap:
        for g in range(groups):
            off_t[g, cap:padded, :] = jnp.zeros((padded - cap, LANES), jnp.int32)
            w_t[g, cap:padded, :] = jnp.zeros((padded - cap, LANES), jnp.float32)
    for g in range(groups):
        for c in range(cap // LANES):
            here = pl.ds(c * LANES, LANES)
            off_t[g, here, :] = off_ref[pl.ds(g * LANES, LANES), here].T
            w_t[g, here, :] = w_ref[pl.ds(g * LANES, LANES), here].T


def step_kernel(
    n_lat,
    n_lon,
    rows,
    layers,
    control_ref,
    kappa_ref,
    mask_ref,
    vert_ref,
    off_ref,
    w_ref,
    target_ref,
    inc_ref,
    value_ref,
    control,
    kappa,
    mask,
    vert,
    off,
    weight,
    target,
    off_t,
    w_t,
    acc,
    parts,
    received,
    total,
    coefs,
    held,
    laid,
    far_rows,
    side_out,
    side_in,
    corner_out,
    corner_in,
    near,
    far,
    c0,
    k2,
    done,
    load_sem,
    coef_send,
    coef_recv,
    send_sem,
    recv_sem,
    part_send,
    part_recv,
):
    lat, lon = lax.axis_index("lat"), lax.axis_index("lon")
    me, devices = lat * n_lon + lon, n_lat * n_lon
    tall = rows + 2 * STEPS
    pairs = ((control_ref, control), (kappa_ref, kappa), (mask_ref, mask))
    pairs += ((vert_ref, vert), (off_ref, off), (w_ref, weight), (target_ref, target))
    loads = [pltpu.make_async_copy(a, b, load_sem.at[i]) for i, (a, b) in enumerate(pairs)]
    for i in (1, 2, 0, 3, 4, 5, 6):
        loads[i].start()

    def place(i):
        return (lat + WAYS[i][0], lax.rem(lon + WAYS[i][1] + n_lon, n_lon))

    def guard(step, body):
        if step == 0:
            body()
        else:
            pl.when(lat > 0 if step < 0 else lat < n_lat - 1)(body)

    side_in[...] = jnp.zeros_like(side_in)
    corner_in[...] = jnp.zeros_like(corner_in)

    @pl.when(lat == 0)
    def _():
        coefs[:, :rows, :] = jnp.zeros((3, rows, LANES), jnp.float32)
        far_rows[1] = jnp.zeros((STEPS * layers, LANES), jnp.float32)

    @pl.when(lat == n_lat - 1)
    def _():
        coefs[:, 2 * rows :, :] = jnp.zeros((3, rows, LANES), jnp.float32)
        far_rows[0] = jnp.zeros((STEPS * layers, LANES), jnp.float32)

    barrier = pltpu.get_barrier_semaphore()
    def owner(k):
        q = lax.rem(me + k, devices)
        return q, (q // n_lon, q % n_lon)

    def greet(k, carry):
        pl.semaphore_signal(
            barrier, inc=1, device_id=owner(k)[1], device_id_type=pl.DeviceIdType.MESH
        )
        return carry

    lax.fori_loop(1, devices, greet, 0)

    def remote(i, src, dst, out_sem, in_sem):
        return pltpu.make_async_remote_copy(
            src_ref=src,
            dst_ref=dst,
            send_sem=out_sem.at[i],
            recv_sem=in_sem.at[i],
            device_id=place(i),
            device_id_type=pl.DeviceIdType.MESH,
        )

    def coef_copy(i):
        dl, dn = WAYS[i]
        return remote(
            i, coefs.at[1, pl.ds(rows, rows)], coefs.at[1 - dn, pl.ds((1 - dl) * rows, rows)], coef_send, coef_recv
        )

    spots, corner_size = corner_spots()

    def field_copy(i):
        dl, dn = WAYS[i]
        if dn == 0:
            start = 0 if dl < 0 else (rows - STEPS) * layers
            src = laid.at[pl.ds(start, STEPS * layers)]
            dst = far_rows.at[i]
        elif dl == 0:
            src = side_out.at[i - 2, pl.ds(0, rows * STEPS)]
            dst = side_in.at[i - 2, pl.ds(PAD, rows * STEPS)]
        else:
            src = corner_out.at[i - 4, pl.ds(0, corner_size)]
            dst = corner_in.at[i - 4, pl.ds(PAD, corner_size)]
        return remote(i, src, dst, send_sem, recv_sem)

    loads[1].wait()
    loads[2].wait()
    coefs[1, pl.ds(rows, rows), :] = kappa[...] * mask[...].astype(jnp.float32)
    pl.semaphore_wait(barrier, devices - 1)
    for i, way in enumerate(WAYS):
        guard(way[0], lambda i=i: coef_copy(i).start())

    loads[0].wait()
    for r in range(rows):
        here = coefs[1, pl.ds(rows + r, 1), :]
        for g in range(layers // SUB):
            laid[pl.ds(r * layers + g * SUB, SUB), :] = (
                control[pl.ds(g * SUB * rows + r, SUB, stride=rows), :] * here
            )
    guard(-1, lambda: field_copy(0).start())
    guard(1, lambda: field_copy(1).start())

    def upright(block):
        return jnp.concatenate([block, block[: LANES - layers]], axis=0).T

    def main_row(r, carry):
        block = laid[aligned(r * layers, layers), :]
        near[aligned((r + STEPS) * PITCH + PAD, LANES), :] = upright(block)
        return carry

    lax.fori_loop(0, rows, main_row, 0, unroll=2)
    for k, first in ((0, PAD), (1, PAD + LANES - STEPS)):
        for r in range(rows):
            side_out[k, pl.ds(r * STEPS, PAD), :] = near[
                pl.ds((r + STEPS) * PITCH + first, PAD), :
            ]
    guard(0, lambda: field_copy(2).start())
    guard(0, lambda: field_copy(3).start())
    for i in range(4, 8):
        dl, dn = WAYS[i]
        for d, at, count in spots:
            r = d - 1 if dl < 0 else rows - d
            first = PAD if dn < 0 else PAD + LANES - count
            corner_out[i - 4, pl.ds(at, PAD), :] = near[pl.ds((r + STEPS) * PITCH + first, PAD), :]
        guard(dl, lambda i=i: field_copy(i).start())

    for i, way in enumerate(WAYS):
        guard(-way[0], lambda i=i: coef_copy(i).wait_recv())
    weigh(rows, coefs, held)
    broaden(rows, held, 0, c0)
    broaden(rows, held, 1, k2)
    loads[4].wait()
    loads[5].wait()
    turn(off, weight, off_t, w_t)

    for i in (0, 1):
        guard(-WAYS[i][0], lambda i=i: field_copy(i).wait_recv())
        start = (STEPS + rows) if i == 0 else 0

        def far_row(r, carry, i=i, start=start):
            block = far_rows[i, aligned(r * layers, layers), :]
            near[aligned((r + start) * PITCH + PAD, LANES), :] = upright(block)
            return carry

        lax.fori_loop(0, STEPS, far_row, 0, unroll=2)
    for i in (2, 3):
        field_copy(i).wait_recv()
        for r in range(rows):
            base = (r + STEPS) * PITCH
            if i == 3:
                near[pl.ds(base, PAD), :] = side_in[1, pl.ds((r + 1) * STEPS, PAD), :]
            else:
                near[pl.ds(base + PAD + LANES, PAD), :] = side_in[0, pl.ds(PAD + r * STEPS, PAD), :]
    for i in range(4, 8):
        dl, dn = WAYS[i]
        guard(-dl, lambda i=i: field_copy(i).wait_recv())
        for d in range(1, STEPS + 1):
            at, count = spots[d - 1][1:] if d < STEPS else (0, 0)
            r = STEPS + rows + d - 1 if dl < 0 else STEPS - d
            if dn > 0:
                near[pl.ds(r * PITCH, PAD), :] = corner_in[i - 4, pl.ds(at + count, PAD), :]
            else:
                near[pl.ds(r * PITCH + PAD + LANES, PAD), :] = corner_in[i - 4, pl.ds(PAD + at, PAD), :]

    diffuse(rows, near, far, c0, k2)

    def back_row(r, carry):
        done[aligned(r * LANES, LANES), :] = near[aligned((r + STEPS) * PITCH + PAD, LANES), :].T
        return carry

    lax.fori_loop(0, rows, back_row, 0, unroll=2)
    loads[3].wait()
    solve_columns(rows, layers, done, control, coefs.at[1], vert, inc_ref)
    for i, way in enumerate(WAYS):
        guard(way[0], lambda i=i: coef_copy(i).wait_send())
        guard(way[0], lambda i=i: field_copy(i).wait_send())

    def part_copy(c, k):
        q, there = owner(k)
        return pltpu.make_async_remote_copy(
            src_ref=parts.at[c, q],
            dst_ref=received.at[c, k],
            send_sem=part_send.at[c, k],
            recv_sem=part_recv.at[c, k],
            device_id=there,
            device_id_type=pl.DeviceIdType.MESH,
        )

    blocks, high = parts.shape[2], value_ref.shape[0]
    size = blocks * LANES
    turns = off_t.shape[1] // layers
    done_turns = 0
    total[...] = jnp.zeros_like(total)
    for c in range(CHUNKS):
        last = min(turns, -(-(c + 1) * size // layers))
        lookup(rows, layers, range(done_turns, last), inc_ref, off_t, w_t, acc)
        done_turns = last
        for b in range(blocks):
            block = acc[pl.ds(c * size + b * LANES, LANES), :].T
            part = block[:devices]
            for k in range(1, LANES // devices):
                part = part + block[k * devices : (k + 1) * devices]
            parts[c, :, b, :] = part
        received[c, 0] = parts[c, me]

        def send(k, carry, c=c):
            part_copy(c, k).start()
            return carry

        lax.fori_loop(1, devices, send, 0)

    loads[6].wait()
    for c in range(CHUNKS):

        def add_group(g, carry, c=c):
            result = total[...]
            for k in range(GROUP):
                k = g * GROUP + k
                pl.when(k > 0)(lambda k=k: part_copy(c, k).wait_recv())
            for k in range(GROUP):
                k = g * GROUP + k
                p = lax.rem(me - k + devices, devices)
                cells = received[c, k]
                v = jnp.concatenate([cells[b : b + 1, :] for b in range(blocks)], axis=1)
                result = result + spread(v, target[pl.ds(p, 1), c * size : (c + 1) * size], high)
            total[...] = result
            return carry

        lax.fori_loop(0, devices // GROUP, add_group, 0)
    value_ref[...] = total[:high] + total[high:]
    for c in range(CHUNKS):

        def drain(k, carry, c=c):
            part_copy(c, k).wait_send()
            return carry

        lax.fori_loop(1, devices, drain, 0)


def pick(table, row, col):
    level = [jnp.take_along_axis(t, col, axis=1) for t in table]
    bit = 1
    while len(level) > 1:
        odd = (row & bit) != 0
        level = [jnp.where(odd, level[i + 1], level[i]) for i in range(0, len(level), 2)]
        bit *= 2
    return level[0]


def lookup(rows, layers, turns, inc_ref, off_t, w_t, acc):
    groups = off_t.shape[0]

    def one_group(lg, carry):
        base = pl.multiple_of(lg * SUB, SUB)
        table = [inc_ref[pl.ds(base * rows + r, SUB, stride=rows), :] for r in range(rows)]
        for m in turns:
            at = pl.ds(m * layers + base, SUB)
            total = None
            for g in range(groups):
                idx = off_t[g, at, :]
                term = pick(table, idx >> 7, idx & (LANES - 1)) * w_t[g, at, :]
                total = term if total is None else total + term
            acc[at, :] = total
        return carry

    lax.fori_loop(0, layers // SUB, one_group, 0, unroll=2)


def floats(*shape):
    return jax.ShapeDtypeStruct(shape, jnp.float32)


def spread(v, t, high):
    shape, bf = (high, v.shape[1]), jnp.bfloat16
    flat = (LANES, v.shape[1])
    upper = lax.broadcasted_iota(jnp.int32, shape, 0).astype(bf)
    lower = lax.broadcasted_iota(jnp.int32, flat, 0).astype(bf)
    hit = upper == jnp.broadcast_to((t >> 7).astype(jnp.float32), shape).astype(bf)
    one = lower == jnp.broadcast_to((t & (LANES - 1)).astype(jnp.float32), flat).astype(bf)
    first = v.astype(bf).astype(jnp.float32)
    left = jnp.concatenate(
        [
            jnp.where(hit, jnp.broadcast_to(part, shape).astype(bf), jnp.zeros(shape, bf))
            for part in (first, v - first)
        ],
        axis=0,
    )
    right = jnp.where(one, jnp.ones(flat, bf), jnp.zeros(flat, bf))
    return lax.dot_general(
        left, right, (((1,), (1,)), ((), ())), preferred_element_type=jnp.float32
    )


def per_device(
    control,
    kappa,
    sea_mask,
    vert_coef,
    stencil_offsets,
    stencil_weights,
    slot_target,
    observed,
    inv_error,
):
    levels, fields, rows, cols = control.shape
    layers = levels * fields
    tall = rows + 2 * STEPS
    sten, owners, cap = stencil_offsets.shape
    bundles = sten * owners // LANES
    padded = -(-cap // layers) * layers
    corner = corner_spots()[1] + 2 * PAD
    high = observed.shape[0] // LANES
    blocks = cap // LANES // CHUNKS

    def vmem(*shape, dtype=jnp.float32):
        return pltpu.VMEM(shape, dtype)

    wide = (tall * PITCH, LANES)
    dma = pltpu.SemaphoreType.DMA
    increment, value = pl.pallas_call(
        functools.partial(step_kernel, lax.axis_size("lat"), lax.axis_size("lon"), rows, layers),
        out_shape=(floats(layers * rows, LANES), floats(high, LANES)),
        in_specs=[pl.BlockSpec(memory_space=pltpu.HBM)] * 7,
        out_specs=(pl.BlockSpec(memory_space=pltpu.VMEM), pl.BlockSpec(memory_space=pltpu.VMEM)),
        scratch_shapes=[
            vmem(layers * rows, LANES),
            vmem(rows, LANES),
            vmem(rows, LANES, dtype=jnp.int32),
            vmem(levels * rows, LANES),
            vmem(sten * owners, cap, dtype=jnp.int32),
            vmem(sten * owners, cap),
            vmem(owners, cap, dtype=jnp.int32),
            vmem(bundles, padded, LANES, dtype=jnp.int32),
            vmem(bundles, padded, LANES),
            vmem(padded, LANES),
            vmem(CHUNKS, owners, blocks, LANES),
            vmem(CHUNKS, owners, blocks, LANES),
            vmem(2 * high, LANES),
            vmem(3, 3 * rows, LANES),
            vmem(2, 3, 40, LANES),
            vmem(rows * layers, LANES),
            vmem(2, STEPS * layers, LANES),
            vmem(2, rows * STEPS + 2 * PAD, LANES),
            vmem(2, rows * STEPS + 2 * PAD, LANES),
            vmem(4, corner, LANES),
            vmem(4, corner, LANES),
            vmem(*wide),
            vmem(*wide),
            vmem(*wide),
            vmem(*wide),
            vmem(rows * LANES, LANES),
            dma((7,)),
            dma((len(WAYS),)),
            dma((len(WAYS),)),
            dma((len(WAYS),)),
            dma((len(WAYS),)),
            dma((CHUNKS, owners)),
            dma((CHUNKS, owners)),
        ],
        compiler_params=pltpu.CompilerParams(
            vmem_limit_bytes=52 * 1024 * 1024, collective_id=2, has_side_effects=True
        ),
        name="assimilate",
    )(
        control.reshape(layers * rows, cols),
        kappa,
        sea_mask,
        vert_coef.reshape(levels * rows, cols),
        stencil_offsets.reshape(sten * owners, cap),
        stencil_weights.reshape(sten * owners, cap),
        slot_target,
    )
    return increment.reshape(control.shape), (value.reshape(-1) - observed) * inv_error


def solution(mesh):
    return jax.shard_map(
        per_device,
        mesh=mesh,
        in_specs=(
            P(None, None, "lat", "lon"),
            P("lat", "lon"),
            P("lat", "lon"),
            P(None, "lat", "lon"),
            P(None, ("lat", "lon"), None),
            P(None, ("lat", "lon"), None),
            P(("lat", "lon"), None),
            P(("lat", "lon")),
            P(("lat", "lon")),
        ),
        out_specs=(P(None, None, "lat", "lon"), P(("lat", "lon"))),
        check_vma=False,
    )
```

```python
import functools

import jax
import jax.numpy as jnp
from jax import lax
from jax.experimental import pallas as pl
from jax.experimental.pallas import tpu as pltpu
from jax.sharding import PartitionSpec as P

STEPS = 10
LANES = 128
SUB = 8


GROUP = 8
WAYS = ((-1, 0), (1, 0), (0, -1), (0, 1), (-1, -1), (-1, 1), (1, -1), (1, 1))
PAD = 16
PITCH = LANES + 2 * PAD


def aligned(start, size):
    return pl.ds(pl.multiple_of(start, SUB), size)


def corner_spots():
    spots, at = [], 0
    for d in range(1, STEPS):
        spots.append((d, at, STEPS - d))
        at += STEPS - d
    return spots, -(-at // SUB) * SUB


def corner_split():
    count = STEPS * (STEPS - 1) // 2
    return count - count // 3, count // 3


def side_split(rows):
    return (rows - rows // 3) * STEPS, rows // 3 * STEPS


def message(kept, few):
    return max(-(-kept // SUB), -(-few // SUB) + -(-few // SUB)) * SUB


def update(old, new, c0, k2, count, first, low, high, per):
    def some_rows(turn, carry):
        base = (first + per * turn) * PITCH
        for v in range(low, high):
            spot = [aligned(base + d * PITCH + v * SUB, SUB) for d in range(-1, per + 1)]
            cells = [old[s, :] for s in spot]
            for d in range(per):
                at = base + d * PITCH + v * SUB
                side = old[pl.ds(at - 1, SUB), :] + old[pl.ds(at + 1, SUB), :]
                around = (cells[d] + cells[d + 2]) + side
                new[spot[d + 1], :] = c0[spot[d + 1], :] * cells[d + 1] + k2[spot[d + 1], :] * around
        return carry

    lax.fori_loop(0, count, some_rows, 0)


def diffuse(rows, old, new, c0, k2):
    tall = rows + 2 * STEPS
    width = PITCH // SUB
    fours = (tall - 2) // 4
    update(old, new, c0, k2, fours, 1, 0, width, 4)
    if (tall - 2) % 4:
        update(old, new, c0, k2, 1, 1 + 4 * fours, 0, width, 2)
    update(new, old, c0, k2, -(-(tall - 4) // 4), 2, 1, width - 1, 4)

    def two_steps(s, carry):
        first = 2 * s + 1
        update(old, new, c0, k2, (tall - 2 * first + 2) // 4, first, 1, width - 1, 4)
        update(new, old, c0, k2, (tall - 2 * first) // 4, first + 1, 1, width - 1, 4)
        return carry

    lax.fori_loop(1, STEPS // 2, two_steps, 0)


def solve_columns(rows, layers, done, control, coef, vert_ref, inc_ref):
    levels = vert_ref.shape[0] // rows
    fields = layers // levels
    for h in range(rows // SUB):
        here = coef[pl.ds(rows + h * SUB, SUB), :]
        sea = here != 0.0
        back = 1.0 / jnp.where(sea, here, 1.0)
        ratio = []
        above = vert_ref[pl.ds(h * SUB, SUB), :]
        cprev = jnp.zeros((SUB, LANES), jnp.float32)
        prev = [cprev] * fields
        for k in range(levels):
            if k + 1 < levels:
                below = vert_ref[pl.ds((k + 1) * rows + h * SUB, SUB), :]
            else:
                below = jnp.zeros((SUB, LANES), jnp.float32)
            inv = 1.0 / (((1.0 + above) + below) + above * cprev)
            cprev = -below * inv
            ratio.append(cprev)
            for f in range(fields):
                layer = k * fields + f
                at = pl.ds(layer * rows + h * SUB, SUB)
                right = done[pl.ds(h * SUB * LANES + layer, SUB, stride=LANES), :] * back
                right = jnp.where(sea, right, control[at, :])
                prev[f] = (right + above * prev[f]) * inv
                inc_ref[at, :] = prev[f]
            above = below
        for k in range(levels - 2, -1, -1):
            for f in range(fields):
                at = pl.ds((k * fields + f) * rows + h * SUB, SUB)
                prev[f] = inc_ref[at, :] - ratio[k] * prev[f]
                inc_ref[at, :] = prev[f]


def weigh(rows, coefs, held):
    lane = lax.broadcasted_iota(jnp.int32, (40, LANES), 1)
    mid = pl.ds(rows - STEPS + 1, 40)
    up = pl.ds(rows - STEPS, 40)
    down = pl.ds(rows - STEPS + 2, 40)
    here = [coefs[k, mid, :] for k in range(3)]
    right = [pltpu.roll(c, 1, 1) for c in here]
    left = [pltpu.roll(c, LANES - 1, 1) for c in here]
    first, last = lane == 0, lane == LANES - 1
    wests = [right[0], jnp.where(first, right[0], right[1]), jnp.where(first, right[1], right[2])]
    easts = [jnp.where(last, left[1], left[0]), jnp.where(last, left[2], left[1]), left[2]]
    for k in range(3):
        around = (coefs[k, up, :] + coefs[k, down, :]) + (wests[k] + easts[k])
        held[0, k, :, :] = 1.0 - here[k] * around
        held[1, k, :, :] = here[k] * here[k]


def broaden(rows, held, kind, out):
    lane = lax.broadcasted_iota(jnp.int32, (40, LANES), 1)
    rest = jnp.zeros((LANES - 40, LANES), jnp.float32)
    main = jnp.concatenate([held[kind, 1, :, :], rest], axis=0).T
    outer = jnp.where(lane >= LANES - PAD, held[kind, 0, :, :], held[kind, 2, :, :])
    outer = jnp.concatenate([outer, rest], axis=0).T
    for j in range(rows + 2 * STEPS - 2):
        base = (j + 1) * PITCH
        column = outer[:, j : j + 1]
        out[pl.ds(base, PAD), :] = jnp.broadcast_to(column[LANES - PAD :], (PAD, LANES))
        out[pl.ds(base + PAD, LANES), :] = jnp.broadcast_to(main[:, j : j + 1], (LANES, LANES))
        out[pl.ds(base + PAD + LANES, PAD), :] = jnp.broadcast_to(column[:PAD], (PAD, LANES))


def turn(owners, off_ref, w_ref, off_t, w_t):
    cap = off_ref.shape[1]
    sten = off_ref.shape[0] // owners
    members = LANES // sten
    padded = off_t.shape[1]
    for g in range(owners // members):
        if padded > cap:
            off_t[g, cap:padded, :] = jnp.zeros((padded - cap, LANES), jnp.int32)
            w_t[g, cap:padded, :] = jnp.zeros((padded - cap, LANES), jnp.float32)
        for c in range(cap // LANES):
            here = pl.ds(c * LANES, LANES)
            for src, dst in ((off_ref, off_t), (w_ref, w_t)):
                dst[g, here, :] = jnp.concatenate(
                    [src[pl.ds(j * owners + g * members, members), here] for j in range(sten)], axis=0
                ).T


def squeeze(layers, kept, few, src, dst):
    spare = LANES - layers
    size = -(-few // SUB) * SUB
    whole = dst.shape[0]
    lane = lax.broadcasted_iota(jnp.int32, (size, LANES), 1)
    dst[...] = src[pl.ds(0, whole), :]
    rest = src[pl.ds(kept, size), :]
    dst[pl.ds(0, size), :] = jnp.where(lane < layers, src[pl.ds(0, size), :], rest)
    moved = pltpu.roll(rest, layers - spare, 1)
    dst[pl.ds(few, size), :] = jnp.where(lane < layers, src[pl.ds(few, size), :], moved)


def unsqueeze(layers, kept, few, src, dst):
    spare = LANES - layers
    size = -(-few // SUB) * SUB
    lane = lax.broadcasted_iota(jnp.int32, (size, LANES), 1)
    dst[pl.ds(PAD, src.shape[0]), :] = src[...]
    first = pltpu.roll(src[pl.ds(0, size), :], spare, 1)
    second = pltpu.roll(src[pl.ds(few, size), :], LANES - layers + spare, 1)
    dst[pl.ds(PAD + kept, size), :] = jnp.where(lane < spare, first, second)


def step_kernel(
    n_lat,
    n_lon,
    rows,
    layers,
    control_ref,
    kappa_ref,
    mask_ref,
    vert_ref,
    off_ref,
    w_ref,
    target_ref,
    inc_ref,
    value_ref,
    control,
    kappa,
    mask,
    vert,
    off,
    weight,
    target,
    off_t,
    w_t,
    acc,
    parts,
    received,
    total,
    coefs,
    held,
    laid,
    far_rows,
    side_out,
    side_in,
    corner_out,
    corner_in,
    side_sent,
    side_got,
    corner_sent,
    corner_got,
    near,
    far,
    c0,
    k2,
    done,
    load_sem,
    coef_send,
    coef_recv,
    send_sem,
    recv_sem,
    part_send,
    part_recv,
):
    lat, lon = lax.axis_index("lat"), lax.axis_index("lon")
    me, devices = lat * n_lon + lon, n_lat * n_lon
    tall = rows + 2 * STEPS
    pairs = ((control_ref, control), (kappa_ref, kappa), (mask_ref, mask))
    pairs += ((vert_ref, vert), (off_ref, off), (w_ref, weight), (target_ref, target))
    loads = [pltpu.make_async_copy(a, b, load_sem.at[i]) for i, (a, b) in enumerate(pairs)]
    for i in (1, 2, 0, 3, 4, 5, 6):
        loads[i].start()

    def place(i):
        return (lat + WAYS[i][0], lax.rem(lon + WAYS[i][1] + n_lon, n_lon))

    def guard(step, body):
        if step == 0:
            body()
        else:
            pl.when(lat > 0 if step < 0 else lat < n_lat - 1)(body)

    corner_got[...] = jnp.zeros_like(corner_got)
    barrier = pltpu.get_barrier_semaphore()
    def owner(k):
        q = lax.rem(me + k, devices)
        return q, (q // n_lon, q % n_lon)

    def greet(k, carry):
        pl.semaphore_signal(
            barrier, inc=1, device_id=owner(k)[1], device_id_type=pl.DeviceIdType.MESH
        )
        return carry

    lax.fori_loop(1, devices, greet, 0)

    side_in[...] = jnp.zeros_like(side_in)
    corner_in[...] = jnp.zeros_like(corner_in)

    @pl.when(lat == 0)
    def _():
        coefs[:, :rows, :] = jnp.zeros((3, rows, LANES), jnp.float32)
        far_rows[1] = jnp.zeros((STEPS * layers, LANES), jnp.float32)

    @pl.when(lat == n_lat - 1)
    def _():
        coefs[:, 2 * rows :, :] = jnp.zeros((3, rows, LANES), jnp.float32)
        far_rows[0] = jnp.zeros((STEPS * layers, LANES), jnp.float32)

    def remote(i, src, dst, out_sem, in_sem):
        return pltpu.make_async_remote_copy(
            src_ref=src,
            dst_ref=dst,
            send_sem=out_sem.at[i],
            recv_sem=in_sem.at[i],
            device_id=place(i),
            device_id_type=pl.DeviceIdType.MESH,
        )

    def coef_copy(i):
        dl, dn = WAYS[i]
        return remote(
            i, coefs.at[1, pl.ds(rows, rows)], coefs.at[1 - dn, pl.ds((1 - dl) * rows, rows)], coef_send, coef_recv
        )

    spots = corner_spots()[0]

    def field_copy(i):
        dl, dn = WAYS[i]
        if dn == 0:
            start = 0 if dl < 0 else (rows - STEPS) * layers
            src = laid.at[pl.ds(start, STEPS * layers)]
            dst = far_rows.at[i]
        elif dl == 0:
            src, dst = side_sent.at[i - 2], side_got.at[i - 2]
        else:
            src, dst = corner_sent.at[i - 4], corner_got.at[i - 4]
        return remote(i, src, dst, send_sem, recv_sem)

    loads[1].wait()
    loads[2].wait()
    coefs[1, pl.ds(rows, rows), :] = kappa[...] * mask[...].astype(jnp.float32)
    loads[0].wait()
    for r in range(rows):
        here = coefs[1, pl.ds(rows + r, 1), :]
        for g in range(layers // SUB):
            laid[pl.ds(r * layers + g * SUB, SUB), :] = (
                control[pl.ds(g * SUB * rows + r, SUB, stride=rows), :] * here
            )
    def upright(block):
        return jnp.concatenate([block, block[: LANES - layers]], axis=0).T

    def main_row(r, carry):
        block = laid[aligned(r * layers, layers), :]
        near[aligned((r + STEPS) * PITCH + PAD, LANES), :] = upright(block)
        return carry

    lax.fori_loop(0, rows, main_row, 0, unroll=2)
    for k, first in ((0, PAD), (1, PAD + LANES - STEPS)):
        for r in range(rows):
            side_out[k, pl.ds(r * STEPS, PAD), :] = near[
                pl.ds((r + STEPS) * PITCH + first, PAD), :
            ]
        squeeze(layers, *side_split(rows), side_out.at[k], side_sent.at[k])
    for i in range(4, 8):
        dl, dn = WAYS[i]
        for d, at, count in spots:
            r = d - 1 if dl < 0 else rows - d
            first = PAD if dn < 0 else PAD + LANES - count
            corner_out[i - 4, pl.ds(at, PAD), :] = near[pl.ds((r + STEPS) * PITCH + first, PAD), :]
        squeeze(layers, *corner_split(), corner_out.at[i - 4], corner_sent.at[i - 4])
    pl.semaphore_wait(barrier, devices - 1)
    for i, way in enumerate(WAYS):
        guard(way[0], lambda i=i: coef_copy(i).start())
    for i in (2, 3, 0, 1, 4, 5, 6, 7):
        guard(WAYS[i][0], lambda i=i: field_copy(i).start())

    for i, way in enumerate(WAYS):
        guard(-way[0], lambda i=i: coef_copy(i).wait_recv())
    weigh(rows, coefs, held)
    broaden(rows, held, 0, c0)
    broaden(rows, held, 1, k2)
    loads[4].wait()
    loads[5].wait()
    turn(devices, off, weight, off_t, w_t)

    for i in (0, 1):
        guard(-WAYS[i][0], lambda i=i: field_copy(i).wait_recv())
        start = (STEPS + rows) if i == 0 else 0

        def far_row(r, carry, i=i, start=start):
            block = far_rows[i, aligned(r * layers, layers), :]
            near[aligned((r + start) * PITCH + PAD, LANES), :] = upright(block)
            return carry

        lax.fori_loop(0, STEPS, far_row, 0, unroll=2)
    for i in (2, 3):
        field_copy(i).wait_recv()
        unsqueeze(layers, *side_split(rows), side_got.at[i - 2], side_in.at[i - 2])
        for r in range(rows):
            base = (r + STEPS) * PITCH
            if i == 3:
                near[pl.ds(base, PAD), :] = side_in[1, pl.ds((r + 1) * STEPS, PAD), :]
            else:
                near[pl.ds(base + PAD + LANES, PAD), :] = side_in[0, pl.ds(PAD + r * STEPS, PAD), :]
    for i in range(4, 8):
        dl, dn = WAYS[i]
        guard(-dl, lambda i=i: field_copy(i).wait_recv())
        unsqueeze(layers, *corner_split(), corner_got.at[i - 4], corner_in.at[i - 4])
        for d in range(1, STEPS + 1):
            at, count = spots[d - 1][1:] if d < STEPS else (0, 0)
            r = STEPS + rows + d - 1 if dl < 0 else STEPS - d
            if dn > 0:
                near[pl.ds(r * PITCH, PAD), :] = corner_in[i - 4, pl.ds(at + count, PAD), :]
            else:
                near[pl.ds(r * PITCH + PAD + LANES, PAD), :] = corner_in[i - 4, pl.ds(PAD + at, PAD), :]

    diffuse(rows, near, far, c0, k2)

    def back_row(r, carry):
        done[aligned(r * LANES, LANES), :] = near[aligned((r + STEPS) * PITCH + PAD, LANES), :].T
        return carry

    lax.fori_loop(0, rows, back_row, 0, unroll=2)
    loads[3].wait()
    solve_columns(rows, layers, done, control, coefs.at[1], vert, inc_ref)
    for i, way in enumerate(WAYS):
        guard(way[0], lambda i=i: coef_copy(i).wait_send())
        guard(way[0], lambda i=i: field_copy(i).wait_send())

    passes, padded = off_t.shape[0], off_t.shape[1]
    members = devices // passes
    mine, local = me // members, me % members
    blocks, high = parts.shape[2], value_ref.shape[0]

    def toward(t):
        return lax.rem(mine + t + 1, passes)

    def part_copy(t, i):
        there = lax.rem(local + i, members)
        q = toward(t) * members + there
        return pltpu.make_async_remote_copy(
            src_ref=parts.at[t, there],
            dst_ref=received.at[t, i],
            send_sem=part_send.at[t, i],
            recv_sem=part_recv.at[t, i],
            device_id=(q // n_lon, q % n_lon),
            device_id_type=pl.DeviceIdType.MESH,
        )

    def apart(t, i):
        return jnp.logical_or(t < passes - 1, i > 0)

    def look_up(t, carry):
        lookup(rows, layers, padded // layers, inc_ref, off_t.at[toward(t)], w_t.at[toward(t)], acc)
        for b in range(blocks):
            block = acc[pl.ds(b * LANES, LANES), :].T
            part = block[:members]
            for k in range(1, LANES // members):
                part = part + block[k * members : (k + 1) * members]
            parts[t, :, b, :] = part

        def send(i, carry):
            pl.when(apart(t, i))(lambda: part_copy(t, i).start())
            return carry

        lax.fori_loop(0, members, send, 0)
        return carry

    total[...] = jnp.zeros_like(total)
    lax.fori_loop(0, passes, look_up, 0)
    received[passes - 1, 0] = parts[passes - 1, local]
    loads[6].wait()

    def add_group(turn, carry):
        t, g = turn // (members // GROUP), turn % (members // GROUP)
        result = total[...]
        source = lax.rem(mine + passes - t - 1, passes) * members
        for k in range(GROUP):
            i = g * GROUP + k
            pl.when(apart(t, i))(lambda i=i: part_copy(t, i).wait_recv())
        for k in range(GROUP):
            i = g * GROUP + k
            p = source + lax.rem(local - i + members, members)
            cells = received[t, i]
            v = jnp.concatenate([cells[b : b + 1, :] for b in range(blocks)], axis=1)
            result = result + spread(v, target[pl.ds(p, 1), :], high)
        total[...] = result
        return carry

    lax.fori_loop(0, devices // GROUP, add_group, 0)
    value_ref[...] = total[:high] + total[high:]

    def drain(turn, carry):
        t, i = turn // members, turn % members
        pl.when(apart(t, i))(lambda: part_copy(t, i).wait_send())
        return carry

    lax.fori_loop(0, devices, drain, 0)


def pick(table, row, col):
    level = [jnp.take_along_axis(t, col, axis=1) for t in table]
    bit = 1
    while len(level) > 1:
        odd = (row & bit) != 0
        level = [jnp.where(odd, level[i + 1], level[i]) for i in range(0, len(level), 2)]
        bit *= 2
    return level[0]


def lookup(rows, layers, turns, inc_ref, off_t, w_t, acc):
    def one_group(lg, carry):
        base = pl.multiple_of(lg * SUB, SUB)
        table = [inc_ref[pl.ds(base * rows + r, SUB, stride=rows), :] for r in range(rows)]
        for m in range(turns):
            at = pl.ds(m * layers + base, SUB)
            idx = off_t[at, :]
            acc[at, :] = pick(table, idx >> 7, idx & (LANES - 1)) * w_t[at, :]
        return carry

    lax.fori_loop(0, layers // SUB, one_group, 0, unroll=2)


def floats(*shape):
    return jax.ShapeDtypeStruct(shape, jnp.float32)


def spread(v, t, high):
    shape, bf = (high, v.shape[1]), jnp.bfloat16
    flat = (LANES, v.shape[1])
    upper = lax.broadcasted_iota(jnp.int32, shape, 0).astype(bf)
    lower = lax.broadcasted_iota(jnp.int32, flat, 0).astype(bf)
    hit = upper == jnp.broadcast_to((t >> 7).astype(jnp.float32), shape).astype(bf)
    one = lower == jnp.broadcast_to((t & (LANES - 1)).astype(jnp.float32), flat).astype(bf)
    first = v.astype(bf).astype(jnp.float32)
    left = jnp.concatenate(
        [
            jnp.where(hit, jnp.broadcast_to(part, shape).astype(bf), jnp.zeros(shape, bf))
            for part in (first, v - first)
        ],
        axis=0,
    )
    right = jnp.where(one, jnp.ones(flat, bf), jnp.zeros(flat, bf))
    return lax.dot_general(
        left, right, (((1,), (1,)), ((), ())), preferred_element_type=jnp.float32
    )


def per_device(
    control,
    kappa,
    sea_mask,
    vert_coef,
    stencil_offsets,
    stencil_weights,
    slot_target,
    observed,
    inv_error,
):
    levels, fields, rows, cols = control.shape
    layers = levels * fields
    tall = rows + 2 * STEPS
    sten, owners, cap = stencil_offsets.shape
    bundles = sten * owners // LANES
    padded = -(-cap // layers) * layers
    corner = corner_spots()[1] + 2 * PAD
    high = observed.shape[0] // LANES
    blocks = cap // LANES
    members = owners // bundles

    def vmem(*shape, dtype=jnp.float32):
        return pltpu.VMEM(shape, dtype)

    wide = (tall * PITCH, LANES)
    dma = pltpu.SemaphoreType.DMA
    increment, value = pl.pallas_call(
        functools.partial(step_kernel, lax.axis_size("lat"), lax.axis_size("lon"), rows, layers),
        out_shape=(floats(layers * rows, LANES), floats(high, LANES)),
        in_specs=[pl.BlockSpec(memory_space=pltpu.HBM)] * 7,
        out_specs=(pl.BlockSpec(memory_space=pltpu.VMEM), pl.BlockSpec(memory_space=pltpu.VMEM)),
        scratch_shapes=[
            vmem(layers * rows, LANES),
            vmem(rows, LANES),
            vmem(rows, LANES, dtype=jnp.int32),
            vmem(levels * rows, LANES),
            vmem(sten * owners, cap, dtype=jnp.int32),
            vmem(sten * owners, cap),
            vmem(owners, cap, dtype=jnp.int32),
            vmem(bundles, padded, LANES, dtype=jnp.int32),
            vmem(bundles, padded, LANES),
            vmem(padded, LANES),
            vmem(bundles, members, blocks, LANES),
            vmem(bundles, members, blocks, LANES),
            vmem(2 * high, LANES),
            vmem(3, 3 * rows, LANES),
            vmem(2, 3, 40, LANES),
            vmem(rows * layers, LANES),
            vmem(2, STEPS * layers, LANES),
            vmem(2, rows * STEPS + 2 * PAD, LANES),
            vmem(2, rows * STEPS + 2 * PAD, LANES),
            vmem(4, corner, LANES),
            vmem(4, corner, LANES),
            vmem(2, message(*side_split(rows)), LANES),
            vmem(2, message(*side_split(rows)), LANES),
            vmem(4, message(*corner_split()), LANES),
            vmem(4, message(*corner_split()), LANES),
            vmem(*wide),
            vmem(*wide),
            vmem(*wide),
            vmem(*wide),
            vmem(rows * LANES, LANES),
            dma((7,)),
            dma((len(WAYS),)),
            dma((len(WAYS),)),
            dma((len(WAYS),)),
            dma((len(WAYS),)),
            dma((bundles, members)),
            dma((bundles, members)),
        ],
        compiler_params=pltpu.CompilerParams(
            vmem_limit_bytes=52 * 1024 * 1024, collective_id=2, has_side_effects=True
        ),
        name="assimilate",
    )(
        *[
            pltpu.with_memory_space_constraint(a, pltpu.HBM)
            for a in (
                control.reshape(layers * rows, cols),
                kappa,
                sea_mask,
                vert_coef.reshape(levels * rows, cols),
                stencil_offsets.reshape(sten * owners, cap),
                stencil_weights.reshape(sten * owners, cap),
                slot_target,
            )
        ]
    )
    return increment.reshape(control.shape), (value.reshape(-1) - observed) * inv_error


def solution(mesh):
    return jax.shard_map(
        per_device,
        mesh=mesh,
        in_specs=(
            P(None, None, "lat", "lon"),
            P("lat", "lon"),
            P("lat", "lon"),
            P(None, "lat", "lon"),
            P(None, ("lat", "lon"), None),
            P(None, ("lat", "lon"), None),
            P(("lat", "lon"), None),
            P(("lat", "lon")),
            P(("lat", "lon")),
        ),
        out_specs=(P(None, None, "lat", "lon"), P(("lat", "lon"))),
        check_vma=False,
    )
```

```python
import functools

import jax
import jax.numpy as jnp
from jax import lax
from jax.experimental import pallas as pl
from jax.experimental.pallas import tpu as pltpu
from jax.sharding import PartitionSpec as P

STEPS = 10
LANES = 128
SUB = 8


GROUP = 8
WAYS = ((-1, 0), (1, 0), (0, -1), (0, 1), (-1, -1), (-1, 1), (1, -1), (1, 1))
PAD = 16
PITCH = LANES + 2 * PAD


def aligned(start, size):
    return pl.ds(pl.multiple_of(start, SUB), size)


def corner_spots():
    spots, at = [], 0
    for d in range(1, STEPS):
        spots.append((d, at, STEPS - d))
        at += STEPS - d
    return spots, -(-at // SUB) * SUB


def corner_split():
    count = STEPS * (STEPS - 1) // 2
    return count - count // 3, count // 3


def side_split(rows):
    return (rows - rows // 3) * STEPS, rows // 3 * STEPS


def message(kept, few):
    return max(-(-kept // SUB), -(-few // SUB) + -(-few // SUB)) * SUB


def update(old, new, c0, k2, count, first, low, high, per):
    def some_rows(turn, carry):
        base = (first + per * turn) * PITCH
        for v in range(low, high):
            spot = [aligned(base + d * PITCH + v * SUB, SUB) for d in range(-1, per + 1)]
            cells = [old[s, :] for s in spot]
            for d in range(per):
                at = base + d * PITCH + v * SUB
                side = old[pl.ds(at - 1, SUB), :] + old[pl.ds(at + 1, SUB), :]
                around = (cells[d] + cells[d + 2]) + side
                new[spot[d + 1], :] = c0[spot[d + 1], :] * cells[d + 1] + k2[spot[d + 1], :] * around
        return carry

    lax.fori_loop(0, count, some_rows, 0)


def span(old, new, c0, k2, first, count, low, high):
    per = 5 if count % 5 == 0 else 4
    update(old, new, c0, k2, count // per, first, low, high, per)
    if count % per:
        update(old, new, c0, k2, 1, first + count // per * per, low, high, count % per)


def diffuse_inner(rows, old, new, c0, k2):
    width = PITCH // SUB
    span(old, new, c0, k2, STEPS + 1, rows - 2, 0, width)
    span(new, old, c0, k2, STEPS + 2, rows - 4, 1, width - 1)


def diffuse_rest(rows, old, new, c0, k2):
    tall = rows + 2 * STEPS
    width = PITCH // SUB
    for first in (1, STEPS + rows - 1):
        span(old, new, c0, k2, first, STEPS, 0, width)
    for first in (2, STEPS + rows - 2):
        span(new, old, c0, k2, first, STEPS, 1, width - 1)

    def two_steps(s, carry):
        first = 2 * s + 1
        update(old, new, c0, k2, (tall - 2 * first + 2) // 4, first, 1, width - 1, 4)
        update(new, old, c0, k2, (tall - 2 * first) // 4, first + 1, 1, width - 1, 4)
        return carry

    lax.fori_loop(1, STEPS // 2, two_steps, 0)


def factor(rows, vert, inverse, ratio):
    levels = vert.shape[0] // rows
    above = vert[pl.ds(0, rows), :]
    cprev = jnp.zeros((rows, LANES), jnp.float32)
    for k in range(levels):
        if k + 1 < levels:
            below = vert[pl.ds((k + 1) * rows, rows), :]
        else:
            below = jnp.zeros((rows, LANES), jnp.float32)
        inv = 1.0 / (((1.0 + above) + below) + above * cprev)
        cprev = -below * inv
        inverse[pl.ds(k * rows, rows), :] = inv
        ratio[pl.ds(k * rows, rows), :] = cprev
        above = below


def solve_columns(rows, layers, done, control, coef, vert, inverse, ratio, inc_ref):
    levels = vert.shape[0] // rows
    fields = layers // levels
    for h in range(rows // SUB):
        here = coef[pl.ds(rows + h * SUB, SUB), :]
        sea = here != 0.0
        back = 1.0 / jnp.where(sea, here, 1.0)
        prev = [jnp.zeros((SUB, LANES), jnp.float32)] * fields
        for k in range(levels):
            level = pl.ds(k * rows + h * SUB, SUB)
            above, inv = vert[level, :], inverse[level, :]
            for f in range(fields):
                layer = k * fields + f
                at = pl.ds(layer * rows + h * SUB, SUB)
                right = done[pl.ds(h * SUB * LANES + layer, SUB, stride=LANES), :] * back
                right = jnp.where(sea, right, control[at, :])
                prev[f] = (right + above * prev[f]) * inv
                inc_ref[at, :] = prev[f]
        for k in range(levels - 2, -1, -1):
            fall = ratio[pl.ds(k * rows + h * SUB, SUB), :]
            for f in range(fields):
                at = pl.ds((k * fields + f) * rows + h * SUB, SUB)
                prev[f] = inc_ref[at, :] - fall * prev[f]
                inc_ref[at, :] = prev[f]


def weigh(rows, coefs, held):
    lane = lax.broadcasted_iota(jnp.int32, (40, LANES), 1)
    mid = pl.ds(rows - STEPS + 1, 40)
    up = pl.ds(rows - STEPS, 40)
    down = pl.ds(rows - STEPS + 2, 40)
    here = [coefs[k, mid, :] for k in range(3)]
    right = [pltpu.roll(c, 1, 1) for c in here]
    left = [pltpu.roll(c, LANES - 1, 1) for c in here]
    first, last = lane == 0, lane == LANES - 1
    wests = [right[0], jnp.where(first, right[0], right[1]), jnp.where(first, right[1], right[2])]
    easts = [jnp.where(last, left[1], left[0]), jnp.where(last, left[2], left[1]), left[2]]
    for k in range(3):
        around = (coefs[k, up, :] + coefs[k, down, :]) + (wests[k] + easts[k])
        held[0, k, :, :] = 1.0 - here[k] * around
        held[1, k, :, :] = here[k] * here[k]


def broaden(rows, held, kind, out):
    lane = lax.broadcasted_iota(jnp.int32, (40, LANES), 1)
    rest = jnp.zeros((LANES - 40, LANES), jnp.float32)
    main = jnp.concatenate([held[kind, 1, :, :], rest], axis=0).T
    outer = jnp.where(lane >= LANES - PAD, held[kind, 0, :, :], held[kind, 2, :, :])
    outer = jnp.concatenate([outer, rest], axis=0).T
    for j in range(rows + 2 * STEPS - 2):
        base = (j + 1) * PITCH
        column = outer[:, j : j + 1]
        out[pl.ds(base, PAD), :] = jnp.broadcast_to(column[LANES - PAD :], (PAD, LANES))
        out[pl.ds(base + PAD, LANES), :] = jnp.broadcast_to(main[:, j : j + 1], (LANES, LANES))
        out[pl.ds(base + PAD + LANES, PAD), :] = jnp.broadcast_to(column[:PAD], (PAD, LANES))


def turn(n_lat, n_lon, off, weight, off_t, w_t):
    blocks, height, _ = off.shape
    cap, padded = blocks * LANES, off_t.shape[1]
    width = n_lon // off_t.shape[0]
    ways = SUB // width
    row = lax.broadcasted_iota(jnp.int32, (SUB, LANES), 0) // width

    def gather(src, c, g):
        tiles = []
        for start in range(0, height, n_lon * ways):
            tile = src[c, pl.ds(start + g * width, SUB), :]
            for k in range(1, ways):
                piece = src[c, pl.ds(start + k * n_lon + g * width - k * width, SUB), :]
                tile = jnp.where(row == k, piece, tile)
            tiles.append(tile)
        return jnp.concatenate(tiles, axis=0).T

    for g in range(off_t.shape[0]):
        if padded > cap:
            off_t[g, cap:padded, :] = jnp.zeros((padded - cap, LANES), jnp.int32)
            w_t[g, cap:padded, :] = jnp.zeros((padded - cap, LANES), jnp.float32)
        for c in range(blocks):
            off_t[g, pl.ds(c * LANES, LANES), :] = gather(off, c, g)
            w_t[g, pl.ds(c * LANES, LANES), :] = gather(weight, c, g)


def squeeze(layers, kept, few, src, dst):
    spare = LANES - layers
    size = -(-few // SUB) * SUB
    whole = dst.shape[0]
    lane = lax.broadcasted_iota(jnp.int32, (size, LANES), 1)
    dst[...] = src[pl.ds(0, whole), :]
    rest = src[pl.ds(kept, size), :]
    dst[pl.ds(0, size), :] = jnp.where(lane < layers, src[pl.ds(0, size), :], rest)
    moved = pltpu.roll(rest, layers - spare, 1)
    dst[pl.ds(few, size), :] = jnp.where(lane < layers, src[pl.ds(few, size), :], moved)


def unsqueeze(layers, kept, few, src, dst):
    spare = LANES - layers
    size = -(-few // SUB) * SUB
    lane = lax.broadcasted_iota(jnp.int32, (size, LANES), 1)
    dst[pl.ds(PAD, src.shape[0]), :] = src[...]
    first = pltpu.roll(src[pl.ds(0, size), :], spare, 1)
    second = pltpu.roll(src[pl.ds(few, size), :], LANES - layers + spare, 1)
    dst[pl.ds(PAD + kept, size), :] = jnp.where(lane < spare, first, second)


def field_kernel(
    n_lat,
    n_lon,
    rows,
    layers,
    control_ref,
    kappa_ref,
    mask_ref,
    vert_ref,
    off_ref,
    w_ref,
    inc_ref,
    off_t,
    w_t,
    control,
    kappa,
    mask,
    vert,
    off,
    weight,
    inverse,
    ratio,
    coefs,
    held,
    laid,
    far_rows,
    side_out,
    side_in,
    corner_out,
    corner_in,
    side_sent,
    side_got,
    corner_sent,
    corner_got,
    near,
    far,
    c0,
    k2,
    done,
    load_sem,
    coef_send,
    coef_recv,
    send_sem,
    recv_sem,
):
    lat, lon = lax.axis_index("lat"), lax.axis_index("lon")
    tall = rows + 2 * STEPS
    pairs = ((control_ref, control), (kappa_ref, kappa), (mask_ref, mask))
    pairs += ((vert_ref, vert),)
    for c in range(off.shape[0]):
        here = pl.ds(c * LANES, LANES)
        pairs += ((off_ref.at[:, here], off.at[c]), (w_ref.at[:, here], weight.at[c]))
    loads = [pltpu.make_async_copy(a, b, load_sem.at[i]) for i, (a, b) in enumerate(pairs)]
    for i in (1, 2, 0, *range(3, len(loads))):
        loads[i].start()

    def place(i):
        return (lat + WAYS[i][0], lax.rem(lon + WAYS[i][1] + n_lon, n_lon))

    def guard(step, body):
        if step == 0:
            body()
        else:
            pl.when(lat > 0 if step < 0 else lat < n_lat - 1)(body)

    corner_got[...] = jnp.zeros_like(corner_got)
    barrier = pltpu.get_barrier_semaphore()
    for i, way in enumerate(WAYS):
        guard(
            way[0],
            lambda i=i: pl.semaphore_signal(
                barrier, inc=1, device_id=place(i), device_id_type=pl.DeviceIdType.MESH
            ),
        )

    side_in[...] = jnp.zeros_like(side_in)
    corner_in[...] = jnp.zeros_like(corner_in)

    @pl.when(lat == 0)
    def _():
        coefs[:, :rows, :] = jnp.zeros((3, rows, LANES), jnp.float32)
        far_rows[1] = jnp.zeros((STEPS * layers, LANES), jnp.float32)

    @pl.when(lat == n_lat - 1)
    def _():
        coefs[:, 2 * rows :, :] = jnp.zeros((3, rows, LANES), jnp.float32)
        far_rows[0] = jnp.zeros((STEPS * layers, LANES), jnp.float32)

    def remote(i, src, dst, out_sem, in_sem):
        return pltpu.make_async_remote_copy(
            src_ref=src,
            dst_ref=dst,
            send_sem=out_sem.at[i],
            recv_sem=in_sem.at[i],
            device_id=place(i),
            device_id_type=pl.DeviceIdType.MESH,
        )

    def coef_copy(i):
        dl, dn = WAYS[i]
        return remote(
            i, coefs.at[1, pl.ds(rows, rows)], coefs.at[1 - dn, pl.ds((1 - dl) * rows, rows)], coef_send, coef_recv
        )

    spots = corner_spots()[0]

    def field_copy(i):
        dl, dn = WAYS[i]
        if dn == 0:
            start = 0 if dl < 0 else (rows - STEPS) * layers
            src = laid.at[pl.ds(start, STEPS * layers)]
            dst = far_rows.at[i]
        elif dl == 0:
            src, dst = side_sent.at[i - 2], side_got.at[i - 2]
        else:
            src, dst = corner_sent.at[i - 4], corner_got.at[i - 4]
        return remote(i, src, dst, send_sem, recv_sem)

    loads[1].wait()
    loads[2].wait()
    coefs[1, pl.ds(rows, rows), :] = kappa[...] * mask[...].astype(jnp.float32)
    loads[0].wait()
    for r in range(rows):
        here = coefs[1, pl.ds(rows + r, 1), :]
        for g in range(layers // SUB):
            laid[pl.ds(r * layers + g * SUB, SUB), :] = (
                control[pl.ds(g * SUB * rows + r, SUB, stride=rows), :] * here
            )
    def upright(block):
        return jnp.concatenate([block, block[: LANES - layers]], axis=0).T

    def main_row(r, carry):
        block = laid[aligned(r * layers, layers), :]
        near[aligned((r + STEPS) * PITCH + PAD, LANES), :] = upright(block)
        return carry

    lax.fori_loop(0, rows, main_row, 0, unroll=2)
    for k, first in ((0, PAD), (1, PAD + LANES - STEPS)):
        for r in range(rows):
            side_out[k, pl.ds(r * STEPS, PAD), :] = near[
                pl.ds((r + STEPS) * PITCH + first, PAD), :
            ]
        squeeze(layers, *side_split(rows), side_out.at[k], side_sent.at[k])
    for i in range(4, 8):
        dl, dn = WAYS[i]
        for d, at, count in spots:
            r = d - 1 if dl < 0 else rows - d
            first = PAD if dn < 0 else PAD + LANES - count
            corner_out[i - 4, pl.ds(at, PAD), :] = near[pl.ds((r + STEPS) * PITCH + first, PAD), :]
        squeeze(layers, *corner_split(), corner_out.at[i - 4], corner_sent.at[i - 4])
    beside = (lat > 0).astype(jnp.int32) + (lat < n_lat - 1).astype(jnp.int32)
    pl.semaphore_wait(barrier, 2 + 3 * beside)
    for i, way in enumerate(WAYS):
        guard(way[0], lambda i=i: coef_copy(i).start())
    for i in (2, 3, 0, 1, 4, 5, 6, 7):
        guard(WAYS[i][0], lambda i=i: field_copy(i).start())

    for i, way in enumerate(WAYS):
        guard(-way[0], lambda i=i: coef_copy(i).wait_recv())
    weigh(rows, coefs, held)
    broaden(rows, held, 0, c0)
    broaden(rows, held, 1, k2)
    for i in range(3, len(loads)):
        loads[i].wait()
    turn(n_lat, n_lon, off, weight, off_t, w_t)
    factor(rows, vert, inverse, ratio)

    for i in (2, 3):
        field_copy(i).wait_recv()
        unsqueeze(layers, *side_split(rows), side_got.at[i - 2], side_in.at[i - 2])
        for r in range(rows):
            base = (r + STEPS) * PITCH
            if i == 3:
                near[pl.ds(base, PAD), :] = side_in[1, pl.ds((r + 1) * STEPS, PAD), :]
            else:
                near[pl.ds(base + PAD + LANES, PAD), :] = side_in[0, pl.ds(PAD + r * STEPS, PAD), :]
    for i in range(4, 8):
        dl, dn = WAYS[i]
        guard(-dl, lambda i=i: field_copy(i).wait_recv())
        unsqueeze(layers, *corner_split(), corner_got.at[i - 4], corner_in.at[i - 4])
        for d in range(1, STEPS + 1):
            at, count = spots[d - 1][1:] if d < STEPS else (0, 0)
            r = STEPS + rows + d - 1 if dl < 0 else STEPS - d
            if dn > 0:
                near[pl.ds(r * PITCH, PAD), :] = corner_in[i - 4, pl.ds(at + count, PAD), :]
            else:
                near[pl.ds(r * PITCH + PAD + LANES, PAD), :] = corner_in[i - 4, pl.ds(PAD + at, PAD), :]

    diffuse_inner(rows, near, far, c0, k2)
    for i in (0, 1):
        guard(-WAYS[i][0], lambda i=i: field_copy(i).wait_recv())
        start = (STEPS + rows) if i == 0 else 0

        def far_row(r, carry, i=i, start=start):
            block = far_rows[i, aligned(r * layers, layers), :]
            near[aligned((r + start) * PITCH + PAD, LANES), :] = upright(block)
            return carry

        lax.fori_loop(0, STEPS, far_row, 0, unroll=2)
    diffuse_rest(rows, near, far, c0, k2)

    def back_row(r, carry):
        done[aligned(r * LANES, LANES), :] = near[aligned((r + STEPS) * PITCH + PAD, LANES), :].T
        return carry

    lax.fori_loop(0, rows, back_row, 0, unroll=2)
    solve_columns(rows, layers, done, control, coefs.at[1], vert, inverse, ratio, inc_ref)
    for i, way in enumerate(WAYS):
        guard(way[0], lambda i=i: coef_copy(i).wait_send())
        guard(way[0], lambda i=i: field_copy(i).wait_send())


def pick(table, row, col):
    level = [jnp.take_along_axis(t, col, axis=1) for t in table]
    bit = 1
    while len(level) > 1:
        odd = (row & bit) != 0
        level = [jnp.where(odd, level[i + 1], level[i]) for i in range(0, len(level), 2)]
        bit *= 2
    return level[0]


def lookup(rows, layers, turns, inc_ref, off_t, w_t, acc):
    def one_group(lg, carry):
        base = pl.multiple_of(lg * SUB, SUB)
        table = [inc_ref[pl.ds(base * rows + r, SUB, stride=rows), :] for r in range(rows)]
        for m in range(turns):
            at = pl.ds(m * layers + base, SUB)
            idx = off_t[at, :]
            acc[at, :] = pick(table, idx >> 7, idx & (LANES - 1)) * w_t[at, :]
        return carry

    lax.fori_loop(0, layers // SUB, one_group, 0, unroll=5)


def observe_kernel(
    n_lat,
    n_lon,
    rows,
    layers,
    inc_ref,
    off_t,
    w_t,
    target_ref,
    value_ref,
    target,
    acc,
    parts,
    received,
    total,
    load_sem,
    part_send,
    part_recv,
):
    lat, lon = lax.axis_index("lat"), lax.axis_index("lon")
    me, devices = lat * n_lon + lon, n_lat * n_lon
    passes, padded = off_t.shape[0], off_t.shape[1]
    members, width = devices // passes, n_lon // passes
    mine, local = lon // width, lat * width + lon % width
    blocks, high = parts.shape[1], value_ref.shape[0]
    load = pltpu.make_async_copy(target_ref, target, load_sem.at[0])
    load.start()
    barrier = pltpu.get_barrier_semaphore()

    def greet(k, carry):
        q = lax.rem(me + k, devices)
        pl.semaphore_signal(
            barrier, inc=1, device_id=(q // n_lon, q % n_lon), device_id_type=pl.DeviceIdType.MESH
        )
        return carry

    lax.fori_loop(1, devices, greet, 0)

    def toward(t):
        return lax.rem(mine + t + 1, passes)

    def slots(t, i, count=1):
        return pl.ds(t * members + i, count)

    def copy(src, dst, in_sem, there):
        return pltpu.make_async_remote_copy(
            src_ref=src,
            dst_ref=dst,
            send_sem=part_send.at[0],
            recv_sem=in_sem,
            device_id=there,
            device_id_type=pl.DeviceIdType.MESH,
        )

    def part_copy(t, i):
        there = lax.rem(local + i, members)
        place = (there // width, toward(t) * width + there % width)
        src, dst = parts.at[slots(t, there)], received.at[slots(t, i)]
        return copy(src, dst, part_recv.at[t, i // GROUP], place)

    def wait_group(t, g, first, count):
        here = slots(t, g * GROUP + first, count)
        copy(parts.at[here], received.at[here], part_recv.at[t, g], (lat, lon)).wait_recv()

    def look_up(t, carry):
        lookup(rows, layers, padded // layers, inc_ref, off_t.at[toward(t)], w_t.at[toward(t)], acc)
        for b in range(blocks):
            block = acc[pl.ds(b * LANES, LANES), :].T
            part = block[:members]
            for k in range(1, LANES // members):
                part = part + block[k * members : (k + 1) * members]
            parts[slots(t, 0, members), b, :] = part

        @pl.when(t == 0)
        def _():
            pl.semaphore_wait(barrier, devices - 1)

        def send(i, carry):
            part_copy(t, i).start()
            return carry

        lax.fori_loop((t == passes - 1).astype(jnp.int32), members, send, 0)
        return carry

    total[...] = jnp.zeros_like(total)
    lax.fori_loop(0, passes, look_up, 0)
    received[slots(passes - 1, 0)] = parts[slots(passes - 1, local)]
    load.wait()

    def add_group(turn, carry):
        t, g = turn // (members // GROUP), turn % (members // GROUP)
        result = total[...]
        source = lax.rem(mine + passes - t - 1, passes) * width
        own = jnp.logical_and(t == passes - 1, g == 0)
        pl.when(own)(lambda: wait_group(t, g, 1, GROUP - 1))
        pl.when(jnp.logical_not(own))(lambda: wait_group(t, g, 0, GROUP))
        for k in range(GROUP):
            i = g * GROUP + k
            p = lax.rem(local - i + members, members)
            p = p // width * n_lon + source + p % width
            cells = received[t * members + i]
            v = jnp.concatenate([cells[b : b + 1, :] for b in range(blocks)], axis=1)
            result = result + spread(v, target[pl.ds(p, 1), :], high)
        total[...] = result
        return carry

    lax.fori_loop(0, devices // GROUP, add_group, 0)
    value_ref[...] = total[:high] + total[high:]
    sent = pl.ds(0, devices - 1)
    copy(parts.at[sent], received.at[sent], part_recv.at[0, 0], (lat, lon)).wait_send()


def floats(*shape):
    return jax.ShapeDtypeStruct(shape, jnp.float32)


def spread(v, t, high):
    shape, bf = (high, v.shape[1]), jnp.bfloat16
    flat = (LANES, v.shape[1])
    upper = lax.broadcasted_iota(jnp.int32, shape, 0).astype(bf)
    lower = lax.broadcasted_iota(jnp.int32, flat, 0).astype(bf)
    hit = upper == jnp.broadcast_to((t >> 7).astype(jnp.float32), shape).astype(bf)
    one = lower == jnp.broadcast_to((t & (LANES - 1)).astype(jnp.float32), flat).astype(bf)
    first = v.astype(bf).astype(jnp.float32)
    left = jnp.concatenate(
        [
            jnp.where(hit, jnp.broadcast_to(part, shape).astype(bf), jnp.zeros(shape, bf))
            for part in (first, v - first)
        ],
        axis=0,
    )
    right = jnp.where(one, jnp.ones(flat, bf), jnp.zeros(flat, bf))
    return lax.dot_general(
        left, right, (((1,), (1,)), ((), ())), preferred_element_type=jnp.float32
    )


def per_device(
    control,
    kappa,
    sea_mask,
    vert_coef,
    stencil_offsets,
    stencil_weights,
    slot_target,
    observed,
    inv_error,
):
    levels, fields, rows, cols = control.shape
    layers = levels * fields
    tall = rows + 2 * STEPS
    sten, owners, cap = stencil_offsets.shape
    bundles = sten * owners // LANES
    padded = -(-cap // layers) * layers
    corner = corner_spots()[1] + 2 * PAD
    high = observed.shape[0] // LANES
    blocks = cap // LANES
    members = owners // bundles

    def vmem(*shape, dtype=jnp.float32):
        return pltpu.VMEM(shape, dtype)

    wide = (tall * PITCH, LANES)
    dma = pltpu.SemaphoreType.DMA
    place = (lax.axis_size("lat"), lax.axis_size("lon"))
    shapes = (
        floats(layers * rows, LANES),
        jax.ShapeDtypeStruct((bundles, padded, LANES), jnp.int32),
        floats(bundles, padded, LANES),
    )
    arrays = (
        control.reshape(layers * rows, cols),
        kappa,
        sea_mask,
        vert_coef.reshape(levels * rows, cols),
        stencil_offsets.reshape(sten * owners, cap),
        stencil_weights.reshape(sten * owners, cap),
    )
    increment, off_t, w_t = pl.pallas_call(
        functools.partial(field_kernel, *place, rows, layers),
        out_shape=shapes,
        in_specs=[pl.BlockSpec(memory_space=pltpu.HBM)] * len(arrays),
        out_specs=tuple(pl.BlockSpec(memory_space=pltpu.VMEM) for _ in shapes),
        scratch_shapes=[
            vmem(layers * rows, LANES),
            vmem(rows, LANES),
            vmem(rows, LANES, dtype=jnp.int32),
            vmem(levels * rows, LANES),
            vmem(blocks, sten * owners, LANES, dtype=jnp.int32),
            vmem(blocks, sten * owners, LANES),
            vmem(levels * rows, LANES),
            vmem(levels * rows, LANES),
            vmem(3, 3 * rows, LANES),
            vmem(2, 3, 40, LANES),
            vmem(rows * layers, LANES),
            vmem(2, STEPS * layers, LANES),
            vmem(2, rows * STEPS + 2 * PAD, LANES),
            vmem(2, rows * STEPS + 2 * PAD, LANES),
            vmem(4, corner, LANES),
            vmem(4, corner, LANES),
            vmem(2, message(*side_split(rows)), LANES),
            vmem(2, message(*side_split(rows)), LANES),
            vmem(4, message(*corner_split()), LANES),
            vmem(4, message(*corner_split()), LANES),
            vmem(*wide),
            vmem(*wide),
            vmem(*wide),
            vmem(*wide),
            vmem(rows * LANES, LANES),
            dma((4 + 2 * blocks,)),
            dma((len(WAYS),)),
            dma((len(WAYS),)),
            dma((len(WAYS),)),
            dma((len(WAYS),)),
        ],
        compiler_params=pltpu.CompilerParams(
            vmem_limit_bytes=44 * 1024 * 1024, collective_id=2, has_side_effects=True
        ),
        name="field",
    )(*[pltpu.with_memory_space_constraint(a, pltpu.HBM) for a in arrays])
    vm = pl.BlockSpec(memory_space=pltpu.VMEM)
    value = pl.pallas_call(
        functools.partial(observe_kernel, *place, rows, layers),
        out_shape=floats(high, LANES),
        in_specs=[vm, vm, vm, pl.BlockSpec(memory_space=pltpu.HBM)],
        out_specs=vm,
        scratch_shapes=[
            vmem(owners, cap, dtype=jnp.int32),
            vmem(padded, LANES),
            vmem(owners, blocks, LANES),
            vmem(owners, blocks, LANES),
            vmem(2 * high, LANES),
            dma((1,)),
            dma((1,)),
            dma((bundles, members // GROUP)),
        ],
        compiler_params=pltpu.CompilerParams(
            vmem_limit_bytes=24 * 1024 * 1024, collective_id=3, has_side_effects=True
        ),
        name="observe",
    )(increment, off_t, w_t, pltpu.with_memory_space_constraint(slot_target, pltpu.HBM))
    return increment.reshape(control.shape), (value.reshape(-1) - observed) * inv_error


def solution(mesh):
    return jax.shard_map(
        per_device,
        mesh=mesh,
        in_specs=(
            P(None, None, "lat", "lon"),
            P("lat", "lon"),
            P("lat", "lon"),
            P(None, "lat", "lon"),
            P(None, ("lat", "lon"), None),
            P(None, ("lat", "lon"), None),
            P(("lat", "lon"), None),
            P(("lat", "lon")),
            P(("lat", "lon")),
        ),
        out_specs=(P(None, None, "lat", "lon"), P(("lat", "lon"))),
        check_vma=False,
    )
```

```python
import functools

import jax
import jax.numpy as jnp
from jax import lax
from jax.experimental import pallas as pl
from jax.experimental.pallas import tpu as pltpu
from jax.sharding import PartitionSpec as P

STEPS = 10
LANES = 128
SUB = 8


GROUP = 8
WAYS = ((-1, 0), (1, 0), (0, -1), (0, 1), (-1, -1), (-1, 1), (1, -1), (1, 1))
PAD = 16
PITCH = LANES + 2 * PAD


def aligned(start, size):
    return pl.ds(pl.multiple_of(start, SUB), size)


def corner_spots():
    spots, at = [], 0
    for d in range(1, STEPS):
        spots.append((d, at, STEPS - d))
        at += STEPS - d
    return spots, -(-at // SUB) * SUB


def corner_split():
    count = STEPS * (STEPS - 1) // 2
    return count - count // 3, count // 3


def side_split(rows):
    return (rows - rows // 3) * STEPS, rows // 3 * STEPS


def message(kept, few):
    return max(-(-kept // SUB), -(-few // SUB) + -(-few // SUB)) * SUB


def update(old, new, c0, k2, count, first, low, high, per):
    def some_rows(turn, carry):
        base = (first + per * turn) * PITCH
        for v in range(low, high):
            spot = [aligned(base + d * PITCH + v * SUB, SUB) for d in range(-1, per + 1)]
            cells = [old[s, :] for s in spot]
            for d in range(per):
                at = base + d * PITCH + v * SUB
                side = old[pl.ds(at - 1, SUB), :] + old[pl.ds(at + 1, SUB), :]
                around = (cells[d] + cells[d + 2]) + side
                new[spot[d + 1], :] = c0[spot[d + 1], :] * cells[d + 1] + k2[spot[d + 1], :] * around
        return carry

    lax.fori_loop(0, count, some_rows, 0)


def span(old, new, c0, k2, first, count, low, high):
    per = 5 if count % 5 == 0 else 4
    update(old, new, c0, k2, count // per, first, low, high, per)
    if count % per:
        update(old, new, c0, k2, 1, first + count // per * per, low, high, count % per)


def diffuse_inner(rows, old, new, c0, k2):
    width = PITCH // SUB
    span(old, new, c0, k2, STEPS + 1, rows - 2, 0, width)
    span(new, old, c0, k2, STEPS + 2, rows - 4, 1, width - 1)


def diffuse_rest(rows, old, new, c0, k2):
    tall = rows + 2 * STEPS
    width = PITCH // SUB
    for first in (1, STEPS + rows - 1):
        span(old, new, c0, k2, first, STEPS, 0, width)
    for first in (2, STEPS + rows - 2):
        span(new, old, c0, k2, first, STEPS, 1, width - 1)

    def two_steps(s, carry):
        first = 2 * s + 1
        update(old, new, c0, k2, (tall - 2 * first + 2) // 4, first, 1, width - 1, 4)
        update(new, old, c0, k2, (tall - 2 * first) // 4, first + 1, 1, width - 1, 4)
        return carry

    lax.fori_loop(1, STEPS // 2, two_steps, 0)


def factor(rows, vert, inverse, ratio):
    levels = vert.shape[0] // rows
    above = vert[pl.ds(0, rows), :]
    cprev = jnp.zeros((rows, LANES), jnp.float32)
    for k in range(levels):
        if k + 1 < levels:
            below = vert[pl.ds((k + 1) * rows, rows), :]
        else:
            below = jnp.zeros((rows, LANES), jnp.float32)
        inv = 1.0 / (((1.0 + above) + below) + above * cprev)
        cprev = -below * inv
        inverse[pl.ds(k * rows, rows), :] = inv
        ratio[pl.ds(k * rows, rows), :] = cprev
        above = below


def solve_columns(rows, layers, done, control, coef, vert, inverse, ratio, inc_ref):
    levels = vert.shape[0] // rows
    fields = layers // levels
    for h in range(rows // SUB):
        here = coef[pl.ds(rows + h * SUB, SUB), :]
        sea = here != 0.0
        back = 1.0 / jnp.where(sea, here, 1.0)
        prev = [jnp.zeros((SUB, LANES), jnp.float32)] * fields
        for k in range(levels):
            level = pl.ds(k * rows + h * SUB, SUB)
            above, inv = vert[level, :], inverse[level, :]
            for f in range(fields):
                layer = k * fields + f
                at = pl.ds(layer * rows + h * SUB, SUB)
                right = done[pl.ds(h * SUB * LANES + layer, SUB, stride=LANES), :] * back
                right = jnp.where(sea, right, control[at, :])
                prev[f] = (right + above * prev[f]) * inv
                inc_ref[at, :] = prev[f]
        for k in range(levels - 2, -1, -1):
            fall = ratio[pl.ds(k * rows + h * SUB, SUB), :]
            for f in range(fields):
                at = pl.ds((k * fields + f) * rows + h * SUB, SUB)
                prev[f] = inc_ref[at, :] - fall * prev[f]
                inc_ref[at, :] = prev[f]


def weigh(rows, coefs, held):
    lane = lax.broadcasted_iota(jnp.int32, (40, LANES), 1)
    mid = pl.ds(rows - STEPS + 1, 40)
    up = pl.ds(rows - STEPS, 40)
    down = pl.ds(rows - STEPS + 2, 40)
    here = [coefs[k, mid, :] for k in range(3)]
    right = [pltpu.roll(c, 1, 1) for c in here]
    left = [pltpu.roll(c, LANES - 1, 1) for c in here]
    first, last = lane == 0, lane == LANES - 1
    wests = [right[0], jnp.where(first, right[0], right[1]), jnp.where(first, right[1], right[2])]
    easts = [jnp.where(last, left[1], left[0]), jnp.where(last, left[2], left[1]), left[2]]
    for k in range(3):
        around = (coefs[k, up, :] + coefs[k, down, :]) + (wests[k] + easts[k])
        held[0, k, :, :] = 1.0 - here[k] * around
        held[1, k, :, :] = here[k] * here[k]


def broaden(rows, held, kind, out):
    lane = lax.broadcasted_iota(jnp.int32, (40, LANES), 1)
    rest = jnp.zeros((LANES - 40, LANES), jnp.float32)
    main = jnp.concatenate([held[kind, 1, :, :], rest], axis=0).T
    outer = jnp.where(lane >= LANES - PAD, held[kind, 0, :, :], held[kind, 2, :, :])
    outer = jnp.concatenate([outer, rest], axis=0).T
    for j in range(rows + 2 * STEPS - 2):
        base = (j + 1) * PITCH
        column = outer[:, j : j + 1]
        out[pl.ds(base, PAD), :] = jnp.broadcast_to(column[LANES - PAD :], (PAD, LANES))
        out[pl.ds(base + PAD, LANES), :] = jnp.broadcast_to(main[:, j : j + 1], (LANES, LANES))
        out[pl.ds(base + PAD + LANES, PAD), :] = jnp.broadcast_to(column[:PAD], (PAD, LANES))


def turn(n_lat, n_lon, off, weight, off_t, w_t):
    blocks, height, _ = off.shape
    cap, padded = blocks * LANES, off_t.shape[1]
    width = n_lon // off_t.shape[0]
    ways = SUB // width
    row = lax.broadcasted_iota(jnp.int32, (SUB, LANES), 0) // width

    def gather(src, c, g):
        tiles = []
        for start in range(0, height, n_lon * ways):
            tile = src[c, pl.ds(start + g * width, SUB), :]
            for k in range(1, ways):
                piece = src[c, pl.ds(start + k * n_lon + g * width - k * width, SUB), :]
                tile = jnp.where(row == k, piece, tile)
            tiles.append(tile)
        return jnp.concatenate(tiles, axis=0).T

    for g in range(off_t.shape[0]):
        if padded > cap:
            off_t[g, cap:padded, :] = jnp.zeros((padded - cap, LANES), jnp.int32)
            w_t[g, cap:padded, :] = jnp.zeros((padded - cap, LANES), jnp.float32)
        for c in range(blocks):
            off_t[g, pl.ds(c * LANES, LANES), :] = gather(off, c, g)
            w_t[g, pl.ds(c * LANES, LANES), :] = gather(weight, c, g)


def squeeze(layers, kept, few, src, dst):
    spare = LANES - layers
    size = -(-few // SUB) * SUB
    whole = dst.shape[0]
    lane = lax.broadcasted_iota(jnp.int32, (size, LANES), 1)
    dst[...] = src[pl.ds(0, whole), :]
    rest = src[pl.ds(kept, size), :]
    dst[pl.ds(0, size), :] = jnp.where(lane < layers, src[pl.ds(0, size), :], rest)
    moved = pltpu.roll(rest, layers - spare, 1)
    dst[pl.ds(few, size), :] = jnp.where(lane < layers, src[pl.ds(few, size), :], moved)


def unsqueeze(layers, kept, few, src, dst):
    spare = LANES - layers
    size = -(-few // SUB) * SUB
    lane = lax.broadcasted_iota(jnp.int32, (size, LANES), 1)
    dst[pl.ds(PAD, src.shape[0]), :] = src[...]
    first = pltpu.roll(src[pl.ds(0, size), :], spare, 1)
    second = pltpu.roll(src[pl.ds(few, size), :], LANES - layers + spare, 1)
    dst[pl.ds(PAD + kept, size), :] = jnp.where(lane < spare, first, second)


def field_kernel(
    n_lat,
    n_lon,
    rows,
    layers,
    control_ref,
    kappa_ref,
    mask_ref,
    vert_ref,
    off_ref,
    w_ref,
    inc_ref,
    off_t,
    w_t,
    control,
    kappa,
    mask,
    vert,
    off,
    weight,
    inverse,
    ratio,
    coefs,
    held,
    laid,
    far_rows,
    side_out,
    side_in,
    corner_out,
    corner_in,
    side_sent,
    side_got,
    corner_sent,
    corner_got,
    near,
    far,
    c0,
    k2,
    done,
    load_sem,
    coef_send,
    coef_recv,
    send_sem,
    recv_sem,
):
    lat, lon = lax.axis_index("lat"), lax.axis_index("lon")
    tall = rows + 2 * STEPS
    pairs = ((control_ref, control), (kappa_ref, kappa), (mask_ref, mask))
    pairs += ((vert_ref, vert),)
    for c in range(off.shape[0]):
        here = pl.ds(c * LANES, LANES)
        pairs += ((off_ref.at[:, here], off.at[c]), (w_ref.at[:, here], weight.at[c]))
    loads = [pltpu.make_async_copy(a, b, load_sem.at[i]) for i, (a, b) in enumerate(pairs)]
    for i in (1, 2, 0, *range(3, len(loads))):
        loads[i].start()

    def place(i):
        return (lat + WAYS[i][0], lax.rem(lon + WAYS[i][1] + n_lon, n_lon))

    def guard(step, body):
        if step == 0:
            body()
        else:
            pl.when(lat > 0 if step < 0 else lat < n_lat - 1)(body)

    corner_got[...] = jnp.zeros_like(corner_got)
    barrier = pltpu.get_barrier_semaphore()
    for i, way in enumerate(WAYS):
        guard(
            way[0],
            lambda i=i: pl.semaphore_signal(
                barrier, inc=1, device_id=place(i), device_id_type=pl.DeviceIdType.MESH
            ),
        )

    side_in[...] = jnp.zeros_like(side_in)
    corner_in[...] = jnp.zeros_like(corner_in)

    @pl.when(lat == 0)
    def _():
        coefs[:, :rows, :] = jnp.zeros((3, rows, LANES), jnp.float32)
        far_rows[1] = jnp.zeros((STEPS * layers, LANES), jnp.float32)

    @pl.when(lat == n_lat - 1)
    def _():
        coefs[:, 2 * rows :, :] = jnp.zeros((3, rows, LANES), jnp.float32)
        far_rows[0] = jnp.zeros((STEPS * layers, LANES), jnp.float32)

    def remote(i, src, dst, out_sem, in_sem, part=0):
        return pltpu.make_async_remote_copy(
            src_ref=src,
            dst_ref=dst,
            send_sem=out_sem.at[i + part * len(WAYS)],
            recv_sem=in_sem.at[i + part * len(WAYS)],
            device_id=place(i),
            device_id_type=pl.DeviceIdType.MESH,
        )

    def coef_copy(i):
        dl, dn = WAYS[i]
        return remote(
            i, coefs.at[1, pl.ds(rows, rows)], coefs.at[1 - dn, pl.ds((1 - dl) * rows, rows)], coef_send, coef_recv
        )

    spots = corner_spots()[0]

    half = STEPS // 2 * layers

    def field_copy(i, part=0):
        dl, dn = WAYS[i]
        if dn == 0:
            start = 0 if dl < 0 else (rows - STEPS) * layers
            src = laid.at[pl.ds(start + part * half, half)]
            dst = far_rows.at[i, pl.ds(part * half, half)]
        elif dl == 0:
            src, dst = side_sent.at[i - 2], side_got.at[i - 2]
        else:
            src, dst = corner_sent.at[i - 4], corner_got.at[i - 4]
        return remote(i, src, dst, send_sem, recv_sem, part)

    loads[1].wait()
    loads[2].wait()
    coefs[1, pl.ds(rows, rows), :] = kappa[...] * mask[...].astype(jnp.float32)
    loads[0].wait()
    for r in range(rows):
        here = coefs[1, pl.ds(rows + r, 1), :]
        for g in range(layers // SUB):
            laid[pl.ds(r * layers + g * SUB, SUB), :] = (
                control[pl.ds(g * SUB * rows + r, SUB, stride=rows), :] * here
            )
    def upright(block):
        return jnp.concatenate([block, block[: LANES - layers]], axis=0).T

    def main_row(r, carry):
        block = laid[aligned(r * layers, layers), :]
        near[aligned((r + STEPS) * PITCH + PAD, LANES), :] = upright(block)
        return carry

    lax.fori_loop(0, rows, main_row, 0, unroll=2)
    for k, first in ((0, PAD), (1, PAD + LANES - STEPS)):
        for r in range(rows):
            side_out[k, pl.ds(r * STEPS, PAD), :] = near[
                pl.ds((r + STEPS) * PITCH + first, PAD), :
            ]
        squeeze(layers, *side_split(rows), side_out.at[k], side_sent.at[k])
    for i in range(4, 8):
        dl, dn = WAYS[i]
        for d, at, count in spots:
            r = d - 1 if dl < 0 else rows - d
            first = PAD if dn < 0 else PAD + LANES - count
            corner_out[i - 4, pl.ds(at, PAD), :] = near[pl.ds((r + STEPS) * PITCH + first, PAD), :]
        squeeze(layers, *corner_split(), corner_out.at[i - 4], corner_sent.at[i - 4])
    beside = (lat > 0).astype(jnp.int32) + (lat < n_lat - 1).astype(jnp.int32)
    pl.semaphore_wait(barrier, 2 + 3 * beside)
    for i, way in enumerate(WAYS):
        guard(way[0], lambda i=i: coef_copy(i).start())
    for i in (2, 3, 0, 1, 4, 5, 6, 7):
        guard(WAYS[i][0], lambda i=i: field_copy(i).start())
    for i in (0, 1):
        guard(WAYS[i][0], lambda i=i: field_copy(i, 1).start())

    for i in range(3, len(loads)):
        loads[i].wait()
    turn(n_lat, n_lon, off, weight, off_t, w_t)
    factor(rows, vert, inverse, ratio)
    for i, way in enumerate(WAYS):
        guard(-way[0], lambda i=i: coef_copy(i).wait_recv())
    weigh(rows, coefs, held)
    broaden(rows, held, 0, c0)
    broaden(rows, held, 1, k2)

    for i in (2, 3):
        field_copy(i).wait_recv()
        unsqueeze(layers, *side_split(rows), side_got.at[i - 2], side_in.at[i - 2])
        for r in range(rows):
            base = (r + STEPS) * PITCH
            if i == 3:
                near[pl.ds(base, PAD), :] = side_in[1, pl.ds((r + 1) * STEPS, PAD), :]
            else:
                near[pl.ds(base + PAD + LANES, PAD), :] = side_in[0, pl.ds(PAD + r * STEPS, PAD), :]
    for i in range(4, 8):
        dl, dn = WAYS[i]
        guard(-dl, lambda i=i: field_copy(i).wait_recv())
        unsqueeze(layers, *corner_split(), corner_got.at[i - 4], corner_in.at[i - 4])
        for d in range(1, STEPS + 1):
            at, count = spots[d - 1][1:] if d < STEPS else (0, 0)
            r = STEPS + rows + d - 1 if dl < 0 else STEPS - d
            if dn > 0:
                near[pl.ds(r * PITCH, PAD), :] = corner_in[i - 4, pl.ds(at + count, PAD), :]
            else:
                near[pl.ds(r * PITCH + PAD + LANES, PAD), :] = corner_in[i - 4, pl.ds(PAD + at, PAD), :]

    diffuse_inner(rows, near, far, c0, k2)
    for part in (0, 1):
        for i in (0, 1):
            guard(-WAYS[i][0], lambda i=i, part=part: field_copy(i, part).wait_recv())
            start = (STEPS + rows) if i == 0 else 0

            def far_row(r, carry, i=i, start=start):
                block = far_rows[i, aligned(r * layers, layers), :]
                near[aligned((r + start) * PITCH + PAD, LANES), :] = upright(block)
                return carry

            first = part * (STEPS // 2)
            lax.fori_loop(first, first + STEPS // 2, far_row, 0, unroll=True)

    diffuse_rest(rows, near, far, c0, k2)

    def back_row(r, carry):
        done[aligned(r * LANES, LANES), :] = near[aligned((r + STEPS) * PITCH + PAD, LANES), :].T
        return carry

    lax.fori_loop(0, rows, back_row, 0, unroll=2)
    solve_columns(rows, layers, done, control, coefs.at[1], vert, inverse, ratio, inc_ref)
    for i, way in enumerate(WAYS):
        guard(way[0], lambda i=i: coef_copy(i).wait_send())
        guard(way[0], lambda i=i: field_copy(i).wait_send())
        if way[1] == 0:
            guard(way[0], lambda i=i: field_copy(i, 1).wait_send())


def pick(table, row, col):
    level = [jnp.take_along_axis(t, col, axis=1) for t in table]
    bit = 1
    while len(level) > 1:
        odd = (row & bit) != 0
        level = [jnp.where(odd, level[i + 1], level[i]) for i in range(0, len(level), 2)]
        bit *= 2
    return level[0]


def lookup(rows, layers, turns, inc_ref, off_t, w_t, acc):
    def one_group(lg, carry):
        base = pl.multiple_of(lg * SUB, SUB)
        table = [inc_ref[pl.ds(base * rows + r, SUB, stride=rows), :] for r in range(rows)]
        for m in range(turns):
            at = pl.ds(m * layers + base, SUB)
            idx = off_t[at, :]
            acc[at, :] = pick(table, idx >> 7, idx & (LANES - 1)) * w_t[at, :]
        return carry

    lax.fori_loop(0, layers // SUB, one_group, 0, unroll=5)


def observe_kernel(
    n_lat,
    n_lon,
    rows,
    layers,
    inc_ref,
    off_t,
    w_t,
    target_ref,
    value_ref,
    target,
    acc,
    parts,
    received,
    total,
    load_sem,
    part_send,
    part_recv,
):
    lat, lon = lax.axis_index("lat"), lax.axis_index("lon")
    me, devices = lat * n_lon + lon, n_lat * n_lon
    passes, padded = off_t.shape[0], off_t.shape[1]
    members, width = devices // passes, n_lon // passes
    mine, local = lon // width, lat * width + lon % width
    blocks, high = parts.shape[1], value_ref.shape[0]
    load = pltpu.make_async_copy(target_ref, target, load_sem.at[0])
    load.start()
    barrier = pltpu.get_barrier_semaphore()

    def greet(k, carry):
        q = lax.rem(me + k, devices)
        pl.semaphore_signal(
            barrier, inc=1, device_id=(q // n_lon, q % n_lon), device_id_type=pl.DeviceIdType.MESH
        )
        return carry

    lax.fori_loop(1, devices, greet, 0)

    def toward(t):
        return lax.rem(mine + t + 1, passes)

    def slots(t, i, count=1):
        return pl.ds(t * members + i, count)

    def copy(src, dst, in_sem, there):
        return pltpu.make_async_remote_copy(
            src_ref=src,
            dst_ref=dst,
            send_sem=part_send.at[0],
            recv_sem=in_sem,
            device_id=there,
            device_id_type=pl.DeviceIdType.MESH,
        )

    def part_copy(t, i):
        there = lax.rem(local + i, members)
        place = (there // width, toward(t) * width + there % width)
        src, dst = parts.at[slots(t, there)], received.at[slots(t, i)]
        return copy(src, dst, part_recv.at[t, i // GROUP], place)

    def wait_group(t, g, first, count):
        here = slots(t, g * GROUP + first, count)
        copy(parts.at[here], received.at[here], part_recv.at[t, g], (lat, lon)).wait_recv()

    def look_up(t, carry):
        lookup(rows, layers, padded // layers, inc_ref, off_t.at[toward(t)], w_t.at[toward(t)], acc)
        for b in range(blocks):
            block = acc[pl.ds(b * LANES, LANES), :].T
            part = block[:members]
            for k in range(1, LANES // members):
                part = part + block[k * members : (k + 1) * members]
            parts[slots(t, 0, members), b, :] = part

        @pl.when(t == 0)
        def _():
            pl.semaphore_wait(barrier, devices - 1)

        def send(i, carry):
            part_copy(t, i).start()
            return carry

        lax.fori_loop((t == passes - 1).astype(jnp.int32), members, send, 0)
        return carry

    total[...] = jnp.zeros_like(total)
    lax.fori_loop(0, passes, look_up, 0)
    received[slots(passes - 1, 0)] = parts[slots(passes - 1, local)]
    load.wait()

    def add_group(turn, carry):
        t, g = turn // (members // GROUP), turn % (members // GROUP)
        result = total[...]
        source = lax.rem(mine + passes - t - 1, passes) * width
        own = jnp.logical_and(t == passes - 1, g == 0)
        pl.when(own)(lambda: wait_group(t, g, 1, GROUP - 1))
        pl.when(jnp.logical_not(own))(lambda: wait_group(t, g, 0, GROUP))
        for k in range(GROUP):
            i = g * GROUP + k
            p = lax.rem(local - i + members, members)
            p = p // width * n_lon + source + p % width
            cells = received[t * members + i]
            v = jnp.concatenate([cells[b : b + 1, :] for b in range(blocks)], axis=1)
            result = result + spread(v, target[pl.ds(p, 1), :], high)
        total[...] = result
        return carry

    lax.fori_loop(0, devices // GROUP, add_group, 0)
    value_ref[...] = total[:high] + total[high:]
    sent = pl.ds(0, devices - 1)
    copy(parts.at[sent], received.at[sent], part_recv.at[0, 0], (lat, lon)).wait_send()


def floats(*shape):
    return jax.ShapeDtypeStruct(shape, jnp.float32)


def spread(v, t, high):
    shape, bf = (high, v.shape[1]), jnp.bfloat16
    flat = (LANES, v.shape[1])
    upper = lax.broadcasted_iota(jnp.int32, shape, 0).astype(bf)
    lower = lax.broadcasted_iota(jnp.int32, flat, 0).astype(bf)
    hit = upper == jnp.broadcast_to((t >> 7).astype(jnp.float32), shape).astype(bf)
    one = lower == jnp.broadcast_to((t & (LANES - 1)).astype(jnp.float32), flat).astype(bf)
    first = v.astype(bf).astype(jnp.float32)
    left = jnp.concatenate(
        [
            jnp.where(hit, jnp.broadcast_to(part, shape).astype(bf), jnp.zeros(shape, bf))
            for part in (first, v - first)
        ],
        axis=0,
    )
    right = jnp.where(one, jnp.ones(flat, bf), jnp.zeros(flat, bf))
    return lax.dot_general(
        left, right, (((1,), (1,)), ((), ())), preferred_element_type=jnp.float32
    )


def per_device(
    control,
    kappa,
    sea_mask,
    vert_coef,
    stencil_offsets,
    stencil_weights,
    slot_target,
    observed,
    inv_error,
):
    levels, fields, rows, cols = control.shape
    layers = levels * fields
    tall = rows + 2 * STEPS
    sten, owners, cap = stencil_offsets.shape
    bundles = sten * owners // LANES
    padded = -(-cap // layers) * layers
    corner = corner_spots()[1] + 2 * PAD
    high = observed.shape[0] // LANES
    blocks = cap // LANES
    members = owners // bundles

    def vmem(*shape, dtype=jnp.float32):
        return pltpu.VMEM(shape, dtype)

    wide = (tall * PITCH, LANES)
    dma = pltpu.SemaphoreType.DMA
    place = (lax.axis_size("lat"), lax.axis_size("lon"))
    shapes = (
        floats(layers * rows, LANES),
        jax.ShapeDtypeStruct((bundles, padded, LANES), jnp.int32),
        floats(bundles, padded, LANES),
    )
    arrays = (
        control.reshape(layers * rows, cols),
        kappa,
        sea_mask,
        vert_coef.reshape(levels * rows, cols),
        stencil_offsets.reshape(sten * owners, cap),
        stencil_weights.reshape(sten * owners, cap),
    )
    increment, off_t, w_t = pl.pallas_call(
        functools.partial(field_kernel, *place, rows, layers),
        out_shape=shapes,
        in_specs=[pl.BlockSpec(memory_space=pltpu.HBM)] * len(arrays),
        out_specs=tuple(pl.BlockSpec(memory_space=pltpu.VMEM) for _ in shapes),
        scratch_shapes=[
            vmem(layers * rows, LANES),
            vmem(rows, LANES),
            vmem(rows, LANES, dtype=jnp.int32),
            vmem(levels * rows, LANES),
            vmem(blocks, sten * owners, LANES, dtype=jnp.int32),
            vmem(blocks, sten * owners, LANES),
            vmem(levels * rows, LANES),
            vmem(levels * rows, LANES),
            vmem(3, 3 * rows, LANES),
            vmem(2, 3, 40, LANES),
            vmem(rows * layers, LANES),
            vmem(2, STEPS * layers, LANES),
            vmem(2, rows * STEPS + 2 * PAD, LANES),
            vmem(2, rows * STEPS + 2 * PAD, LANES),
            vmem(4, corner, LANES),
            vmem(4, corner, LANES),
            vmem(2, message(*side_split(rows)), LANES),
            vmem(2, message(*side_split(rows)), LANES),
            vmem(4, message(*corner_split()), LANES),
            vmem(4, message(*corner_split()), LANES),
            vmem(*wide),
            vmem(*wide),
            vmem(*wide),
            vmem(*wide),
            vmem(rows * LANES, LANES),
            dma((4 + 2 * blocks,)),
            dma((len(WAYS),)),
            dma((len(WAYS),)),
            dma((2 * len(WAYS),)),
            dma((2 * len(WAYS),)),
        ],
        compiler_params=pltpu.CompilerParams(
            vmem_limit_bytes=44 * 1024 * 1024, collective_id=2, has_side_effects=True
        ),
        name="field",
    )(*[pltpu.with_memory_space_constraint(a, pltpu.HBM) for a in arrays])
    vm = pl.BlockSpec(memory_space=pltpu.VMEM)
    value = pl.pallas_call(
        functools.partial(observe_kernel, *place, rows, layers),
        out_shape=floats(high, LANES),
        in_specs=[vm, vm, vm, pl.BlockSpec(memory_space=pltpu.HBM)],
        out_specs=vm,
        scratch_shapes=[
            vmem(owners, cap, dtype=jnp.int32),
            vmem(padded, LANES),
            vmem(owners, blocks, LANES),
            vmem(owners, blocks, LANES),
            vmem(2 * high, LANES),
            dma((1,)),
            dma((1,)),
            dma((bundles, members // GROUP)),
        ],
        compiler_params=pltpu.CompilerParams(
            vmem_limit_bytes=24 * 1024 * 1024, collective_id=3, has_side_effects=True
        ),
        name="observe",
    )(increment, off_t, w_t, pltpu.with_memory_space_constraint(slot_target, pltpu.HBM))
    return increment.reshape(control.shape), (value.reshape(-1) - observed) * inv_error


def solution(mesh):
    return jax.shard_map(
        per_device,
        mesh=mesh,
        in_specs=(
            P(None, None, "lat", "lon"),
            P("lat", "lon"),
            P("lat", "lon"),
            P(None, "lat", "lon"),
            P(None, ("lat", "lon"), None),
            P(None, ("lat", "lon"), None),
            P(("lat", "lon"), None),
            P(("lat", "lon")),
            P(("lat", "lon")),
        ),
        out_specs=(P(None, None, "lat", "lon"), P(("lat", "lon"))),
        check_vma=False,
    )
```

```python
import functools

import jax
import jax.numpy as jnp
from jax import lax
from jax.experimental import pallas as pl
from jax.experimental.pallas import tpu as pltpu
from jax.sharding import PartitionSpec as P

STEPS = 10
LANES = 128
SUB = 8


GROUP = 8
WAYS = ((-1, 0), (1, 0), (0, -1), (0, 1), (-1, -1), (-1, 1), (1, -1), (1, 1))
PAD = 16
PITCH = LANES + 2 * PAD


def aligned(start, size):
    return pl.ds(pl.multiple_of(start, SUB), size)


def corner_spots():
    spots, at = [], 0
    for d in range(1, STEPS):
        spots.append((d, at, STEPS - d))
        at += STEPS - d
    return spots, -(-at // SUB) * SUB


def corner_split():
    count = STEPS * (STEPS - 1) // 2
    return count - count // 3, count // 3


def side_split(rows):
    return (rows - rows // 3) * STEPS, rows // 3 * STEPS


def message(kept, few):
    return max(-(-kept // SUB), -(-few // SUB) + -(-few // SUB)) * SUB


def update(old, new, c0, k2, count, first, low, high, per):
    def some_rows(turn, carry):
        base = (first + per * turn) * PITCH
        for v in range(low, high):
            spot = [aligned(base + d * PITCH + v * SUB, SUB) for d in range(-1, per + 1)]
            cells = [old[s, :] for s in spot]
            for d in range(per):
                at = base + d * PITCH + v * SUB
                side = old[pl.ds(at - 1, SUB), :] + old[pl.ds(at + 1, SUB), :]
                around = (cells[d] + cells[d + 2]) + side
                new[spot[d + 1], :] = c0[spot[d + 1], :] * cells[d + 1] + k2[spot[d + 1], :] * around
        return carry

    lax.fori_loop(0, count, some_rows, 0)


def span(old, new, c0, k2, first, count, low, high):
    per = 5 if count % 10 == 0 and count < 20 else 6
    update(old, new, c0, k2, count // per, first, low, high, per)
    if count % per:
        update(old, new, c0, k2, 1, first + count // per * per, low, high, count % per)


def diffuse_inner(rows, old, new, c0, k2):
    width = PITCH // SUB
    span(old, new, c0, k2, STEPS + 1, rows - 2, 0, width)
    span(new, old, c0, k2, STEPS + 2, rows - 4, 1, width - 1)


def diffuse_rest(rows, old, new, c0, k2):
    tall = rows + 2 * STEPS
    width = PITCH // SUB
    for first in (1, STEPS + rows - 1):
        span(old, new, c0, k2, first, STEPS, 0, width)
    for first in (2, STEPS + rows - 2):
        span(new, old, c0, k2, first, STEPS, 1, width - 1)

    for s in range(2, STEPS):
        edge = 1 if s < STEPS - 1 else PAD // SUB
        span(old, new, c0, k2, s + 1, tall - 2 - 2 * s, edge, width - edge)
        old, new = new, old


def factor(rows, vert, inverse, ratio):
    levels = vert.shape[0] // rows
    above = vert[pl.ds(0, rows), :]
    cprev = jnp.zeros((rows, LANES), jnp.float32)
    for k in range(levels):
        if k + 1 < levels:
            below = vert[pl.ds((k + 1) * rows, rows), :]
        else:
            below = jnp.zeros((rows, LANES), jnp.float32)
        inv = 1.0 / (((1.0 + above) + below) + above * cprev)
        cprev = -below * inv
        inverse[pl.ds(k * rows, rows), :] = inv
        ratio[pl.ds(k * rows, rows), :] = cprev
        above = below


def solve_columns(rows, layers, done, control, coef, vert, inverse, ratio, inc_ref):
    levels = vert.shape[0] // rows
    fields = layers // levels
    for h in range(rows // SUB):
        here = coef[pl.ds(rows + h * SUB, SUB), :]
        sea = here != 0.0
        back = 1.0 / jnp.where(sea, here, 1.0)
        prev = [jnp.zeros((SUB, LANES), jnp.float32)] * fields
        for k in range(levels):
            level = pl.ds(k * rows + h * SUB, SUB)
            above, inv = vert[level, :], inverse[level, :]
            for f in range(fields):
                layer = k * fields + f
                at = pl.ds(layer * rows + h * SUB, SUB)
                right = done[pl.ds(h * SUB * LANES + layer, SUB, stride=LANES), :] * back
                right = jnp.where(sea, right, control[at, :])
                prev[f] = (right + above * prev[f]) * inv
                inc_ref[at, :] = prev[f]
        for k in range(levels - 2, -1, -1):
            fall = ratio[pl.ds(k * rows + h * SUB, SUB), :]
            for f in range(fields):
                at = pl.ds((k * fields + f) * rows + h * SUB, SUB)
                prev[f] = inc_ref[at, :] - fall * prev[f]
                inc_ref[at, :] = prev[f]


def weigh(rows, coefs, held):
    lane = lax.broadcasted_iota(jnp.int32, (40, LANES), 1)
    mid = pl.ds(rows - STEPS + 1, 40)
    up = pl.ds(rows - STEPS, 40)
    down = pl.ds(rows - STEPS + 2, 40)
    here = [coefs[k, mid, :] for k in range(3)]
    right = [pltpu.roll(c, 1, 1) for c in here]
    left = [pltpu.roll(c, LANES - 1, 1) for c in here]
    first, last = lane == 0, lane == LANES - 1
    wests = [right[0], jnp.where(first, right[0], right[1]), jnp.where(first, right[1], right[2])]
    easts = [jnp.where(last, left[1], left[0]), jnp.where(last, left[2], left[1]), left[2]]
    for k in range(3):
        around = (coefs[k, up, :] + coefs[k, down, :]) + (wests[k] + easts[k])
        held[0, k, :, :] = 1.0 - here[k] * around
        held[1, k, :, :] = here[k] * here[k]


def broaden(rows, held, kind, out):
    lane = lax.broadcasted_iota(jnp.int32, (40, LANES), 1)
    rest = jnp.zeros((LANES - 40, LANES), jnp.float32)
    main = jnp.concatenate([held[kind, 1, :, :], rest], axis=0).T
    outer = jnp.where(lane >= LANES - PAD, held[kind, 0, :, :], held[kind, 2, :, :])
    outer = jnp.concatenate([outer, rest], axis=0).T
    for j in range(rows + 2 * STEPS - 2):
        base = (j + 1) * PITCH
        column = outer[:, j : j + 1]
        out[pl.ds(base, PAD), :] = jnp.broadcast_to(column[LANES - PAD :], (PAD, LANES))
        out[pl.ds(base + PAD, LANES), :] = jnp.broadcast_to(main[:, j : j + 1], (LANES, LANES))
        out[pl.ds(base + PAD + LANES, PAD), :] = jnp.broadcast_to(column[:PAD], (PAD, LANES))


def turn(n_lat, n_lon, off, weight, off_t, w_t):
    blocks, height, _ = off.shape
    cap, padded = blocks * LANES, off_t.shape[1]
    width = n_lon // off_t.shape[0]
    ways = SUB // width
    row = lax.broadcasted_iota(jnp.int32, (SUB, LANES), 0) // width

    def gather(src, c, g):
        tiles = []
        for start in range(0, height, n_lon * ways):
            tile = src[c, pl.ds(start + g * width, SUB), :]
            for k in range(1, ways):
                piece = src[c, pl.ds(start + k * n_lon + g * width - k * width, SUB), :]
                tile = jnp.where(row == k, piece, tile)
            tiles.append(tile)
        return jnp.concatenate(tiles, axis=0).T

    for g in range(off_t.shape[0]):
        if padded > cap:
            off_t[g, cap:padded, :] = jnp.zeros((padded - cap, LANES), jnp.int32)
            w_t[g, cap:padded, :] = jnp.zeros((padded - cap, LANES), jnp.float32)
        for c in range(blocks):
            off_t[g, pl.ds(c * LANES, LANES), :] = gather(off, c, g)
            w_t[g, pl.ds(c * LANES, LANES), :] = gather(weight, c, g)


def squeeze(layers, kept, few, src, dst):
    spare = LANES - layers
    size = -(-few // SUB) * SUB
    whole = dst.shape[0]
    lane = lax.broadcasted_iota(jnp.int32, (size, LANES), 1)
    dst[...] = src[pl.ds(0, whole), :]
    rest = src[pl.ds(kept, size), :]
    dst[pl.ds(0, size), :] = jnp.where(lane < layers, src[pl.ds(0, size), :], rest)
    moved = pltpu.roll(rest, layers - spare, 1)
    dst[pl.ds(few, size), :] = jnp.where(lane < layers, src[pl.ds(few, size), :], moved)


def unsqueeze(layers, kept, few, src, dst):
    spare = LANES - layers
    size = -(-few // SUB) * SUB
    lane = lax.broadcasted_iota(jnp.int32, (size, LANES), 1)
    dst[pl.ds(PAD, src.shape[0]), :] = src[...]
    first = pltpu.roll(src[pl.ds(0, size), :], spare, 1)
    second = pltpu.roll(src[pl.ds(few, size), :], LANES - layers + spare, 1)
    dst[pl.ds(PAD + kept, size), :] = jnp.where(lane < spare, first, second)


def field_kernel(
    n_lat,
    n_lon,
    rows,
    layers,
    control_ref,
    kappa_ref,
    mask_ref,
    vert_ref,
    off_ref,
    w_ref,
    inc_ref,
    off_t,
    w_t,
    control,
    kappa,
    mask,
    vert,
    off,
    weight,
    inverse,
    ratio,
    coefs,
    held,
    laid,
    far_rows,
    side_out,
    side_in,
    corner_out,
    corner_in,
    side_sent,
    side_got,
    corner_sent,
    corner_got,
    near,
    far,
    c0,
    k2,
    done,
    load_sem,
    coef_send,
    coef_recv,
    send_sem,
    recv_sem,
):
    lat, lon = lax.axis_index("lat"), lax.axis_index("lon")
    tall = rows + 2 * STEPS
    pairs = ((control_ref, control), (kappa_ref, kappa), (mask_ref, mask))
    pairs += ((vert_ref, vert),)
    for c in range(off.shape[0]):
        here = pl.ds(c * LANES, LANES)
        pairs += ((off_ref.at[:, here], off.at[c]), (w_ref.at[:, here], weight.at[c]))
    loads = [pltpu.make_async_copy(a, b, load_sem.at[i]) for i, (a, b) in enumerate(pairs)]
    for i in (1, 2, 0, *range(3, len(loads))):
        loads[i].start()

    def place(i):
        return (lat + WAYS[i][0], lax.rem(lon + WAYS[i][1] + n_lon, n_lon))

    def guard(step, body):
        if step == 0:
            body()
        else:
            pl.when(lat > 0 if step < 0 else lat < n_lat - 1)(body)

    corner_got[...] = jnp.zeros_like(corner_got)
    barrier = pltpu.get_barrier_semaphore()
    for i, way in enumerate(WAYS):
        guard(
            way[0],
            lambda i=i: pl.semaphore_signal(
                barrier, inc=1, device_id=place(i), device_id_type=pl.DeviceIdType.MESH
            ),
        )

    side_in[...] = jnp.zeros_like(side_in)
    corner_in[...] = jnp.zeros_like(corner_in)

    @pl.when(lat == 0)
    def _():
        coefs[:, :rows, :] = jnp.zeros((3, rows, LANES), jnp.float32)
        far_rows[1] = jnp.zeros((STEPS * layers, LANES), jnp.float32)

    @pl.when(lat == n_lat - 1)
    def _():
        coefs[:, 2 * rows :, :] = jnp.zeros((3, rows, LANES), jnp.float32)
        far_rows[0] = jnp.zeros((STEPS * layers, LANES), jnp.float32)

    def remote(i, src, dst, out_sem, in_sem, part=0):
        return pltpu.make_async_remote_copy(
            src_ref=src,
            dst_ref=dst,
            send_sem=out_sem.at[i + part * len(WAYS)],
            recv_sem=in_sem.at[i + part * len(WAYS)],
            device_id=place(i),
            device_id_type=pl.DeviceIdType.MESH,
        )

    def coef_copy(i):
        dl, dn = WAYS[i]
        return remote(
            i, coefs.at[1, pl.ds(rows, rows)], coefs.at[1 - dn, pl.ds((1 - dl) * rows, rows)], coef_send, coef_recv
        )

    spots = corner_spots()[0]

    half = STEPS // 2 * layers

    def field_copy(i, part=0):
        dl, dn = WAYS[i]
        if dn == 0:
            start = 0 if dl < 0 else (rows - STEPS) * layers
            src = laid.at[pl.ds(start + part * half, half)]
            dst = far_rows.at[i, pl.ds(part * half, half)]
        elif dl == 0:
            src, dst = side_sent.at[i - 2], side_got.at[i - 2]
        else:
            src, dst = corner_sent.at[i - 4], corner_got.at[i - 4]
        return remote(i, src, dst, send_sem, recv_sem, part)

    loads[1].wait()
    loads[2].wait()
    coefs[1, pl.ds(rows, rows), :] = kappa[...] * mask[...].astype(jnp.float32)
    loads[0].wait()
    for r in range(rows):
        here = coefs[1, pl.ds(rows + r, 1), :]
        for g in range(layers // SUB):
            laid[pl.ds(r * layers + g * SUB, SUB), :] = (
                control[pl.ds(g * SUB * rows + r, SUB, stride=rows), :] * here
            )
    def upright(block):
        return jnp.concatenate([block, block[: LANES - layers]], axis=0).T

    def main_row(r, carry):
        block = laid[aligned(r * layers, layers), :]
        near[aligned((r + STEPS) * PITCH + PAD, LANES), :] = upright(block)
        return carry

    lax.fori_loop(0, rows, main_row, 0, unroll=2)
    for k, first in ((0, PAD), (1, PAD + LANES - STEPS)):
        for r in range(rows):
            side_out[k, pl.ds(r * STEPS, PAD), :] = near[
                pl.ds((r + STEPS) * PITCH + first, PAD), :
            ]
        squeeze(layers, *side_split(rows), side_out.at[k], side_sent.at[k])
    for i in range(4, 8):
        dl, dn = WAYS[i]
        for d, at, count in spots:
            r = d - 1 if dl < 0 else rows - d
            first = PAD if dn < 0 else PAD + LANES - count
            corner_out[i - 4, pl.ds(at, PAD), :] = near[pl.ds((r + STEPS) * PITCH + first, PAD), :]
        squeeze(layers, *corner_split(), corner_out.at[i - 4], corner_sent.at[i - 4])
    beside = (lat > 0).astype(jnp.int32) + (lat < n_lat - 1).astype(jnp.int32)
    pl.semaphore_wait(barrier, 2 + 3 * beside)
    for i, way in enumerate(WAYS):
        guard(way[0], lambda i=i: coef_copy(i).start())
    for i in (2, 3, 0, 1, 4, 5, 6, 7):
        guard(WAYS[i][0], lambda i=i: field_copy(i).start())
    for i in (0, 1):
        guard(WAYS[i][0], lambda i=i: field_copy(i, 1).start())

    for i in range(3, len(loads)):
        loads[i].wait()
    turn(n_lat, n_lon, off, weight, off_t, w_t)
    factor(rows, vert, inverse, ratio)
    for i, way in enumerate(WAYS):
        guard(-way[0], lambda i=i: coef_copy(i).wait_recv())
    weigh(rows, coefs, held)
    broaden(rows, held, 0, c0)
    broaden(rows, held, 1, k2)

    for i in (2, 3):
        field_copy(i).wait_recv()
        unsqueeze(layers, *side_split(rows), side_got.at[i - 2], side_in.at[i - 2])
        for r in range(rows):
            base = (r + STEPS) * PITCH
            if i == 3:
                near[pl.ds(base, PAD), :] = side_in[1, pl.ds((r + 1) * STEPS, PAD), :]
            else:
                near[pl.ds(base + PAD + LANES, PAD), :] = side_in[0, pl.ds(PAD + r * STEPS, PAD), :]
    for i in range(4, 8):
        dl, dn = WAYS[i]
        guard(-dl, lambda i=i: field_copy(i).wait_recv())
        unsqueeze(layers, *corner_split(), corner_got.at[i - 4], corner_in.at[i - 4])
        for d in range(1, STEPS + 1):
            at, count = spots[d - 1][1:] if d < STEPS else (0, 0)
            r = STEPS + rows + d - 1 if dl < 0 else STEPS - d
            if dn > 0:
                near[pl.ds(r * PITCH, PAD), :] = corner_in[i - 4, pl.ds(at + count, PAD), :]
            else:
                near[pl.ds(r * PITCH + PAD + LANES, PAD), :] = corner_in[i - 4, pl.ds(PAD + at, PAD), :]

    diffuse_inner(rows, near, far, c0, k2)
    for part in (0, 1):
        for i in (0, 1):
            guard(-WAYS[i][0], lambda i=i, part=part: field_copy(i, part).wait_recv())
            start = (STEPS + rows) if i == 0 else 0

            def far_row(r, carry, i=i, start=start):
                block = far_rows[i, aligned(r * layers, layers), :]
                near[aligned((r + start) * PITCH + PAD, LANES), :] = upright(block)
                return carry

            first = part * (STEPS // 2)
            lax.fori_loop(first, first + STEPS // 2, far_row, 0, unroll=True)

    diffuse_rest(rows, near, far, c0, k2)

    def back_row(r, carry):
        done[aligned(r * LANES, LANES), :] = near[aligned((r + STEPS) * PITCH + PAD, LANES), :].T
        return carry

    lax.fori_loop(0, rows, back_row, 0, unroll=2)
    solve_columns(rows, layers, done, control, coefs.at[1], vert, inverse, ratio, inc_ref)
    for i, way in enumerate(WAYS):
        guard(way[0], lambda i=i: coef_copy(i).wait_send())
        guard(way[0], lambda i=i: field_copy(i).wait_send())
        if way[1] == 0:
            guard(way[0], lambda i=i: field_copy(i, 1).wait_send())


def pick(table, row, col):
    level = [jnp.take_along_axis(t, col, axis=1) for t in table]
    bit = 1
    while len(level) > 1:
        odd = (row & bit) != 0
        level = [jnp.where(odd, level[i + 1], level[i]) for i in range(0, len(level), 2)]
        bit *= 2
    return level[0]


def lookup(rows, layers, turns, inc_ref, off_t, w_t, acc):
    def one_group(lg, carry):
        base = pl.multiple_of(lg * SUB, SUB)
        table = [inc_ref[pl.ds(base * rows + r, SUB, stride=rows), :] for r in range(rows)]
        for m in range(turns):
            at = pl.ds(m * layers + base, SUB)
            idx = off_t[at, :]
            acc[at, :] = pick(table, idx >> 7, idx & (LANES - 1)) * w_t[at, :]
        return carry

    lax.fori_loop(0, layers // SUB, one_group, 0, unroll=5)


def observe_kernel(
    n_lat,
    n_lon,
    rows,
    layers,
    inc_ref,
    off_t,
    w_t,
    target_ref,
    value_ref,
    target,
    acc,
    parts,
    received,
    total,
    load_sem,
    part_send,
    part_recv,
):
    lat, lon = lax.axis_index("lat"), lax.axis_index("lon")
    me, devices = lat * n_lon + lon, n_lat * n_lon
    passes, padded = off_t.shape[0], off_t.shape[1]
    members, width = devices // passes, n_lon // passes
    mine, local = lon // width, lat * width + lon % width
    blocks, high = parts.shape[1], value_ref.shape[0]
    load = pltpu.make_async_copy(target_ref, target, load_sem.at[0])
    load.start()
    barrier = pltpu.get_barrier_semaphore()

    def greet(k, carry):
        q = lax.rem(me + k, devices)
        pl.semaphore_signal(
            barrier, inc=1, device_id=(q // n_lon, q % n_lon), device_id_type=pl.DeviceIdType.MESH
        )
        return carry

    lax.fori_loop(1, devices, greet, 0, unroll=True)

    def toward(t):
        return lax.rem(mine + t + 1, passes)

    def slots(t, i, count=1):
        return pl.ds(t * members + i, count)

    def copy(src, dst, in_sem, there):
        return pltpu.make_async_remote_copy(
            src_ref=src,
            dst_ref=dst,
            send_sem=part_send.at[0],
            recv_sem=in_sem,
            device_id=there,
            device_id_type=pl.DeviceIdType.MESH,
        )

    def part_copy(t, i):
        there = lax.rem(local + i, members)
        place = (there // width, toward(t) * width + there % width)
        src, dst = parts.at[slots(t, there)], received.at[slots(t, i)]
        return copy(src, dst, part_recv.at[t, i // GROUP], place)

    def wait_group(t, g, first, count):
        here = slots(t, g * GROUP + first, count)
        copy(parts.at[here], received.at[here], part_recv.at[t, g], (lat, lon)).wait_recv()

    def look_up(t, carry):
        lookup(rows, layers, padded // layers, inc_ref, off_t.at[toward(t)], w_t.at[toward(t)], acc)
        for b in range(blocks):
            block = acc[pl.ds(b * LANES, LANES), :].T
            part = block[:members]
            for k in range(1, LANES // members):
                part = part + block[k * members : (k + 1) * members]
            parts[slots(t, 0, members), b, :] = part

        @pl.when(t == 0)
        def _():
            pl.semaphore_wait(barrier, devices - 1)

        def send(i, carry):
            part_copy(t, i).start()
            return carry

        lax.fori_loop((t == passes - 1).astype(jnp.int32), members, send, 0)
        return carry

    total[...] = jnp.zeros_like(total)
    lax.fori_loop(0, passes, look_up, 0)
    received[slots(passes - 1, 0)] = parts[slots(passes - 1, local)]
    load.wait()

    def add_group(turn, carry):
        t, g = turn // (members // GROUP), turn % (members // GROUP)
        result = total[...]
        source = lax.rem(mine + passes - t - 1, passes) * width
        own = jnp.logical_and(t == passes - 1, g == 0)
        pl.when(own)(lambda: wait_group(t, g, 1, GROUP - 1))
        pl.when(jnp.logical_not(own))(lambda: wait_group(t, g, 0, GROUP))
        for k in range(GROUP):
            i = g * GROUP + k
            p = lax.rem(local - i + members, members)
            p = p // width * n_lon + source + p % width
            cells = received[t * members + i]
            v = jnp.concatenate([cells[b : b + 1, :] for b in range(blocks)], axis=1)
            result = result + spread(v, target[pl.ds(p, 1), :], high)
        total[...] = result
        return carry

    lax.fori_loop(0, devices // GROUP, add_group, 0)
    value_ref[...] = total[:high] + total[high:]
    sent = pl.ds(0, devices - 1)
    copy(parts.at[sent], received.at[sent], part_recv.at[0, 0], (lat, lon)).wait_send()


def floats(*shape):
    return jax.ShapeDtypeStruct(shape, jnp.float32)


def spread(v, t, high):
    shape, bf = (high, v.shape[1]), jnp.bfloat16
    flat = (LANES, v.shape[1])
    upper = lax.broadcasted_iota(jnp.int32, shape, 0).astype(bf)
    lower = lax.broadcasted_iota(jnp.int32, flat, 0).astype(bf)
    hit = upper == jnp.broadcast_to((t >> 7).astype(jnp.float32), shape).astype(bf)
    one = lower == jnp.broadcast_to((t & (LANES - 1)).astype(jnp.float32), flat).astype(bf)
    first = v.astype(bf).astype(jnp.float32)
    left = jnp.concatenate(
        [
            jnp.where(hit, jnp.broadcast_to(part, shape).astype(bf), jnp.zeros(shape, bf))
            for part in (first, v - first)
        ],
        axis=0,
    )
    right = jnp.where(one, jnp.ones(flat, bf), jnp.zeros(flat, bf))
    return lax.dot_general(
        left, right, (((1,), (1,)), ((), ())), preferred_element_type=jnp.float32
    )


def per_device(
    control,
    kappa,
    sea_mask,
    vert_coef,
    stencil_offsets,
    stencil_weights,
    slot_target,
    observed,
    inv_error,
):
    levels, fields, rows, cols = control.shape
    layers = levels * fields
    tall = rows + 2 * STEPS
    sten, owners, cap = stencil_offsets.shape
    bundles = sten * owners // LANES
    padded = -(-cap // layers) * layers
    corner = corner_spots()[1] + 2 * PAD
    high = observed.shape[0] // LANES
    blocks = cap // LANES
    members = owners // bundles

    def vmem(*shape, dtype=jnp.float32):
        return pltpu.VMEM(shape, dtype)

    wide = (tall * PITCH, LANES)
    dma = pltpu.SemaphoreType.DMA
    place = (lax.axis_size("lat"), lax.axis_size("lon"))
    shapes = (
        floats(layers * rows, LANES),
        jax.ShapeDtypeStruct((bundles, padded, LANES), jnp.int32),
        floats(bundles, padded, LANES),
    )
    arrays = (
        control.reshape(layers * rows, cols),
        kappa,
        sea_mask,
        vert_coef.reshape(levels * rows, cols),
        stencil_offsets.reshape(sten * owners, cap),
        stencil_weights.reshape(sten * owners, cap),
    )
    increment, off_t, w_t = pl.pallas_call(
        functools.partial(field_kernel, *place, rows, layers),
        out_shape=shapes,
        in_specs=[pl.BlockSpec(memory_space=pltpu.HBM)] * len(arrays),
        out_specs=tuple(pl.BlockSpec(memory_space=pltpu.VMEM) for _ in shapes),
        scratch_shapes=[
            vmem(layers * rows, LANES),
            vmem(rows, LANES),
            vmem(rows, LANES, dtype=jnp.int32),
            vmem(levels * rows, LANES),
            vmem(blocks, sten * owners, LANES, dtype=jnp.int32),
            vmem(blocks, sten * owners, LANES),
            vmem(levels * rows, LANES),
            vmem(levels * rows, LANES),
            vmem(3, 3 * rows, LANES),
            vmem(2, 3, 40, LANES),
            vmem(rows * layers, LANES),
            vmem(2, STEPS * layers, LANES),
            vmem(2, rows * STEPS + 2 * PAD, LANES),
            vmem(2, rows * STEPS + 2 * PAD, LANES),
            vmem(4, corner, LANES),
            vmem(4, corner, LANES),
            vmem(2, message(*side_split(rows)), LANES),
            vmem(2, message(*side_split(rows)), LANES),
            vmem(4, message(*corner_split()), LANES),
            vmem(4, message(*corner_split()), LANES),
            vmem(*wide),
            vmem(*wide),
            vmem(*wide),
            vmem(*wide),
            vmem(rows * LANES, LANES),
            dma((4 + 2 * blocks,)),
            dma((len(WAYS),)),
            dma((len(WAYS),)),
            dma((2 * len(WAYS),)),
            dma((2 * len(WAYS),)),
        ],
        compiler_params=pltpu.CompilerParams(
            vmem_limit_bytes=44 * 1024 * 1024, collective_id=2, has_side_effects=True
        ),
        name="field",
    )(*[pltpu.with_memory_space_constraint(a, pltpu.HBM) for a in arrays])
    vm = pl.BlockSpec(memory_space=pltpu.VMEM)
    value = pl.pallas_call(
        functools.partial(observe_kernel, *place, rows, layers),
        out_shape=floats(high, LANES),
        in_specs=[vm, vm, vm, pl.BlockSpec(memory_space=pltpu.HBM)],
        out_specs=vm,
        scratch_shapes=[
            vmem(owners, cap, dtype=jnp.int32),
            vmem(padded, LANES),
            vmem(owners, blocks, LANES),
            vmem(owners, blocks, LANES),
            vmem(2 * high, LANES),
            dma((1,)),
            dma((1,)),
            dma((bundles, members // GROUP)),
        ],
        compiler_params=pltpu.CompilerParams(
            vmem_limit_bytes=24 * 1024 * 1024, collective_id=3, has_side_effects=True
        ),
        name="observe",
    )(increment, off_t, w_t, pltpu.with_memory_space_constraint(slot_target, pltpu.HBM))
    return increment.reshape(control.shape), (value.reshape(-1) - observed) * inv_error


def solution(mesh):
    return jax.shard_map(
        per_device,
        mesh=mesh,
        in_specs=(
            P(None, None, "lat", "lon"),
            P("lat", "lon"),
            P("lat", "lon"),
            P(None, "lat", "lon"),
            P(None, ("lat", "lon"), None),
            P(None, ("lat", "lon"), None),
            P(("lat", "lon"), None),
            P(("lat", "lon")),
            P(("lat", "lon")),
        ),
        out_specs=(P(None, None, "lat", "lon"), P(("lat", "lon"))),
        check_vma=False,
    )
```

```python
import functools

import jax
import jax.numpy as jnp
from jax import lax
from jax.experimental import pallas as pl
from jax.experimental.pallas import tpu as pltpu
from jax.sharding import PartitionSpec as P

STEPS = 10
LANES = 128
SUB = 8


GROUP = 16
WAYS = ((-1, 0), (1, 0), (0, -1), (0, 1), (-1, -1), (-1, 1), (1, -1), (1, 1))
PAD = 16
PITCH = LANES + 2 * PAD


def aligned(start, size):
    return pl.ds(pl.multiple_of(start, SUB), size)


def corner_spots():
    spots, at = [], 0
    for d in range(1, STEPS):
        spots.append((d, at, STEPS - d))
        at += STEPS - d
    return spots, -(-at // SUB) * SUB


def corner_split():
    count = STEPS * (STEPS - 1) // 2
    return count - count // 3, count // 3


def side_split(rows):
    return (rows - rows // 3) * STEPS, rows // 3 * STEPS


def message(kept, few):
    return max(-(-kept // SUB), -(-few // SUB) + -(-few // SUB)) * SUB


def update(old, new, c0, k2, count, first, low, high, per):
    def some_rows(turn, carry):
        base = (first + per * turn) * PITCH
        for v in range(low, high):
            spot = [aligned(base + d * PITCH + v * SUB, SUB) for d in range(-1, per + 1)]
            cells = [old[s, :] for s in spot]
            for d in range(per):
                at = base + d * PITCH + v * SUB
                side = old[pl.ds(at - 1, SUB), :] + old[pl.ds(at + 1, SUB), :]
                around = (cells[d] + cells[d + 2]) + side
                new[spot[d + 1], :] = c0[spot[d + 1], :] * cells[d + 1] + k2[spot[d + 1], :] * around
        return carry

    lax.fori_loop(0, count, some_rows, 0)


def span(old, new, c0, k2, first, count, low, high):
    per = 5 if count % 10 == 0 and count < 20 else 6
    update(old, new, c0, k2, count // per, first, low, high, per)
    if count % per:
        update(old, new, c0, k2, 1, first + count // per * per, low, high, count % per)


def diffuse_inner(rows, old, new, c0, k2):
    width = PITCH // SUB
    span(old, new, c0, k2, STEPS + 1, rows - 2, 0, width)
    span(new, old, c0, k2, STEPS + 2, rows - 4, 1, width - 1)


def diffuse_rest(rows, old, new, c0, k2):
    tall = rows + 2 * STEPS
    width = PITCH // SUB
    for first in (1, STEPS + rows - 1):
        span(old, new, c0, k2, first, STEPS, 0, width)
    for first in (2, STEPS + rows - 2):
        span(new, old, c0, k2, first, STEPS, 1, width - 1)

    for s in range(2, STEPS):
        edge = 1 if s < STEPS - 1 else PAD // SUB
        span(old, new, c0, k2, s + 1, tall - 2 - 2 * s, edge, width - edge)
        old, new = new, old


def factor(rows, vert, inverse, ratio):
    levels = vert.shape[0] // rows
    above = vert[pl.ds(0, rows), :]
    cprev = jnp.zeros((rows, LANES), jnp.float32)
    for k in range(levels):
        if k + 1 < levels:
            below = vert[pl.ds((k + 1) * rows, rows), :]
        else:
            below = jnp.zeros((rows, LANES), jnp.float32)
        inv = 1.0 / (((1.0 + above) + below) + above * cprev)
        cprev = -below * inv
        inverse[pl.ds(k * rows, rows), :] = inv
        ratio[pl.ds(k * rows, rows), :] = cprev
        above = below


def solve_columns(rows, layers, done, control, coef, vert, inverse, ratio, inc_ref):
    levels = vert.shape[0] // rows
    fields = layers // levels
    for h in range(rows // SUB):
        here = coef[pl.ds(rows + h * SUB, SUB), :]
        sea = here != 0.0
        back = 1.0 / jnp.where(sea, here, 1.0)
        prev = [jnp.zeros((SUB, LANES), jnp.float32)] * fields
        for k in range(levels):
            level = pl.ds(k * rows + h * SUB, SUB)
            above, inv = vert[level, :], inverse[level, :]
            for f in range(fields):
                layer = k * fields + f
                at = pl.ds(layer * rows + h * SUB, SUB)
                right = done[pl.ds(h * SUB * LANES + layer, SUB, stride=LANES), :] * back
                right = jnp.where(sea, right, control[at, :])
                prev[f] = (right + above * prev[f]) * inv
                inc_ref[at, :] = prev[f]
        for k in range(levels - 2, -1, -1):
            fall = ratio[pl.ds(k * rows + h * SUB, SUB), :]
            for f in range(fields):
                at = pl.ds((k * fields + f) * rows + h * SUB, SUB)
                prev[f] = inc_ref[at, :] - fall * prev[f]
                inc_ref[at, :] = prev[f]


def weigh(rows, coefs, held):
    lane = lax.broadcasted_iota(jnp.int32, (40, LANES), 1)
    mid = pl.ds(rows - STEPS + 1, 40)
    up = pl.ds(rows - STEPS, 40)
    down = pl.ds(rows - STEPS + 2, 40)
    here = [coefs[k, mid, :] for k in range(3)]
    right = [pltpu.roll(c, 1, 1) for c in here]
    left = [pltpu.roll(c, LANES - 1, 1) for c in here]
    first, last = lane == 0, lane == LANES - 1
    wests = [right[0], jnp.where(first, right[0], right[1]), jnp.where(first, right[1], right[2])]
    easts = [jnp.where(last, left[1], left[0]), jnp.where(last, left[2], left[1]), left[2]]
    for k in range(3):
        around = (coefs[k, up, :] + coefs[k, down, :]) + (wests[k] + easts[k])
        held[0, k, :, :] = 1.0 - here[k] * around
        held[1, k, :, :] = here[k] * here[k]


def broaden(rows, held, kind, out):
    lane = lax.broadcasted_iota(jnp.int32, (40, LANES), 1)
    rest = jnp.zeros((LANES - 40, LANES), jnp.float32)
    main = jnp.concatenate([held[kind, 1, :, :], rest], axis=0).T
    outer = jnp.where(lane >= LANES - PAD, held[kind, 0, :, :], held[kind, 2, :, :])
    outer = jnp.concatenate([outer, rest], axis=0).T
    for j in range(rows + 2 * STEPS - 2):
        base = (j + 1) * PITCH
        column = outer[:, j : j + 1]
        out[pl.ds(base, PAD), :] = jnp.broadcast_to(column[LANES - PAD :], (PAD, LANES))
        out[pl.ds(base + PAD, LANES), :] = jnp.broadcast_to(main[:, j : j + 1], (LANES, LANES))
        out[pl.ds(base + PAD + LANES, PAD), :] = jnp.broadcast_to(column[:PAD], (PAD, LANES))


def turn(n_lat, n_lon, off, weight, off_t, w_t):
    blocks, height, _ = off.shape
    cap, padded = blocks * LANES, off_t.shape[1]
    width = n_lon // off_t.shape[0]
    ways = SUB // width
    row = lax.broadcasted_iota(jnp.int32, (SUB, LANES), 0) // width

    def gather(src, c, g):
        tiles = []
        for start in range(0, height, n_lon * ways):
            tile = src[c, pl.ds(start + g * width, SUB), :]
            for k in range(1, ways):
                piece = src[c, pl.ds(start + k * n_lon + g * width - k * width, SUB), :]
                tile = jnp.where(row == k, piece, tile)
            tiles.append(tile)
        return jnp.concatenate(tiles, axis=0).T

    for g in range(off_t.shape[0]):
        if padded > cap:
            off_t[g, cap:padded, :] = jnp.zeros((padded - cap, LANES), jnp.int32)
            w_t[g, cap:padded, :] = jnp.zeros((padded - cap, LANES), jnp.float32)
        for c in range(blocks):
            off_t[g, pl.ds(c * LANES, LANES), :] = gather(off, c, g)
            w_t[g, pl.ds(c * LANES, LANES), :] = gather(weight, c, g)


def squeeze(layers, kept, few, src, dst):
    spare = LANES - layers
    size = -(-few // SUB) * SUB
    whole = dst.shape[0]
    lane = lax.broadcasted_iota(jnp.int32, (size, LANES), 1)
    dst[...] = src[pl.ds(0, whole), :]
    rest = src[pl.ds(kept, size), :]
    dst[pl.ds(0, size), :] = jnp.where(lane < layers, src[pl.ds(0, size), :], rest)
    moved = pltpu.roll(rest, layers - spare, 1)
    dst[pl.ds(few, size), :] = jnp.where(lane < layers, src[pl.ds(few, size), :], moved)


def unsqueeze(layers, kept, few, src, dst):
    spare = LANES - layers
    size = -(-few // SUB) * SUB
    lane = lax.broadcasted_iota(jnp.int32, (size, LANES), 1)
    dst[pl.ds(PAD, src.shape[0]), :] = src[...]
    first = pltpu.roll(src[pl.ds(0, size), :], spare, 1)
    second = pltpu.roll(src[pl.ds(few, size), :], LANES - layers + spare, 1)
    dst[pl.ds(PAD + kept, size), :] = jnp.where(lane < spare, first, second)


def field_kernel(
    n_lat,
    n_lon,
    rows,
    layers,
    control_ref,
    kappa_ref,
    mask_ref,
    vert_ref,
    off_ref,
    w_ref,
    inc_ref,
    off_t,
    w_t,
    control,
    kappa,
    mask,
    vert,
    off,
    weight,
    inverse,
    ratio,
    coefs,
    held,
    laid,
    far_rows,
    side_out,
    side_in,
    corner_out,
    corner_in,
    side_sent,
    side_got,
    corner_sent,
    corner_got,
    near,
    far,
    c0,
    k2,
    done,
    load_sem,
    coef_send,
    coef_recv,
    send_sem,
    recv_sem,
):
    lat, lon = lax.axis_index("lat"), lax.axis_index("lon")
    tall = rows + 2 * STEPS
    pairs = ((control_ref, control), (kappa_ref, kappa), (mask_ref, mask))
    pairs += ((vert_ref, vert),)
    for c in range(off.shape[0]):
        here = pl.ds(c * LANES, LANES)
        pairs += ((off_ref.at[:, here], off.at[c]), (w_ref.at[:, here], weight.at[c]))
    loads = [pltpu.make_async_copy(a, b, load_sem.at[i]) for i, (a, b) in enumerate(pairs)]
    for i in (1, 2, 0, *range(3, len(loads))):
        loads[i].start()

    def place(i):
        return (lat + WAYS[i][0], lax.rem(lon + WAYS[i][1] + n_lon, n_lon))

    def guard(step, body):
        if step == 0:
            body()
        else:
            pl.when(lat > 0 if step < 0 else lat < n_lat - 1)(body)

    corner_got[...] = jnp.zeros_like(corner_got)
    barrier = pltpu.get_barrier_semaphore()
    for i, way in enumerate(WAYS):
        guard(
            way[0],
            lambda i=i: pl.semaphore_signal(
                barrier, inc=1, device_id=place(i), device_id_type=pl.DeviceIdType.MESH
            ),
        )

    side_in[...] = jnp.zeros_like(side_in)
    corner_in[...] = jnp.zeros_like(corner_in)

    @pl.when(lat == 0)
    def _():
        coefs[:, :rows, :] = jnp.zeros((3, rows, LANES), jnp.float32)
        far_rows[1] = jnp.zeros((STEPS * layers, LANES), jnp.float32)

    @pl.when(lat == n_lat - 1)
    def _():
        coefs[:, 2 * rows :, :] = jnp.zeros((3, rows, LANES), jnp.float32)
        far_rows[0] = jnp.zeros((STEPS * layers, LANES), jnp.float32)

    def remote(i, src, dst, out_sem, in_sem, part=0):
        return pltpu.make_async_remote_copy(
            src_ref=src,
            dst_ref=dst,
            send_sem=out_sem.at[i + part * len(WAYS)],
            recv_sem=in_sem.at[i + part * len(WAYS)],
            device_id=place(i),
            device_id_type=pl.DeviceIdType.MESH,
        )

    def coef_copy(i):
        dl, dn = WAYS[i]
        return remote(
            i, coefs.at[1, pl.ds(rows, rows)], coefs.at[1 - dn, pl.ds((1 - dl) * rows, rows)], coef_send, coef_recv
        )

    spots = corner_spots()[0]

    half = STEPS // 2 * layers

    def field_copy(i, part=0):
        dl, dn = WAYS[i]
        if dn == 0:
            start = 0 if dl < 0 else (rows - STEPS) * layers
            src = laid.at[pl.ds(start + part * half, half)]
            dst = far_rows.at[i, pl.ds(part * half, half)]
        elif dl == 0:
            src, dst = side_sent.at[i - 2], side_got.at[i - 2]
        else:
            src, dst = corner_sent.at[i - 4], corner_got.at[i - 4]
        return remote(i, src, dst, send_sem, recv_sem, part)

    loads[1].wait()
    loads[2].wait()
    coefs[1, pl.ds(rows, rows), :] = kappa[...] * mask[...].astype(jnp.float32)
    loads[0].wait()
    for r in range(rows):
        here = coefs[1, pl.ds(rows + r, 1), :]
        for g in range(layers // SUB):
            laid[pl.ds(r * layers + g * SUB, SUB), :] = (
                control[pl.ds(g * SUB * rows + r, SUB, stride=rows), :] * here
            )
    def upright(block):
        return jnp.concatenate([block, block[: LANES - layers]], axis=0).T

    def main_row(r, carry):
        block = laid[aligned(r * layers, layers), :]
        near[aligned((r + STEPS) * PITCH + PAD, LANES), :] = upright(block)
        return carry

    lax.fori_loop(0, rows, main_row, 0, unroll=8)
    for k, first in ((0, PAD), (1, PAD + LANES - STEPS)):
        for r in range(rows):
            side_out[k, pl.ds(r * STEPS, PAD), :] = near[
                pl.ds((r + STEPS) * PITCH + first, PAD), :
            ]
        squeeze(layers, *side_split(rows), side_out.at[k], side_sent.at[k])
    for i in range(4, 8):
        dl, dn = WAYS[i]
        for d, at, count in spots:
            r = d - 1 if dl < 0 else rows - d
            first = PAD if dn < 0 else PAD + LANES - count
            corner_out[i - 4, pl.ds(at, PAD), :] = near[pl.ds((r + STEPS) * PITCH + first, PAD), :]
        squeeze(layers, *corner_split(), corner_out.at[i - 4], corner_sent.at[i - 4])
    beside = (lat > 0).astype(jnp.int32) + (lat < n_lat - 1).astype(jnp.int32)
    pl.semaphore_wait(barrier, 2 + 3 * beside)
    for i, way in enumerate(WAYS):
        guard(way[0], lambda i=i: coef_copy(i).start())
    for i in (2, 3, 0, 1, 4, 5, 6, 7):
        guard(WAYS[i][0], lambda i=i: field_copy(i).start())
    for i in (0, 1):
        guard(WAYS[i][0], lambda i=i: field_copy(i, 1).start())

    for i in range(3, len(loads)):
        loads[i].wait()
    turn(n_lat, n_lon, off, weight, off_t, w_t)
    factor(rows, vert, inverse, ratio)
    for i, way in enumerate(WAYS):
        guard(-way[0], lambda i=i: coef_copy(i).wait_recv())
    weigh(rows, coefs, held)
    broaden(rows, held, 0, c0)
    broaden(rows, held, 1, k2)

    for i in (2, 3):
        field_copy(i).wait_recv()
        unsqueeze(layers, *side_split(rows), side_got.at[i - 2], side_in.at[i - 2])
        for r in range(rows):
            base = (r + STEPS) * PITCH
            if i == 3:
                near[pl.ds(base, PAD), :] = side_in[1, pl.ds((r + 1) * STEPS, PAD), :]
            else:
                near[pl.ds(base + PAD + LANES, PAD), :] = side_in[0, pl.ds(PAD + r * STEPS, PAD), :]
    for i in range(4, 8):
        dl, dn = WAYS[i]
        guard(-dl, lambda i=i: field_copy(i).wait_recv())
        unsqueeze(layers, *corner_split(), corner_got.at[i - 4], corner_in.at[i - 4])
        for d in range(1, STEPS + 1):
            at, count = spots[d - 1][1:] if d < STEPS else (0, 0)
            r = STEPS + rows + d - 1 if dl < 0 else STEPS - d
            if dn > 0:
                near[pl.ds(r * PITCH, PAD), :] = corner_in[i - 4, pl.ds(at + count, PAD), :]
            else:
                near[pl.ds(r * PITCH + PAD + LANES, PAD), :] = corner_in[i - 4, pl.ds(PAD + at, PAD), :]

    diffuse_inner(rows, near, far, c0, k2)
    for part in (0, 1):
        for i in (0, 1):
            guard(-WAYS[i][0], lambda i=i, part=part: field_copy(i, part).wait_recv())
            start = (STEPS + rows) if i == 0 else 0

            def far_row(r, carry, i=i, start=start):
                block = far_rows[i, aligned(r * layers, layers), :]
                near[aligned((r + start) * PITCH + PAD, LANES), :] = upright(block)
                return carry

            first = part * (STEPS // 2)
            lax.fori_loop(first, first + STEPS // 2, far_row, 0, unroll=True)

    diffuse_rest(rows, near, far, c0, k2)

    def back_row(r, carry):
        done[aligned(r * LANES, LANES), :] = near[aligned((r + STEPS) * PITCH + PAD, LANES), :].T
        return carry

    lax.fori_loop(0, rows, back_row, 0, unroll=8)
    solve_columns(rows, layers, done, control, coefs.at[1], vert, inverse, ratio, inc_ref)
    for i, way in enumerate(WAYS):
        guard(way[0], lambda i=i: coef_copy(i).wait_send())
        guard(way[0], lambda i=i: field_copy(i).wait_send())
        if way[1] == 0:
            guard(way[0], lambda i=i: field_copy(i, 1).wait_send())


def pick(table, row, col):
    level = [jnp.take_along_axis(t, col, axis=1) for t in table]
    bit = 1
    while len(level) > 1:
        odd = (row & bit) != 0
        level = [jnp.where(odd, level[i + 1], level[i]) for i in range(0, len(level), 2)]
        bit *= 2
    return level[0]


def lookup(rows, layers, turns, inc_ref, off_t, w_t, acc):
    def one_group(lg, carry):
        base = pl.multiple_of(lg * SUB, SUB)
        table = [inc_ref[pl.ds(base * rows + r, SUB, stride=rows), :] for r in range(rows)]
        for m in range(turns):
            at = pl.ds(m * layers + base, SUB)
            idx = off_t[at, :]
            acc[at, :] = pick(table, idx >> 7, idx & (LANES - 1)) * w_t[at, :]
        return carry

    lax.fori_loop(0, layers // SUB, one_group, 0, unroll=5)


def observe_kernel(
    n_lat,
    n_lon,
    rows,
    layers,
    inc_ref,
    off_t,
    w_t,
    target_ref,
    value_ref,
    target,
    acc,
    parts,
    received,
    total,
    load_sem,
    part_send,
    part_recv,
):
    lat, lon = lax.axis_index("lat"), lax.axis_index("lon")
    me, devices = lat * n_lon + lon, n_lat * n_lon
    passes, padded = off_t.shape[0], off_t.shape[1]
    members, width = devices // passes, n_lon // passes
    mine, local = lon // width, lat * width + lon % width
    blocks, high = parts.shape[1], value_ref.shape[0]
    load = pltpu.make_async_copy(target_ref, target, load_sem.at[0])
    load.start()
    barrier = pltpu.get_barrier_semaphore()

    def greet(k, carry):
        q = lax.rem(me + k, devices)
        pl.semaphore_signal(
            barrier, inc=1, device_id=(q // n_lon, q % n_lon), device_id_type=pl.DeviceIdType.MESH
        )
        return carry

    lax.fori_loop(1, devices, greet, 0, unroll=True)

    def toward(t):
        return lax.rem(mine + t + 1, passes)

    def slots(t, i, count=1):
        return pl.ds(t * members + i, count)

    def copy(src, dst, in_sem, there):
        return pltpu.make_async_remote_copy(
            src_ref=src,
            dst_ref=dst,
            send_sem=part_send.at[0],
            recv_sem=in_sem,
            device_id=there,
            device_id_type=pl.DeviceIdType.MESH,
        )

    def part_copy(t, i):
        there = lax.rem(local + i, members)
        place = (there // width, toward(t) * width + there % width)
        src, dst = parts.at[slots(t, there)], received.at[slots(t, i)]
        return copy(src, dst, part_recv.at[t, i // GROUP], place)

    def wait_group(t, g, first, count):
        here = slots(t, g * GROUP + first, count)
        copy(parts.at[here], received.at[here], part_recv.at[t, g], (lat, lon)).wait_recv()

    def look_up(t, carry):
        lookup(rows, layers, padded // layers, inc_ref, off_t.at[toward(t)], w_t.at[toward(t)], acc)
        for b in range(blocks):
            block = acc[pl.ds(b * LANES, LANES), :].T
            part = block[:members]
            for k in range(1, LANES // members):
                part = part + block[k * members : (k + 1) * members]
            parts[slots(t, 0, members), b, :] = part

        @pl.when(t == 0)
        def _():
            pl.semaphore_wait(barrier, devices - 1)

        def send(i, carry):
            part_copy(t, i).start()
            return carry

        lax.fori_loop((t == passes - 1).astype(jnp.int32), members, send, 0)
        return carry

    total[...] = jnp.zeros_like(total)
    lax.fori_loop(0, passes, look_up, 0)
    received[slots(passes - 1, 0)] = parts[slots(passes - 1, local)]
    load.wait()

    def add_group(turn, carry):
        t, g = turn // (members // GROUP), turn % (members // GROUP)
        result = total[...]
        source = lax.rem(mine + passes - t - 1, passes) * width
        own = jnp.logical_and(t == passes - 1, g == 0)
        pl.when(own)(lambda: wait_group(t, g, 1, GROUP - 1))
        pl.when(jnp.logical_not(own))(lambda: wait_group(t, g, 0, GROUP))
        for k in range(GROUP):
            i = g * GROUP + k
            p = lax.rem(local - i + members, members)
            p = p // width * n_lon + source + p % width
            cells = received[t * members + i]
            v = jnp.concatenate([cells[b : b + 1, :] for b in range(blocks)], axis=1)
            result = result + spread(v, target[pl.ds(p, 1), :], high)
        total[...] = result
        return carry

    lax.fori_loop(0, devices // GROUP, add_group, 0)
    value_ref[...] = total[:high] + total[high:]
    sent = pl.ds(0, devices - 1)
    copy(parts.at[sent], received.at[sent], part_recv.at[0, 0], (lat, lon)).wait_send()


def floats(*shape):
    return jax.ShapeDtypeStruct(shape, jnp.float32)


def spread(v, t, high):
    shape, bf = (high, v.shape[1]), jnp.bfloat16
    flat = (LANES, v.shape[1])
    upper = lax.broadcasted_iota(jnp.int32, shape, 0).astype(bf)
    lower = lax.broadcasted_iota(jnp.int32, flat, 0).astype(bf)
    hit = upper == jnp.broadcast_to((t >> 7).astype(jnp.float32), shape).astype(bf)
    one = lower == jnp.broadcast_to((t & (LANES - 1)).astype(jnp.float32), flat).astype(bf)
    first = v.astype(bf).astype(jnp.float32)
    left = jnp.concatenate(
        [
            jnp.where(hit, jnp.broadcast_to(part, shape).astype(bf), jnp.zeros(shape, bf))
            for part in (first, v - first)
        ],
        axis=0,
    )
    right = jnp.where(one, jnp.ones(flat, bf), jnp.zeros(flat, bf))
    return lax.dot_general(
        left, right, (((1,), (1,)), ((), ())), preferred_element_type=jnp.float32
    )


def per_device(
    control,
    kappa,
    sea_mask,
    vert_coef,
    stencil_offsets,
    stencil_weights,
    slot_target,
    observed,
    inv_error,
):
    levels, fields, rows, cols = control.shape
    layers = levels * fields
    tall = rows + 2 * STEPS
    sten, owners, cap = stencil_offsets.shape
    bundles = sten * owners // LANES
    padded = -(-cap // layers) * layers
    corner = corner_spots()[1] + 2 * PAD
    high = observed.shape[0] // LANES
    blocks = cap // LANES
    members = owners // bundles

    def vmem(*shape, dtype=jnp.float32):
        return pltpu.VMEM(shape, dtype)

    wide = (tall * PITCH, LANES)
    dma = pltpu.SemaphoreType.DMA
    place = (lax.axis_size("lat"), lax.axis_size("lon"))
    shapes = (
        floats(layers * rows, LANES),
        jax.ShapeDtypeStruct((bundles, padded, LANES), jnp.int32),
        floats(bundles, padded, LANES),
    )
    arrays = (
        control.reshape(layers * rows, cols),
        kappa,
        sea_mask,
        vert_coef.reshape(levels * rows, cols),
        stencil_offsets.reshape(sten * owners, cap),
        stencil_weights.reshape(sten * owners, cap),
    )
    increment, off_t, w_t = pl.pallas_call(
        functools.partial(field_kernel, *place, rows, layers),
        out_shape=shapes,
        in_specs=[pl.BlockSpec(memory_space=pltpu.HBM)] * len(arrays),
        out_specs=tuple(pl.BlockSpec(memory_space=pltpu.VMEM) for _ in shapes),
        scratch_shapes=[
            vmem(layers * rows, LANES),
            vmem(rows, LANES),
            vmem(rows, LANES, dtype=jnp.int32),
            vmem(levels * rows, LANES),
            vmem(blocks, sten * owners, LANES, dtype=jnp.int32),
            vmem(blocks, sten * owners, LANES),
            vmem(levels * rows, LANES),
            vmem(levels * rows, LANES),
            vmem(3, 3 * rows, LANES),
            vmem(2, 3, 40, LANES),
            vmem(rows * layers, LANES),
            vmem(2, STEPS * layers, LANES),
            vmem(2, rows * STEPS + 2 * PAD, LANES),
            vmem(2, rows * STEPS + 2 * PAD, LANES),
            vmem(4, corner, LANES),
            vmem(4, corner, LANES),
            vmem(2, message(*side_split(rows)), LANES),
            vmem(2, message(*side_split(rows)), LANES),
            vmem(4, message(*corner_split()), LANES),
            vmem(4, message(*corner_split()), LANES),
            vmem(*wide),
            vmem(*wide),
            vmem(*wide),
            vmem(*wide),
            vmem(rows * LANES, LANES),
            dma((4 + 2 * blocks,)),
            dma((len(WAYS),)),
            dma((len(WAYS),)),
            dma((2 * len(WAYS),)),
            dma((2 * len(WAYS),)),
        ],
        compiler_params=pltpu.CompilerParams(
            vmem_limit_bytes=44 * 1024 * 1024, collective_id=2, has_side_effects=True
        ),
        name="field",
    )(*[pltpu.with_memory_space_constraint(a, pltpu.HBM) for a in arrays])
    vm = pl.BlockSpec(memory_space=pltpu.VMEM)
    value = pl.pallas_call(
        functools.partial(observe_kernel, *place, rows, layers),
        out_shape=floats(high, LANES),
        in_specs=[vm, vm, vm, pl.BlockSpec(memory_space=pltpu.HBM)],
        out_specs=vm,
        scratch_shapes=[
            vmem(owners, cap, dtype=jnp.int32),
            vmem(padded, LANES),
            vmem(owners, blocks, LANES),
            vmem(owners, blocks, LANES),
            vmem(2 * high, LANES),
            dma((1,)),
            dma((1,)),
            dma((bundles, members // GROUP)),
        ],
        compiler_params=pltpu.CompilerParams(
            vmem_limit_bytes=24 * 1024 * 1024, collective_id=3, has_side_effects=True
        ),
        name="observe",
    )(increment, off_t, w_t, pltpu.with_memory_space_constraint(slot_target, pltpu.HBM))
    return increment.reshape(control.shape), (value.reshape(-1) - observed) * inv_error


def solution(mesh):
    return jax.shard_map(
        per_device,
        mesh=mesh,
        in_specs=(
            P(None, None, "lat", "lon"),
            P("lat", "lon"),
            P("lat", "lon"),
            P(None, "lat", "lon"),
            P(None, ("lat", "lon"), None),
            P(None, ("lat", "lon"), None),
            P(("lat", "lon"), None),
            P(("lat", "lon")),
            P(("lat", "lon")),
        ),
        out_specs=(P(None, None, "lat", "lon"), P(("lat", "lon"))),
        check_vma=False,
    )
```

```python
import functools

import jax
import jax.numpy as jnp
from jax import lax
from jax.experimental import pallas as pl
from jax.experimental.pallas import tpu as pltpu
from jax.sharding import PartitionSpec as P

STEPS = 10
LANES = 128
SUB = 8


GROUP = 16
WAYS = ((-1, 0), (1, 0), (0, -1), (0, 1), (-1, -1), (-1, 1), (1, -1), (1, 1))
PAD = 16
PITCH = LANES + 2 * PAD


def aligned(start, size):
    return pl.ds(pl.multiple_of(start, SUB), size)


def corner_spots():
    spots, at = [], 0
    for d in range(1, STEPS):
        spots.append((d, at, STEPS - d))
        at += STEPS - d
    return spots, -(-at // SUB) * SUB


def corner_split():
    count = STEPS * (STEPS - 1) // 2
    return count - count // 3, count // 3


def side_split(rows):
    return (rows - rows // 3) * STEPS, rows // 3 * STEPS


def message(kept, few):
    return max(-(-kept // SUB), -(-few // SUB) + -(-few // SUB)) * SUB


def update(old, new, c0, k2, count, first, low, high, per):
    def some_rows(turn, carry):
        base = (first + per * turn) * PITCH
        for v in range(low, high):
            spot = [aligned(base + d * PITCH + v * SUB, SUB) for d in range(-1, per + 1)]
            cells = [old[s, :] for s in spot]
            for d in range(per):
                at = base + d * PITCH + v * SUB
                side = old[pl.ds(at - 1, SUB), :] + old[pl.ds(at + 1, SUB), :]
                around = (cells[d] + cells[d + 2]) + side
                new[spot[d + 1], :] = c0[spot[d + 1], :] * cells[d + 1] + k2[spot[d + 1], :] * around
        return carry

    lax.fori_loop(0, count, some_rows, 0)


def span(old, new, c0, k2, first, count, low, high):
    per = 5 if count % 10 == 0 and count < 20 else 6
    update(old, new, c0, k2, count // per, first, low, high, per)
    if count % per:
        update(old, new, c0, k2, 1, first + count // per * per, low, high, count % per)


def diffuse_inner(rows, old, new, c0, k2):
    width = PITCH // SUB
    span(old, new, c0, k2, STEPS + 1, rows - 2, 0, width)
    span(new, old, c0, k2, STEPS + 2, rows - 4, 1, width - 1)


def diffuse_rest(rows, old, new, c0, k2):
    tall = rows + 2 * STEPS
    width = PITCH // SUB
    for first in (1, STEPS + rows - 1):
        span(old, new, c0, k2, first, STEPS, 0, width)
    for first in (2, STEPS + rows - 2):
        span(new, old, c0, k2, first, STEPS, 1, width - 1)

    for s in range(2, STEPS):
        edge = 1 if s < STEPS - 1 else PAD // SUB
        span(old, new, c0, k2, s + 1, tall - 2 - 2 * s, edge, width - edge)
        old, new = new, old


def factor(rows, vert, inverse, ratio):
    levels = vert.shape[0] // rows
    above = vert[pl.ds(0, rows), :]
    cprev = jnp.zeros((rows, LANES), jnp.float32)
    for k in range(levels):
        if k + 1 < levels:
            below = vert[pl.ds((k + 1) * rows, rows), :]
        else:
            below = jnp.zeros((rows, LANES), jnp.float32)
        inv = 1.0 / (((1.0 + above) + below) + above * cprev)
        cprev = -below * inv
        inverse[pl.ds(k * rows, rows), :] = inv
        ratio[pl.ds(k * rows, rows), :] = cprev
        above = below


def solve_columns(rows, layers, done, control, coef, vert, inverse, ratio, inc_ref):
    levels = vert.shape[0] // rows
    fields = layers // levels
    for h in range(rows // SUB):
        here = coef[pl.ds(rows + h * SUB, SUB), :]
        sea = here != 0.0
        back = 1.0 / jnp.where(sea, here, 1.0)
        prev = [jnp.zeros((SUB, LANES), jnp.float32)] * fields
        for k in range(levels):
            level = pl.ds(k * rows + h * SUB, SUB)
            above, inv = vert[level, :], inverse[level, :]
            for f in range(fields):
                layer = k * fields + f
                at = pl.ds(layer * rows + h * SUB, SUB)
                right = done[pl.ds(h * SUB * LANES + layer, SUB, stride=LANES), :] * back
                right = jnp.where(sea, right, control[at, :])
                prev[f] = (right + above * prev[f]) * inv
                inc_ref[at, :] = prev[f]
        for k in range(levels - 2, -1, -1):
            fall = ratio[pl.ds(k * rows + h * SUB, SUB), :]
            for f in range(fields):
                at = pl.ds((k * fields + f) * rows + h * SUB, SUB)
                prev[f] = inc_ref[at, :] - fall * prev[f]
                inc_ref[at, :] = prev[f]


def weigh(rows, coefs, held):
    lane = lax.broadcasted_iota(jnp.int32, (40, LANES), 1)
    mid = pl.ds(rows - STEPS + 1, 40)
    up = pl.ds(rows - STEPS, 40)
    down = pl.ds(rows - STEPS + 2, 40)
    here = [coefs[k, mid, :] for k in range(3)]
    right = [pltpu.roll(c, 1, 1) for c in here]
    left = [pltpu.roll(c, LANES - 1, 1) for c in here]
    first, last = lane == 0, lane == LANES - 1
    wests = [right[0], jnp.where(first, right[0], right[1]), jnp.where(first, right[1], right[2])]
    easts = [jnp.where(last, left[1], left[0]), jnp.where(last, left[2], left[1]), left[2]]
    for k in range(3):
        around = (coefs[k, up, :] + coefs[k, down, :]) + (wests[k] + easts[k])
        held[0, k, :, :] = 1.0 - here[k] * around
        held[1, k, :, :] = here[k] * here[k]


def broaden(rows, held, kind, out):
    lane = lax.broadcasted_iota(jnp.int32, (40, LANES), 1)
    rest = jnp.zeros((LANES - 40, LANES), jnp.float32)
    main = jnp.concatenate([held[kind, 1, :, :], rest], axis=0).T
    outer = jnp.where(lane >= LANES - PAD, held[kind, 0, :, :], held[kind, 2, :, :])
    outer = jnp.concatenate([outer, rest], axis=0).T
    for j in range(rows + 2 * STEPS - 2):
        base = (j + 1) * PITCH
        column = outer[:, j : j + 1]
        out[pl.ds(base, PAD), :] = jnp.broadcast_to(column[LANES - PAD :], (PAD, LANES))
        out[pl.ds(base + PAD, LANES), :] = jnp.broadcast_to(main[:, j : j + 1], (LANES, LANES))
        out[pl.ds(base + PAD + LANES, PAD), :] = jnp.broadcast_to(column[:PAD], (PAD, LANES))


def turn(n_lat, n_lon, off, weight, off_t, w_t):
    blocks, height, _ = off.shape
    cap, padded = blocks * LANES, off_t.shape[1]
    width = n_lon // off_t.shape[0]
    ways = SUB // width
    row = lax.broadcasted_iota(jnp.int32, (SUB, LANES), 0) // width

    def gather(src, c, g):
        tiles = []
        for start in range(0, height, n_lon * ways):
            tile = src[c, pl.ds(start + g * width, SUB), :]
            for k in range(1, ways):
                piece = src[c, pl.ds(start + k * n_lon + g * width - k * width, SUB), :]
                tile = jnp.where(row == k, piece, tile)
            tiles.append(tile)
        return jnp.concatenate(tiles, axis=0).T

    for g in range(off_t.shape[0]):
        if padded > cap:
            off_t[g, cap:padded, :] = jnp.zeros((padded - cap, LANES), jnp.int32)
            w_t[g, cap:padded, :] = jnp.zeros((padded - cap, LANES), jnp.float32)
        for c in range(blocks):
            off_t[g, pl.ds(c * LANES, LANES), :] = gather(off, c, g)
            w_t[g, pl.ds(c * LANES, LANES), :] = gather(weight, c, g)


def squeeze(layers, kept, few, src, dst):
    spare = LANES - layers
    size = -(-few // SUB) * SUB
    whole = dst.shape[0]
    lane = lax.broadcasted_iota(jnp.int32, (size, LANES), 1)
    dst[...] = src[pl.ds(0, whole), :]
    rest = src[pl.ds(kept, size), :]
    dst[pl.ds(0, size), :] = jnp.where(lane < layers, src[pl.ds(0, size), :], rest)
    moved = pltpu.roll(rest, layers - spare, 1)
    dst[pl.ds(few, size), :] = jnp.where(lane < layers, src[pl.ds(few, size), :], moved)


def unsqueeze(layers, kept, few, src, dst):
    spare = LANES - layers
    size = -(-few // SUB) * SUB
    lane = lax.broadcasted_iota(jnp.int32, (size, LANES), 1)
    dst[pl.ds(PAD, src.shape[0]), :] = src[...]
    first = pltpu.roll(src[pl.ds(0, size), :], spare, 1)
    second = pltpu.roll(src[pl.ds(few, size), :], LANES - layers + spare, 1)
    dst[pl.ds(PAD + kept, size), :] = jnp.where(lane < spare, first, second)


def field_kernel(
    n_lat,
    n_lon,
    rows,
    layers,
    control_ref,
    kappa_ref,
    mask_ref,
    vert_ref,
    off_ref,
    w_ref,
    inc_ref,
    off_t,
    w_t,
    control,
    kappa,
    mask,
    vert,
    off,
    weight,
    inverse,
    ratio,
    coefs,
    held,
    laid,
    far_rows,
    side_out,
    side_in,
    corner_out,
    corner_in,
    side_sent,
    side_got,
    corner_sent,
    corner_got,
    near,
    far,
    c0,
    k2,
    done,
    load_sem,
    coef_send,
    coef_recv,
    send_sem,
    recv_sem,
):
    lat, lon = lax.axis_index("lat"), lax.axis_index("lon")
    tall = rows + 2 * STEPS
    pairs = ((control_ref, control), (kappa_ref, kappa), (mask_ref, mask))
    pairs += ((vert_ref, vert),)
    for c in range(off.shape[0]):
        here = pl.ds(c * LANES, LANES)
        pairs += ((off_ref.at[:, here], off.at[c]), (w_ref.at[:, here], weight.at[c]))
    loads = [pltpu.make_async_copy(a, b, load_sem.at[i]) for i, (a, b) in enumerate(pairs)]
    for i in (1, 2, 0):
        loads[i].start()

    def place(i):
        return (lat + WAYS[i][0], lax.rem(lon + WAYS[i][1] + n_lon, n_lon))

    def guard(step, body):
        if step == 0:
            body()
        else:
            pl.when(lat > 0 if step < 0 else lat < n_lat - 1)(body)

    corner_got[...] = jnp.zeros_like(corner_got)
    barrier = pltpu.get_barrier_semaphore()
    for i, way in enumerate(WAYS):
        guard(
            way[0],
            lambda i=i: pl.semaphore_signal(
                barrier, inc=1, device_id=place(i), device_id_type=pl.DeviceIdType.MESH
            ),
        )

    side_in[...] = jnp.zeros_like(side_in)
    corner_in[...] = jnp.zeros_like(corner_in)

    @pl.when(lat == 0)
    def _():
        coefs[:, :rows, :] = jnp.zeros((3, rows, LANES), jnp.float32)
        far_rows[1] = jnp.zeros((STEPS * layers, LANES), jnp.float32)

    @pl.when(lat == n_lat - 1)
    def _():
        coefs[:, 2 * rows :, :] = jnp.zeros((3, rows, LANES), jnp.float32)
        far_rows[0] = jnp.zeros((STEPS * layers, LANES), jnp.float32)

    def remote(i, src, dst, out_sem, in_sem, part=0):
        return pltpu.make_async_remote_copy(
            src_ref=src,
            dst_ref=dst,
            send_sem=out_sem.at[i + part * len(WAYS)],
            recv_sem=in_sem.at[i + part * len(WAYS)],
            device_id=place(i),
            device_id_type=pl.DeviceIdType.MESH,
        )

    def coef_copy(i):
        dl, dn = WAYS[i]
        return remote(
            i, coefs.at[1, pl.ds(rows, rows)], coefs.at[1 - dn, pl.ds((1 - dl) * rows, rows)], coef_send, coef_recv
        )

    spots = corner_spots()[0]

    half = STEPS // 2 * layers

    def field_copy(i, part=0):
        dl, dn = WAYS[i]
        if dn == 0:
            start = 0 if dl < 0 else (rows - STEPS) * layers
            src = laid.at[pl.ds(start + part * half, half)]
            dst = far_rows.at[i, pl.ds(part * half, half)]
        elif dl == 0:
            src, dst = side_sent.at[i - 2], side_got.at[i - 2]
        else:
            src, dst = corner_sent.at[i - 4], corner_got.at[i - 4]
        return remote(i, src, dst, send_sem, recv_sem, part)

    for i in range(3, len(loads)):
        loads[i].start()
    loads[1].wait()
    loads[2].wait()
    coefs[1, pl.ds(rows, rows), :] = kappa[...] * mask[...].astype(jnp.float32)
    loads[0].wait()
    for r in range(rows):
        here = coefs[1, pl.ds(rows + r, 1), :]
        for g in range(layers // SUB):
            laid[pl.ds(r * layers + g * SUB, SUB), :] = (
                control[pl.ds(g * SUB * rows + r, SUB, stride=rows), :] * here
            )
    def upright(block):
        return jnp.concatenate([block, block[: LANES - layers]], axis=0).T

    def main_row(r, carry):
        block = laid[aligned(r * layers, layers), :]
        near[aligned((r + STEPS) * PITCH + PAD, LANES), :] = upright(block)
        return carry

    lax.fori_loop(0, rows, main_row, 0, unroll=True)
    for k, first in ((0, PAD), (1, PAD + LANES - STEPS)):
        for r in range(rows):
            side_out[k, pl.ds(r * STEPS, PAD), :] = near[
                pl.ds((r + STEPS) * PITCH + first, PAD), :
            ]
        squeeze(layers, *side_split(rows), side_out.at[k], side_sent.at[k])
    for i in range(4, 8):
        dl, dn = WAYS[i]
        for d, at, count in spots:
            r = d - 1 if dl < 0 else rows - d
            first = PAD if dn < 0 else PAD + LANES - count
            corner_out[i - 4, pl.ds(at, PAD), :] = near[pl.ds((r + STEPS) * PITCH + first, PAD), :]
        squeeze(layers, *corner_split(), corner_out.at[i - 4], corner_sent.at[i - 4])
    beside = (lat > 0).astype(jnp.int32) + (lat < n_lat - 1).astype(jnp.int32)
    pl.semaphore_wait(barrier, 2 + 3 * beside)
    for i, way in enumerate(WAYS):
        guard(way[0], lambda i=i: coef_copy(i).start())
    for i in (2, 3, 4, 5, 6, 7, 0, 1):
        guard(WAYS[i][0], lambda i=i: field_copy(i).start())
    for i in (0, 1):
        guard(WAYS[i][0], lambda i=i: field_copy(i, 1).start())

    for i in range(3, len(loads)):
        loads[i].wait()
    turn(n_lat, n_lon, off, weight, off_t, w_t)
    factor(rows, vert, inverse, ratio)
    for i, way in enumerate(WAYS):
        guard(-way[0], lambda i=i: coef_copy(i).wait_recv())
    weigh(rows, coefs, held)
    broaden(rows, held, 0, c0)
    broaden(rows, held, 1, k2)

    for i in (2, 3):
        field_copy(i).wait_recv()
        unsqueeze(layers, *side_split(rows), side_got.at[i - 2], side_in.at[i - 2])
        for r in range(rows):
            base = (r + STEPS) * PITCH
            if i == 3:
                near[pl.ds(base, PAD), :] = side_in[1, pl.ds((r + 1) * STEPS, PAD), :]
            else:
                near[pl.ds(base + PAD + LANES, PAD), :] = side_in[0, pl.ds(PAD + r * STEPS, PAD), :]
    for i in range(4, 8):
        dl, dn = WAYS[i]
        guard(-dl, lambda i=i: field_copy(i).wait_recv())
        unsqueeze(layers, *corner_split(), corner_got.at[i - 4], corner_in.at[i - 4])
        for d in range(1, STEPS + 1):
            at, count = spots[d - 1][1:] if d < STEPS else (0, 0)
            r = STEPS + rows + d - 1 if dl < 0 else STEPS - d
            if dn > 0:
                near[pl.ds(r * PITCH, PAD), :] = corner_in[i - 4, pl.ds(at + count, PAD), :]
            else:
                near[pl.ds(r * PITCH + PAD + LANES, PAD), :] = corner_in[i - 4, pl.ds(PAD + at, PAD), :]

    diffuse_inner(rows, near, far, c0, k2)
    for part in (0, 1):
        for i in (0, 1):
            guard(-WAYS[i][0], lambda i=i, part=part: field_copy(i, part).wait_recv())
            start = (STEPS + rows) if i == 0 else 0

            def far_row(r, carry, i=i, start=start):
                block = far_rows[i, aligned(r * layers, layers), :]
                near[aligned((r + start) * PITCH + PAD, LANES), :] = upright(block)
                return carry

            first = part * (STEPS // 2)
            lax.fori_loop(first, first + STEPS // 2, far_row, 0, unroll=True)

    diffuse_rest(rows, near, far, c0, k2)

    def back_row(r, carry):
        done[aligned(r * LANES, LANES), :] = near[aligned((r + STEPS) * PITCH + PAD, LANES), :].T
        return carry

    lax.fori_loop(0, rows, back_row, 0, unroll=True)
    solve_columns(rows, layers, done, control, coefs.at[1], vert, inverse, ratio, inc_ref)
    for i, way in enumerate(WAYS):
        guard(way[0], lambda i=i: coef_copy(i).wait_send())
        guard(way[0], lambda i=i: field_copy(i).wait_send())
        if way[1] == 0:
            guard(way[0], lambda i=i: field_copy(i, 1).wait_send())


def pick(table, row, col):
    level = [jnp.take_along_axis(t, col, axis=1) for t in table]
    bit = 1
    while len(level) > 1:
        odd = (row & bit) != 0
        level = [jnp.where(odd, level[i + 1], level[i]) for i in range(0, len(level), 2)]
        bit *= 2
    return level[0]


def lookup(rows, layers, turns, inc_ref, off_t, w_t, acc):
    def one_group(lg, carry):
        base = pl.multiple_of(lg * SUB, SUB)
        table = [inc_ref[pl.ds(base * rows + r, SUB, stride=rows), :] for r in range(rows)]
        for m in range(turns):
            at = pl.ds(m * layers + base, SUB)
            idx = off_t[at, :]
            acc[at, :] = pick(table, idx >> 7, idx & (LANES - 1)) * w_t[at, :]
        return carry

    lax.fori_loop(0, layers // SUB, one_group, 0, unroll=5)


def observe_kernel(
    n_lat,
    n_lon,
    rows,
    layers,
    inc_ref,
    off_t,
    w_t,
    target_ref,
    value_ref,
    target,
    acc,
    parts,
    received,
    total,
    load_sem,
    part_send,
    part_recv,
):
    lat, lon = lax.axis_index("lat"), lax.axis_index("lon")
    me, devices = lat * n_lon + lon, n_lat * n_lon
    passes, padded = off_t.shape[0], off_t.shape[1]
    members, width = devices // passes, n_lon // passes
    mine, local = lon // width, lat * width + lon % width
    blocks, high = parts.shape[1], value_ref.shape[0]
    load = pltpu.make_async_copy(target_ref, target, load_sem.at[0])
    load.start()
    barrier = pltpu.get_barrier_semaphore()

    def greet(k, carry):
        q = lax.rem(me + k, devices)
        pl.semaphore_signal(
            barrier, inc=1, device_id=(q // n_lon, q % n_lon), device_id_type=pl.DeviceIdType.MESH
        )
        return carry

    lax.fori_loop(1, devices, greet, 0, unroll=True)

    def toward(t):
        return lax.rem(mine + t + 1, passes)

    def slots(t, i, count=1):
        return pl.ds(t * members + i, count)

    def copy(src, dst, in_sem, there):
        return pltpu.make_async_remote_copy(
            src_ref=src,
            dst_ref=dst,
            send_sem=part_send.at[0],
            recv_sem=in_sem,
            device_id=there,
            device_id_type=pl.DeviceIdType.MESH,
        )

    def part_copy(t, i):
        there = lax.rem(local + i, members)
        place = (there // width, toward(t) * width + there % width)
        src, dst = parts.at[slots(t, there)], received.at[slots(t, i)]
        return copy(src, dst, part_recv.at[t, i // GROUP], place)

    def wait_group(t, g, first, count):
        here = slots(t, g * GROUP + first, count)
        copy(parts.at[here], received.at[here], part_recv.at[t, g], (lat, lon)).wait_recv()

    def look_up(t, carry):
        lookup(rows, layers, padded // layers, inc_ref, off_t.at[toward(t)], w_t.at[toward(t)], acc)
        for b in range(blocks):
            block = acc[pl.ds(b * LANES, LANES), :].T
            part = block[:members]
            for k in range(1, LANES // members):
                part = part + block[k * members : (k + 1) * members]
            parts[slots(t, 0, members), b, :] = part

        @pl.when(t == 0)
        def _():
            pl.semaphore_wait(barrier, devices - 1)

        def send(i, carry):
            part_copy(t, i).start()
            return carry

        lax.fori_loop((t == passes - 1).astype(jnp.int32), members, send, 0)
        return carry

    total[...] = jnp.zeros_like(total)
    lax.fori_loop(0, passes, look_up, 0)
    received[slots(passes - 1, 0)] = parts[slots(passes - 1, local)]
    load.wait()

    def add_group(turn, carry):
        t, g = turn // (members // GROUP), turn % (members // GROUP)
        result = total[...]
        source = lax.rem(mine + passes - t - 1, passes) * width
        own = jnp.logical_and(t == passes - 1, g == 0)
        pl.when(own)(lambda: wait_group(t, g, 1, GROUP - 1))
        pl.when(jnp.logical_not(own))(lambda: wait_group(t, g, 0, GROUP))
        for k in range(GROUP):
            i = g * GROUP + k
            p = lax.rem(local - i + members, members)
            p = p // width * n_lon + source + p % width
            cells = received[t * members + i]
            v = jnp.concatenate([cells[b : b + 1, :] for b in range(blocks)], axis=1)
            result = result + spread(v, target[pl.ds(p, 1), :], high)
        total[...] = result
        return carry

    lax.fori_loop(0, devices // GROUP, add_group, 0)
    value_ref[...] = total[:high] + total[high:]
    sent = pl.ds(0, devices - 1)
    copy(parts.at[sent], received.at[sent], part_recv.at[0, 0], (lat, lon)).wait_send()


def floats(*shape):
    return jax.ShapeDtypeStruct(shape, jnp.float32)


def spread(v, t, high):
    shape, bf = (high, v.shape[1]), jnp.bfloat16
    flat = (LANES, v.shape[1])
    upper = lax.broadcasted_iota(jnp.int32, shape, 0).astype(bf)
    lower = lax.broadcasted_iota(jnp.int32, flat, 0).astype(bf)
    hit = upper == jnp.broadcast_to((t >> 7).astype(jnp.float32), shape).astype(bf)
    one = lower == jnp.broadcast_to((t & (LANES - 1)).astype(jnp.float32), flat).astype(bf)
    first = v.astype(bf).astype(jnp.float32)
    left = jnp.concatenate(
        [
            jnp.where(hit, jnp.broadcast_to(part, shape).astype(bf), jnp.zeros(shape, bf))
            for part in (first, v - first)
        ],
        axis=0,
    )
    right = jnp.where(one, jnp.ones(flat, bf), jnp.zeros(flat, bf))
    return lax.dot_general(
        left, right, (((1,), (1,)), ((), ())), preferred_element_type=jnp.float32
    )


def per_device(
    control,
    kappa,
    sea_mask,
    vert_coef,
    stencil_offsets,
    stencil_weights,
    slot_target,
    observed,
    inv_error,
):
    levels, fields, rows, cols = control.shape
    layers = levels * fields
    tall = rows + 2 * STEPS
    sten, owners, cap = stencil_offsets.shape
    bundles = sten * owners // LANES
    padded = -(-cap // layers) * layers
    corner = corner_spots()[1] + 2 * PAD
    high = observed.shape[0] // LANES
    blocks = cap // LANES
    members = owners // bundles

    def vmem(*shape, dtype=jnp.float32):
        return pltpu.VMEM(shape, dtype)

    wide = (tall * PITCH, LANES)
    dma = pltpu.SemaphoreType.DMA
    place = (lax.axis_size("lat"), lax.axis_size("lon"))
    shapes = (
        floats(layers * rows, LANES),
        jax.ShapeDtypeStruct((bundles, padded, LANES), jnp.int32),
        floats(bundles, padded, LANES),
    )
    arrays = (
        control.reshape(layers * rows, cols),
        kappa,
        sea_mask,
        vert_coef.reshape(levels * rows, cols),
        stencil_offsets.reshape(sten * owners, cap),
        stencil_weights.reshape(sten * owners, cap),
    )
    increment, off_t, w_t = pl.pallas_call(
        functools.partial(field_kernel, *place, rows, layers),
        out_shape=shapes,
        in_specs=[pl.BlockSpec(memory_space=pltpu.HBM)] * len(arrays),
        out_specs=tuple(pl.BlockSpec(memory_space=pltpu.VMEM) for _ in shapes),
        scratch_shapes=[
            vmem(layers * rows, LANES),
            vmem(rows, LANES),
            vmem(rows, LANES, dtype=jnp.int32),
            vmem(levels * rows, LANES),
            vmem(blocks, sten * owners, LANES, dtype=jnp.int32),
            vmem(blocks, sten * owners, LANES),
            vmem(levels * rows, LANES),
            vmem(levels * rows, LANES),
            vmem(3, 3 * rows, LANES),
            vmem(2, 3, 40, LANES),
            vmem(rows * layers, LANES),
            vmem(2, STEPS * layers, LANES),
            vmem(2, rows * STEPS + 2 * PAD, LANES),
            vmem(2, rows * STEPS + 2 * PAD, LANES),
            vmem(4, corner, LANES),
            vmem(4, corner, LANES),
            vmem(2, message(*side_split(rows)), LANES),
            vmem(2, message(*side_split(rows)), LANES),
            vmem(4, message(*corner_split()), LANES),
            vmem(4, message(*corner_split()), LANES),
            vmem(*wide),
            vmem(*wide),
            vmem(*wide),
            vmem(*wide),
            vmem(rows * LANES, LANES),
            dma((4 + 2 * blocks,)),
            dma((len(WAYS),)),
            dma((len(WAYS),)),
            dma((2 * len(WAYS),)),
            dma((2 * len(WAYS),)),
        ],
        compiler_params=pltpu.CompilerParams(
            vmem_limit_bytes=44 * 1024 * 1024, collective_id=2, has_side_effects=True
        ),
        name="field",
    )(*[pltpu.with_memory_space_constraint(a, pltpu.HBM) for a in arrays])
    vm = pl.BlockSpec(memory_space=pltpu.VMEM)
    value = pl.pallas_call(
        functools.partial(observe_kernel, *place, rows, layers),
        out_shape=floats(high, LANES),
        in_specs=[vm, vm, vm, pl.BlockSpec(memory_space=pltpu.HBM)],
        out_specs=vm,
        scratch_shapes=[
            vmem(owners, cap, dtype=jnp.int32),
            vmem(padded, LANES),
            vmem(owners, blocks, LANES),
            vmem(owners, blocks, LANES),
            vmem(2 * high, LANES),
            dma((1,)),
            dma((1,)),
            dma((bundles, members // GROUP)),
        ],
        compiler_params=pltpu.CompilerParams(
            vmem_limit_bytes=24 * 1024 * 1024, collective_id=3, has_side_effects=True
        ),
        name="observe",
    )(increment, off_t, w_t, pltpu.with_memory_space_constraint(slot_target, pltpu.HBM))
    return increment.reshape(control.shape), (value.reshape(-1) - observed) * inv_error


def solution(mesh):
    return jax.shard_map(
        per_device,
        mesh=mesh,
        in_specs=(
            P(None, None, "lat", "lon"),
            P("lat", "lon"),
            P("lat", "lon"),
            P(None, "lat", "lon"),
            P(None, ("lat", "lon"), None),
            P(None, ("lat", "lon"), None),
            P(("lat", "lon"), None),
            P(("lat", "lon")),
            P(("lat", "lon")),
        ),
        out_specs=(P(None, None, "lat", "lon"), P(("lat", "lon"))),
        check_vma=False,
    )
```
